32 devices in a mesh: node: 8 (over y, x, core), rhs: 4 (over z).
Axes of the slice: x: 2, y: 2, z: 4, core: 2. Of those that a mesh axis runs over, the one named last changes fastest.
Arguments:
- right_side: float32 [64, 5, 64, 128], P('rhs', None, 'node'), may hold values from -6 to 6
- diag_tiles: bfloat16 [5, 64, 128, 128], P(None, ('node', 'rhs')), may hold values from -0.25 to 1.65
- off_tiles: bfloat16 [4, 64, 4, 128, 128], P(None, ('node', 'rhs')), may hold values from -0.125 to 0.125
- src_part: int32 [4, 64, 4], P(None, 'node'), may hold values from 0 to 7, all different within a row; in each aligned block of 8 rows (0 to 7, 8 to 15, ..., all dimensions but the last counted through in order) at most 8 rows name the same one
- src_slot: int32 [4, 64, 4], P(None, 'node'), may hold values from 0 to 7
Outputs:
- solution: float32 [64, 5, 64, 128], P('rhs', None, 'node')
The draws below stay inside these ranges and needn't reach their ends.
Inputs may be any that keep to these rules, and one draw needn't show every extreme that they name: `src_part`: over the 8 block rows of one partition at one level, each row names 4 different partitions, and no partition is named by more than 8 rows.
All inputs are finite; a program needn't handle non-finite values.
Results may differ from the reference program's by a relative error of at most 0.006.
Values may be sent and summed in bfloat16 or wider, within the bound.
No kernel may reach another device: no remote copies, remote signals or barrier semaphores. Data moves between devices by JAX's collectives and lax.ppermute only.
A program may use at most 64 MiB of HBM per device.

```python
import math
import jax
import jax.numpy as jnp
import numpy as np
from jax import lax

S = 128
RHS = 64
K = 4
LEVELS = 5
BLK = 8
NB = 64
CAP = 8
N_NODE = 8


def draw_diag_tiles(key, part):
    first_key, second_key = jax.random.split(jax.random.fold_in(key, 7))
    shape = (LEVELS, NB, S, S)
    identity = jnp.eye(S, dtype=jnp.float32)
    scales = jax.random.uniform(first_key, (LEVELS, NB, S, 1), jnp.float32, 0.6, 1.2)
    noise = jnp.clip(jax.random.normal(second_key, shape, jnp.float32), -4.0, 4.0) * 0.35 * S ** (-0.5)
    return (identity * scales + noise).astype(jnp.bfloat16)


def place_ends(drawn, rng, smallest, top_value):
    shape = drawn.shape
    index_at = [jax.random.randint(jax.random.fold_in(rng, axis), (), 0, shape[axis]) for axis in range(len(shape))]
    drawn = drawn.at[tuple(index_at)].set(smallest)
    longest = shape.index(max(shape))
    index_at[longest] = (index_at[longest] + 1) % shape[longest]
    return drawn.at[tuple(index_at)].set(top_value)


def level_of(rng, dims, shards, least, high):
    def one(position, blocks):
        steps = jax.random.uniform(jax.random.fold_in(jax.random.fold_in(rng, 6), position), (blocks,), jnp.float32, least / len(shards), high / len(shards))
        return jnp.repeat(jnp.exp(steps), dims[position] // blocks).reshape((-1,) + (1,) * (len(dims) - position - 1))

    loudness = one(*shards[0])
    for cut in shards[1:]:
        loudness = loudness * one(*cut)
    return loudness


def deal_out(rng, own, number, rows, amount, top, limit, slope):
    ranking = jax.random.permutation(rng, amount)
    packed, ordinary = portions_of(amount, rows * top, limit, slope, True), portions_of(amount, rows * top, limit, slope, False)
    places = jnp.arange(amount)

    def named(lengths, turn):
        used = int((lengths > 0).sum())
        fixed = max(1, used // 4)
        passed = fixed + (places - fixed + turn * (used - fixed)) % max(1, amount - fixed)
        return jnp.zeros((amount,), jnp.int32).at[ranking[jnp.where(places < fixed, places, passed)]].set(jnp.asarray(lengths, jnp.int32))

    lengths = jnp.where(number % 4 == 0, named(packed, number // 4), named(ordinary, number - number // 4 - 1))
    mixed = jax.random.permutation(jax.random.fold_in(own, 3), amount)
    source_of, sink = mixed[0:amount // 2 * 2:2], mixed[1:amount // 2 * 2:2]
    room = jnp.minimum(lengths[source_of] - 1, limit - lengths[sink]) // 2
    room = jnp.where((source_of == ranking[0]) | (sink == ranking[0]) | (lengths[sink] == 0), 0, jnp.maximum(room, 0))
    passed = jax.random.randint(jax.random.fold_in(own, 4), (amount // 2,), 0, 1 << 20) % (room + 1)
    lengths = lengths.at[source_of].add(-passed).at[sink].add(passed)
    members = jnp.searchsorted(jnp.cumsum(lengths), jnp.arange(rows * top), side="right").astype(jnp.int32)
    listing = members.reshape(top, rows).T
    listing = listing[jax.random.permutation(jax.random.fold_in(own, 1), rows)]
    turn = jax.random.randint(jax.random.fold_in(own, 2), (rows, 1), 0, top)
    return jnp.take_along_axis(listing, (jnp.arange(top)[None, :] + turn) % top, axis=1)


def portions_of(amount, total, most, lean, full):
    weights = [(1 << 20) // math.isqrt(rank ** lean) + 1 for rank in range(1, amount + 1)]
    largest = most if full else min(most, max(-(-total // amount), total * weights[0] // sum(weights)))
    least = 1 if total - largest >= amount - 1 else 0
    holding, rest = [largest] + [least] * (amount - 1), total - largest - least * (amount - 1)
    while rest > 0:
        candidates = [i for i in range(1, amount) if holding[i] < largest] or [i for i in range(1, amount) if holding[i] < most]
        whole, remaining = sum([weights[i] for i in candidates]), rest
        for i in candidates:
            more = min(most - holding[i], max(1, remaining * weights[i] // whole), rest)
            holding[i] = holding[i] + more
            rest = rest - more
    return np.array(holding)


def centred(key, extent, deviation, bound, shards=(), kind=jnp.bfloat16):
    entries = jax.random.normal(key, extent, jnp.float32) * deviation
    if len(shards) > 0:
        entries = level_of(key, extent, shards, -0.22, 0.18) * entries
    return jnp.clip(entries, min=-bound, max=bound).astype(kind)


def setup_inputs(seed: int = 0) -> dict:
    keys = jax.random.split(jax.random.key(seed), 6)
    right_side = centred(keys[0], (RHS, LEVELS, NB, S), 1.0, 6.0, ((0, 4), (2, 8)), jnp.float32)
    diag_tiles = draw_diag_tiles(jax.random.fold_in(keys[5], 71), 0)
    off_tiles = centred(keys[2], (LEVELS - 1, NB, K, S, S), (4 * S * K) ** -0.5, 0.125, ((1, 32),))
    src_part_keys = jax.random.split(jax.random.fold_in(keys[3], 1), (LEVELS - 1) * NB // BLK)
    src_part_turns = jax.random.permutation(jax.random.fold_in(keys[3], 3), (LEVELS - 1) * NB // BLK)
    src_part = jax.vmap(lambda own, number: deal_out(jax.random.fold_in(keys[3], 2), own, number, BLK, N_NODE, K, CAP, 2))(src_part_keys, src_part_turns).reshape((LEVELS - 1, NB, K))
    src_slot = place_ends(jax.random.randint(keys[4], (LEVELS - 1, NB, K), 0, BLK), jax.random.fold_in(keys[4], 1), 0, BLK - 1).astype(jnp.int32)
    return {"right_side": right_side, "diag_tiles": diag_tiles, "off_tiles": off_tiles, "src_part": src_part, "src_slot": src_slot}


def reference(right_side, diag_tiles, off_tiles, src_part, src_slot):
    coupled_block = (src_part * BLK + src_slot).astype(jnp.int32)
    stored = []
    previous = None
    for level_at in range(LEVELS):
        current = right_side[:, level_at]
        if level_at > 0:
            picked = jnp.take(previous, coupled_block[level_at - 1].reshape(-1), axis=1)
            picked = picked.reshape(RHS, NB, K, S).astype(jnp.float32)
            coupled = jnp.einsum("cnks,nkts->cnt", picked, off_tiles[level_at - 1].astype(jnp.float32))
            current = current - coupled
        rounded = lax.optimization_barrier(current.astype(jnp.bfloat16)).astype(jnp.float32)
        previous = jnp.einsum("cns,nts->cnt", rounded, diag_tiles[level_at].astype(jnp.float32)).astype(jnp.bfloat16)
        stored.append(previous)
    results = [None] * LEVELS
    upper_round = None
    for level_at in range(LEVELS - 1, -1, -1):
        incoming = jnp.zeros((RHS, NB, S), jnp.float32)
        if level_at < LEVELS - 1:
            contrib_terms = jnp.einsum("cnt,nkts->cnks", upper_round, off_tiles[level_at].astype(jnp.float32))
            incoming = incoming.at[:, coupled_block[level_at].reshape(-1)].add(contrib_terms.reshape(RHS, NB * K, S))
        back_in = (stored[level_at].astype(jnp.float32) - incoming).astype(jnp.bfloat16)
        back_in = lax.optimization_barrier(back_in).astype(jnp.float32)
        solution = jnp.einsum("cns,nst->cnt", back_in, diag_tiles[level_at].astype(jnp.float32))
        upper_round = lax.optimization_barrier(solution.astype(jnp.bfloat16)).astype(jnp.float32)
        results[level_at] = solution
    return jnp.stack(results, axis=1)
```

```python
import functools

import jax
import jax.numpy as jnp
from jax import lax
from jax.experimental import pallas as pl
from jax.experimental.pallas import tpu as pltpu
from jax.sharding import PartitionSpec as P

F32 = jnp.float32
BF16 = jnp.bfloat16
NT = (((1,), (1,)), ((), ()))
NN = (((1,), (0,)), ((), ()))


def ring_of(size):
    return list(range(0, size, 2)) + list(range(1, size, 2))[::-1]


def dot(a, b, dims):
    return lax.dot_general(a, b, dims, preferred_element_type=F32)


class Rows:
    def __init__(self, refs, own_rows):
        self.places = []
        for ref, count in zip(refs, own_rows):
            self.places += [(ref, i) for i in range(count)]

    def tile(self, at, k):
        ref, i = self.places[at]
        return ref[i, k]


def forward_row(ids, src, link, rows, tiles, solved, right, fanout, at):
    row = ids[at]
    current = right[row]
    if link is not None:
        coupled = None
        for k in range(fanout):
            place = src[link, row * fanout + k]
            term = dot(solved[place], tiles.tile(at, k), NT)
            coupled = term if coupled is None else coupled + term
        current = current - coupled
    return dot(current.astype(BF16), tiles.tile(at, tiles.diag), NT).astype(BF16)


def level_kernel(config, *refs):
    refs = list(refs)
    take = lambda n: [refs.pop(0) for _ in range(n)]
    rows, fanout, peers = config["rows"], config["fanout"], config["peers"]
    counts = config["counts"]
    ids, src = take(2)
    down, up = config["down"], config["up"]
    level = config["level"]
    here = take(len(counts))
    if down:
        right_in = take(1)[0]
        arrived = take(peers) if level > 0 else []
    else:
        stored = take(1)[0]
    if up and not down:
        returned = take(peers)
        take(1)
    outs_f = take(1)[0] if down and not up else None
    if up:
        result = take(1)[0]
        sent = take(peers) if level > 0 else []
    scratch = refs
    tiles = Rows(here, counts)
    tiles.diag = fanout if level > 0 else 0
    if down:
        right, solved = scratch[0], scratch[1]
        for n in range(rows):
            right[n] = right_in[:, 0, n, :]
        for d, block in enumerate(arrived):
            solved[d * rows : (d + 1) * rows] = block[...]
    if up:
        out_rows = scratch[-2]
        total = scratch[-1]
        if level > 0:
            total[...] = jnp.zeros_like(total)
    link = level - 1 if level > 0 else None
    for at in range(rows):
        row = ids[at]
        if down:
            value = forward_row(ids, src, link, rows, tiles, solved, right, fanout, at)
            if not up:
                outs_f[row] = value
                continue
            back = value
        else:
            incoming = returned[0][row].astype(F32)
            for block in returned[1:]:
                incoming = incoming + block[row].astype(F32)
            back = (stored[row].astype(F32) - incoming).astype(BF16)
        answer = dot(back, tiles.tile(at, tiles.diag), NN)
        out_rows[row] = answer
        if level > 0:
            upper = answer.astype(BF16)
            for k in range(fanout):
                place = src[link, row * fanout + k]
                total[place] += dot(upper, tiles.tile(at, k), NN)
    if up:
        for n in range(rows):
            result[:, 0, n, :] = out_rows[n]
        for d, block in enumerate(sent):
            block[...] = total[d * rows : (d + 1) * rows].astype(block.dtype)


def whole(x):
    zeros = (0,) * x.ndim
    return pl.BlockSpec(x.shape, lambda i: zeros)


def on_device(right_side, diag_tiles, off_tiles, src_part, src_slot):
    columns, levels, rows, size = right_side.shape
    fanout = src_part.shape[2]
    own = diag_tiles.shape[1]
    peers = lax.axis_size("node")
    group = lax.axis_size("rhs")
    me = lax.axis_index("node")
    mine = lax.axis_index("rhs")
    ring = ring_of(group)
    following = {ring[i]: ring[(i + 1) % group] for i in range(group)}
    from_next = [(following[r], r) for r in range(group)]
    from_prev = [(r, following[r]) for r in range(group)]
    next_of = jnp.array([following[r] for r in range(group)], jnp.int32)
    leading = {following[r]: r for r in range(group)}
    prev_of = jnp.array([leading[r] for r in range(group)], jnp.int32)
    after, before = next_of[mine], prev_of[mine]
    across = next_of[after]
    half = own // 2
    counts = (own, own, own, half, own - half)
    holders = jnp.stack([mine, after, before, across])
    ids = (holders[:, None] * own + jnp.arange(own, dtype=jnp.int32)[None, :]).reshape(-1)
    src = ((src_part ^ me) * rows + src_slot).reshape(levels - 1, rows * fanout)

    tiles = []
    for level in range(levels):
        piece = diag_tiles[level][:, None]
        if level > 0:
            piece = jnp.concatenate([off_tiles[level - 1], piece], axis=1)
        nxt = lax.ppermute(piece, "rhs", from_next)
        prv = lax.ppermute(piece, "rhs", from_prev)
        far_a = lax.ppermute(nxt[:half], "rhs", from_next)
        far_b = lax.ppermute(prv[half:], "rhs", from_prev)
        tiles.append((piece, nxt, prv, far_a, far_b))

    def swap(x, d):
        if d == 0:
            return x
        return lax.ppermute(x, "node", [(q, q ^ d) for q in range(peers)])

    vec = (rows, columns, size)
    smem = pl.BlockSpec(memory_space=pltpu.SMEM)

    def run(level, down, up, arrived=(), stored=None, returned=(), result=None):
        config = dict(rows=rows, fanout=fanout, peers=peers, counts=counts, level=level, down=down, up=up)
        args, specs = [ids, src], [smem, smem]

        def add(*xs):
            for x in xs:
                args.append(x)
                specs.append(whole(x))

        slab = pl.BlockSpec((columns, 1, rows, size), lambda i: (0, level, 0, 0))
        add(*tiles[level])
        scratch, out_shape, out_specs, aliases = [], [], [], {}
        if down:
            args.append(right_side)
            specs.append(slab)
            add(*arrived)
            scratch += [pltpu.VMEM(vec, F32), pltpu.VMEM((peers * rows, columns, size), BF16)]
        else:
            add(stored)
            add(*returned)
            aliases = {len(args): 0}
            args.append(result)
            specs.append(pl.BlockSpec(memory_space=pl.ANY))
        if down and not up:
            shape = jax.ShapeDtypeStruct(vec, BF16)
            out_shape.append(shape)
            out_specs.append(whole(shape))
        if up:
            out_shape.append(jax.ShapeDtypeStruct(right_side.shape, F32))
            out_specs.append(slab)
            if level > 0:
                for d in range(peers):
                    shape = jax.ShapeDtypeStruct(vec, F32 if d == 0 else BF16)
                    out_shape.append(shape)
                    out_specs.append(whole(shape))
            scratch += [pltpu.VMEM(vec, F32), pltpu.VMEM((peers * rows, columns, size), F32)]
        dots = rows * ((fanout if level > 0 else 0) + 1) * (int(down) + int(up))
        moved = sum(x.size * x.dtype.itemsize for x in args[2:] if x.shape != right_side.shape)
        return pl.pallas_call(
            functools.partial(level_kernel, config),
            grid=(1,),
            in_specs=specs,
            out_specs=out_specs,
            out_shape=out_shape,
            scratch_shapes=scratch,
            input_output_aliases=aliases,
            compiler_params=pltpu.CompilerParams(vmem_limit_bytes=32 * 1024 * 1024),
            cost_estimate=pl.CostEstimate(
                flops=2 * dots * columns * size * size, bytes_accessed=moved, transcendentals=0
            ),
        )(*args)

    stored = []
    arrived = ()
    for level in range(levels - 1):
        (value,) = run(level, True, False, arrived=arrived)
        stored.append(value)
        arrived = [swap(value, d) for d in range(peers)]
    result, *sent = run(levels - 1, True, True, arrived=arrived)
    for level in range(levels - 2, -1, -1):
        returned = [swap(x, d) for d, x in enumerate(sent)]
        result, *sent = run(level, False, True, stored=stored[level], returned=returned, result=result)
    return result


def solution(mesh):
    placed = (
        P("rhs", None, "node", None),
        P(None, ("node", "rhs"), None, None),
        P(None, ("node", "rhs"), None, None, None),
        P(None, "node", None),
        P(None, "node", None),
    )
    return jax.shard_map(
        on_device,
        mesh=mesh,
        in_specs=placed,
        out_specs=P("rhs", None, "node", None),
        check_vma=False,
    )
```

```python
import functools

import jax
import jax.numpy as jnp
from jax import lax
from jax.experimental import pallas as pl
from jax.experimental.pallas import tpu as pltpu
from jax.sharding import PartitionSpec as P

F32 = jnp.float32
BF16 = jnp.bfloat16
NT = (((1,), (1,)), ((), ()))
NN = (((1,), (0,)), ((), ()))


def dot(a, b, dims):
    return lax.dot_general(a, b, dims, preferred_element_type=F32)


def position():
    node, z = lax.axis_index("node"), lax.axis_index("rhs")
    return node >> 1, node & 1, z >> 1, z & 1


def prep_kernel(first, count, narrow, right, one, two):
    _, core, _, near = position()
    half = right.shape[2] // 2
    upper = core == 1
    for i in range(count):
        for t in range(half):
            low = right[:, first + i, t, :]
            high = right[:, first + i, t + half, :]
            at = t ^ (near * 2)
            one[i, at] = jnp.where(upper, high, low).astype(narrow)
            two[i, at] = jnp.where(upper, low, high).astype(narrow)


def place_kernel(links, rows, fanout, part, slot, part_other, slot_other, place):
    chip, core, far, near = position()
    half = rows // 2
    for v in range(rows):
        row = far * half + ((v & (half - 1)) ^ (near * 2))
        p_ref, s_ref = (part, slot) if v < half else (part_other, slot_other)
        for link in range(links):
            for k in range(fanout):
                p, s = p_ref[link, row, k], s_ref[link, row, k]
                unit = ((p >> 1) ^ chip) * 2 + ((s >> 2) ^ far)
                inner = ((p & 1) ^ core) * half + ((s & (half - 1)) ^ (near * 2))
                place[link, v * fanout + k] = unit * rows + inner


def tile_of(refs, pick, v):
    per = refs[0].shape[-4]
    ref = refs[v // per]
    if pick is None:
        return lambda k: ref[v % per, k]
    return lambda k: ref[pick, v % per, k]


def level_kernel(config, *refs):
    refs = list(refs)
    take = lambda n: [refs.pop(0) for _ in range(n)]
    rows, fanout, chips = config["rows"], config["fanout"], config["chips"]
    level, down, up, pick = config["level"], config["down"], config["up"], config["pick"]
    half = rows // 2
    linked = level > 0
    last = fanout if linked else 0
    place = take(1)[0] if linked else None
    tiles = take(4)
    if down:
        one, two = take(2)
        arrived = take(chips + 1) if linked else []
    else:
        stored, kept, crossed = take(3)
        returned = take(chips - 1)
    out_f = take(1)[0] if not up else None
    if up:
        result = take(2)
        if linked:
            keep, cross = take(2)
            sent = take(chips - 1)
    solved = take(1)[0] if down and linked else None
    total = take(1)[0] if up and linked else None
    _, core, far, _ = position()
    straight = (core ^ far) == 0
    at = [tile_of(tiles, pick, v) for v in range(rows)]
    if total is not None:
        total[...] = jnp.zeros_like(total)
    if down:
        base = 0
        for block in arrived:
            if len(block.shape) == 3:
                solved[base : base + rows] = block[...]
                base += rows
            else:
                for h in range(2):
                    solved[base : base + rows] = block[h]
                    base += rows
        values = []
        for v in range(rows):
            mine, other = (one, two) if v < half else (two, one)
            index = (level - 1, v % half) if linked else (0, v % half)
            current = jnp.where(straight, mine[index], other[index])
            if linked:
                picked = [solved[place[level - 1, v * fanout + k]] for k in range(fanout)]
                coupled = dot(
                    jnp.concatenate(picked, axis=1),
                    jnp.concatenate([at[v](k) for k in range(fanout)], axis=1),
                    NT,
                )
                current = current - coupled
            values.append(current.astype(BF16))
        values = [dot(values[v], at[v](last), NT).astype(BF16) for v in range(rows)]
        if not up:
            for v in range(rows):
                out_f[v] = values[v]
            return
    else:
        values = []
        for v in range(rows):
            incoming = kept[v] + crossed[v].astype(F32)
            for block in returned:
                incoming = incoming + block[0, v].astype(F32)
            values.append((stored[v].astype(F32) - incoming).astype(BF16))
    answers = [dot(values[v], at[v](last), NN) for v in range(rows)]
    for v in range(half):
        result[0][v] = jnp.where(straight, answers[v], answers[v + half])
        result[1][v] = jnp.where(straight, answers[v + half], answers[v])
    if not linked:
        return
    size = answers[0].shape[1]
    for v in range(rows):
        terms = dot(
            answers[v].astype(BF16),
            jnp.concatenate([at[v](k) for k in range(fanout)], axis=1),
            NN,
        )
        for k in range(fanout):
            total[place[level - 1, v * fanout + k]] += terms[:, k * size : (k + 1) * size]
    keep[...] = total[0:rows]
    cross[...] = total[rows : 2 * rows]
    for d, block in enumerate(sent):
        for h in range(2):
            base = ((d + 1) * 2 + h) * rows
            block[h] = total[base : base + rows].astype(BF16)


def finish_kernel(spans, *refs):
    _, core, _, near = position()
    refs, out = refs[: 2 * len(spans)], refs[-1]
    upper = core == 1
    for j, levels in enumerate(spans):
        one, two = refs[2 * j], refs[2 * j + 1]
        half = one.shape[1]
        for i, place in enumerate(levels):
            for t in range(half):
                at = t ^ (near * 2)
                a, b = one[i, at], two[i, at]
                out[:, place, t, :] = jnp.where(upper, b, a)
                out[:, place, t + half, :] = jnp.where(upper, a, b)


VMEM = pl.BlockSpec(memory_space=pltpu.VMEM)
SMEM = pl.BlockSpec(memory_space=pltpu.SMEM)


def params():
    return pltpu.CompilerParams(vmem_limit_bytes=32 * 1024 * 1024)


def on_device(right_side, diag_tiles, off_tiles, src_part, src_slot):
    columns, levels, rows, size = right_side.shape
    fanout = src_part.shape[2]
    links = levels - 1
    half = rows // 2
    nodes = lax.axis_size("node")
    group = lax.axis_size("rhs")
    chips = nodes // 2
    both = ("node", "rhs")

    def shift(x, node_bits, z_bits):
        pairs = [
            (n * group + z, (n ^ node_bits) * group + (z ^ z_bits))
            for n in range(nodes)
            for z in range(group)
        ]
        return lax.ppermute(x, both, pairs)

    def turn(x, flip, back):
        pairs = []
        for n in range(nodes):
            for z in range(group):
                a, b = n & 1, z >> 1
                target = ((n & ~1) | b) * group + (((a ^ flip) << 1) | (z & 1))
                pairs.append((n * group + z, target))
        if back:
            pairs = [(b, a) for a, b in pairs]
        return lax.ppermute(x, both, pairs)

    def spread(piece):
        near = shift(piece, 0, 1)
        return piece, near, shift(piece, 1, 0), shift(near, 1, 0)

    def prepare(first, count, narrow):
        shape = jax.ShapeDtypeStruct((count, half, columns, size), narrow)
        pair = pl.pallas_call(
            functools.partial(prep_kernel, first, count, narrow),
            in_specs=[VMEM],
            out_specs=[VMEM, VMEM],
            out_shape=[shape, shape],
            compiler_params=params(),
        )(right_side)
        return turn(pair[0], 0, False), turn(pair[1], 1, False)

    first_right = prepare(0, 1, BF16)
    first_tiles = spread(diag_tiles[0][:, None])
    joined = jnp.concatenate([off_tiles, diag_tiles[1:, :, None]], axis=2)
    tiles = [(first_tiles, None)]
    spans = [(0, 1), (1, 2), (2, links)]
    for a, b in spans:
        if b - a == 1:
            tiles.append((spread(joined[a]), None))
        else:
            held = spread(joined[a:b])
            tiles += [(held, i) for i in range(b - a)]
    rest_right = prepare(1, links, F32)
    place = pl.pallas_call(
        functools.partial(place_kernel, links, rows, fanout),
        in_specs=[SMEM] * 4,
        out_specs=SMEM,
        out_shape=jax.ShapeDtypeStruct((links, rows * fanout), jnp.int32),
        compiler_params=params(),
    )(src_part, src_slot, shift(src_part, 1, 0), shift(src_slot, 1, 0))

    vec = (rows, columns, size)

    def run(level, down, up, arrived=(), stored=None, kept=None, crossed=None, returned=()):
        held, pick = tiles[level]
        linked = level > 0
        config = dict(
            rows=rows, fanout=fanout, chips=chips, level=level, down=down, up=up, pick=pick
        )
        args = ([place] if linked else []) + list(held)
        if down:
            args += list(rest_right if linked else first_right) + list(arrived)
        else:
            args += [stored, kept, crossed] + list(returned)
        shapes, scratch = [], []
        if not up:
            shapes.append(jax.ShapeDtypeStruct(vec, BF16))
        else:
            shapes += [jax.ShapeDtypeStruct((half, columns, size), F32)] * 2
            if linked:
                shapes += [jax.ShapeDtypeStruct(vec, F32)] * 2
                shapes += [jax.ShapeDtypeStruct((2,) + vec, BF16)] * (chips - 1)
        if down and linked:
            scratch.append(pltpu.VMEM((2 * chips * rows, columns, size), BF16))
        if up and linked:
            scratch.append(pltpu.VMEM((2 * chips * rows, columns, size), F32))
        dots = rows * ((fanout if linked else 0) + 1) * (int(down) + int(up))
        return pl.pallas_call(
            functools.partial(level_kernel, config),
            in_specs=([SMEM] if linked else []) + [VMEM] * (len(args) - int(linked)),
            out_specs=[VMEM] * len(shapes),
            out_shape=shapes,
            scratch_shapes=scratch,
            compiler_params=params(),
            cost_estimate=pl.CostEstimate(
                flops=2 * dots * columns * size * size,
                bytes_accessed=dots * size * size * 2,
                transcendentals=0,
            ),
        )(*args)

    def exchange(value):
        other = shift(value, 0, 2)
        pair = jnp.stack([value, other])
        return [value, other] + [shift(pair, 2 * d, 0) for d in range(1, chips)]

    stored = []
    arrived = ()
    for level in range(levels - 1):
        (value,) = run(level, True, False, arrived=arrived)
        stored.append(value)
        arrived = exchange(value)
    results = [None] * levels
    one, two, *sent = run(levels - 1, True, True, arrived=arrived)
    results[levels - 1] = (one, two)
    for level in range(levels - 2, -1, -1):
        kept, cross, sent = sent[0], sent[1], sent[2:]
        returned = [shift(x, 2 * (d + 1), 0) for d, x in enumerate(sent)]
        summed = cross
        for x in returned:
            summed = summed + x[1].astype(F32)
        crossed = shift(summed.astype(BF16), 0, 2)
        one, two, *sent = run(
            level, False, True, stored=stored[level], kept=kept, crossed=crossed, returned=returned
        )
        results[level] = (one, two)

    def home(wanted):
        one = jnp.stack([results[x][0] for x in wanted])
        two = jnp.stack([results[x][1] for x in wanted])
        return turn(one, 0, True), turn(two, 1, True)

    groups = [list(range(levels - 1, 1, -1)), [1], [0]]
    early = []
    for wanted in groups[:-1]:
        early += home(wanted)
    final = home(groups[-1])
    return pl.pallas_call(
        functools.partial(finish_kernel, groups),
        in_specs=[VMEM] * (2 * len(groups)),
        out_specs=VMEM,
        out_shape=jax.ShapeDtypeStruct(right_side.shape, F32),
        compiler_params=params(),
    )(*early, *final)


def solution(mesh):
    placed = (
        P("rhs", None, "node", None),
        P(None, ("node", "rhs"), None, None),
        P(None, ("node", "rhs"), None, None, None),
        P(None, "node", None),
        P(None, "node", None),
    )
    return jax.shard_map(
        on_device,
        mesh=mesh,
        in_specs=placed,
        out_specs=P("rhs", None, "node", None),
        check_vma=False,
    )
```

```python
import functools

import jax
import jax.numpy as jnp
from jax import lax
from jax.experimental import pallas as pl
from jax.experimental.pallas import tpu as pltpu
from jax.sharding import PartitionSpec as P

F32 = jnp.float32
BF16 = jnp.bfloat16
NT = (((1,), (1,)), ((), ()))
NN = (((1,), (0,)), ((), ()))


def dot(a, b, dims):
    return lax.dot_general(a, b, dims, preferred_element_type=F32)


def position():
    node, z = lax.axis_index("node"), lax.axis_index("rhs")
    return node >> 1, node & 1, z >> 1, z & 1


def prep_kernel(levels, right, one, two):
    _, core, _, near = position()
    half = right.shape[2] // 2
    upper = core == 1
    for i in range(levels):
        for t in range(half):
            low = right[:, i, t, :]
            high = right[:, i, t + half, :]
            at = t ^ (near * 2)
            one[i, at] = jnp.where(upper, high, low).astype(BF16)
            two[i, at] = jnp.where(upper, low, high).astype(BF16)


def place_kernel(links, rows, fanout, part, slot, part_other, slot_other, place):
    chip, core, far, near = position()
    half = rows // 2
    for v in range(rows):
        row = far * half + ((v & (half - 1)) ^ (near * 2))
        p_ref, s_ref = (part, slot) if v < half else (part_other, slot_other)
        for link in range(links):
            for k in range(fanout):
                p, s = p_ref[link, row, k], s_ref[link, row, k]
                unit = ((p >> 1) ^ chip) * 2 + ((s >> 2) ^ far)
                inner = ((p & 1) ^ core) * half + ((s & (half - 1)) ^ (near * 2))
                place[link, v * fanout + k] = unit * rows + inner


def tile_of(refs, level, v):
    per = refs[0].shape[-4]
    ref = refs[v // per]
    if len(ref.shape) == 5:
        return lambda k: ref[level - 1, v % per, k]
    return lambda k: ref[v % per, k]


def level_kernel(config, *refs):
    refs = list(refs)
    take = lambda n: [refs.pop(0) for _ in range(n)]
    rows, fanout, chips = config["rows"], config["fanout"], config["chips"]
    level, down, up = config["level"], config["down"], config["up"]
    half = rows // 2
    linked = level > 0
    last = fanout if linked else 0
    place = take(1)[0]
    tiles = take(4)
    if down:
        one, two = take(2)
        arrived = take(2 * chips) if linked else []
    else:
        stored, kept, crossed = take(3)
        returned = take(chips - 1)
    out_f = take(1)[0] if not up else None
    if up:
        result = take(2)
        if linked:
            keep, cross = take(2)
            sent = take(2 * (chips - 1))
    solved = take(1)[0] if down and linked else None
    total = take(1)[0] if up and linked else None
    _, core, far, _ = position()
    straight = (core ^ far) == 0
    at = [tile_of(tiles, level, v) for v in range(rows)]
    if total is not None:
        total[...] = jnp.zeros_like(total)
    if down:
        for i, block in enumerate(arrived):
            solved[i * rows : (i + 1) * rows] = block[...]
        values = []
        for v in range(rows):
            mine, other = (one, two) if v < half else (two, one)
            index = (level, v % half)
            current = jnp.where(straight, mine[index], other[index]).astype(F32)
            if linked:
                picked = [solved[place[level - 1, v * fanout + k]] for k in range(fanout)]
                coupled = dot(
                    jnp.concatenate(picked, axis=1),
                    jnp.concatenate([at[v](k) for k in range(fanout)], axis=1),
                    NT,
                )
                current = current - coupled
            values.append(current.astype(BF16))
        values = [dot(values[v], at[v](last), NT).astype(BF16) for v in range(rows)]
        if not up:
            for v in range(rows):
                out_f[v] = values[v]
            return
    else:
        values = []
        for v in range(rows):
            incoming = kept[v] + crossed[v].astype(F32)
            for block in returned:
                incoming = incoming + block[v].astype(F32)
            values.append((stored[v].astype(F32) - incoming).astype(BF16))
    answers = [dot(values[v], at[v](last), NN) for v in range(rows)]
    for v in range(half):
        result[0][v] = jnp.where(straight, answers[v], answers[v + half])
        result[1][v] = jnp.where(straight, answers[v + half], answers[v])
    if not linked:
        return
    size = answers[0].shape[1]
    for v in range(rows):
        terms = dot(
            answers[v].astype(BF16),
            jnp.concatenate([at[v](k) for k in range(fanout)], axis=1),
            NN,
        )
        for k in range(fanout):
            total[place[level - 1, v * fanout + k]] += terms[:, k * size : (k + 1) * size]
    keep[...] = total[0:rows]
    cross[...] = total[rows : 2 * rows]
    for i, block in enumerate(sent):
        base = (2 + i) * rows
        block[...] = total[base : base + rows].astype(BF16)


def finish_kernel(spans, *refs):
    _, core, _, near = position()
    refs, out = refs[: 2 * len(spans)], refs[-1]
    upper = core == 1
    for j, levels in enumerate(spans):
        one, two = refs[2 * j], refs[2 * j + 1]
        half = one.shape[1]
        for i, place in enumerate(levels):
            for t in range(half):
                at = t ^ (near * 2)
                a, b = one[i, at], two[i, at]
                out[:, place, t, :] = jnp.where(upper, b, a)
                out[:, place, t + half, :] = jnp.where(upper, a, b)


VMEM = pl.BlockSpec(memory_space=pltpu.VMEM)
SMEM = pl.BlockSpec(memory_space=pltpu.SMEM)


def params():
    return pltpu.CompilerParams(vmem_limit_bytes=32 * 1024 * 1024)


def on_device(right_side, diag_tiles, off_tiles, src_part, src_slot):
    columns, levels, rows, size = right_side.shape
    fanout = src_part.shape[2]
    links = levels - 1
    half = rows // 2
    nodes = lax.axis_size("node")
    group = lax.axis_size("rhs")
    chips = nodes // 2
    both = ("node", "rhs")

    def shift(x, node_bits, z_bits):
        pairs = [
            (n * group + z, (n ^ node_bits) * group + (z ^ z_bits))
            for n in range(nodes)
            for z in range(group)
        ]
        return lax.ppermute(x, both, pairs)

    def turn(x, flip, back):
        pairs = []
        for n in range(nodes):
            for z in range(group):
                a, b = n & 1, z >> 1
                target = ((n & ~1) | b) * group + (((a ^ flip) << 1) | (z & 1))
                pairs.append((n * group + z, target))
        if back:
            pairs = [(b, a) for a, b in pairs]
        return lax.ppermute(x, both, pairs)

    def after(x, *others):
        return lax.optimization_barrier((x, *others))[0]

    first = diag_tiles[0][:, None]
    first_near = shift(first, 0, 1)
    first_tiles = [first, first_near, shift(first, 1, 0), shift(first_near, 1, 0)]
    shape = jax.ShapeDtypeStruct((levels, half, columns, size), BF16)
    pair = pl.pallas_call(
        functools.partial(prep_kernel, levels),
        in_specs=[VMEM],
        out_specs=[VMEM, VMEM],
        out_shape=[shape, shape],
        compiler_params=params(),
    )(right_side)
    right = [turn(pair[0], 0, False), turn(pair[1], 1, False)]
    own = jnp.concatenate([off_tiles, diag_tiles[1:, :, None]], axis=2)
    own_swapped = shift(after(own, first_near), 1, 0)
    near = {}

    def fetch(level, *others):
        if level < levels:
            near[level] = shift(after(own[level - 1], *others), 0, 1)

    def tiles_of(level, *others):
        if level == 0:
            return first_tiles
        return [own, near[level], own_swapped, shift(after(near[level], *others), 1, 0)]

    place = pl.pallas_call(
        functools.partial(place_kernel, links, rows, fanout),
        in_specs=[SMEM] * 4,
        out_specs=SMEM,
        out_shape=jax.ShapeDtypeStruct((links, rows * fanout), jnp.int32),
        compiler_params=params(),
    )(src_part, src_slot, shift(src_part, 1, 0), shift(src_slot, 1, 0))

    vec = (rows, columns, size)

    def run(level, tiles, down, up, arrived=(), stored=None, kept=None, crossed=None, returned=()):
        linked = level > 0
        config = dict(rows=rows, fanout=fanout, chips=chips, level=level, down=down, up=up)
        args = [place] + list(tiles)
        if down:
            args += list(right) + list(arrived)
        else:
            args += [stored, kept, crossed] + list(returned)
        shapes, scratch = [], []
        if not up:
            shapes.append(jax.ShapeDtypeStruct(vec, BF16))
        else:
            shapes += [jax.ShapeDtypeStruct((half, columns, size), F32)] * 2
            if linked:
                shapes += [jax.ShapeDtypeStruct(vec, F32)] * 2
                shapes += [jax.ShapeDtypeStruct(vec, BF16)] * (2 * (chips - 1))
        if down and linked:
            scratch.append(pltpu.VMEM((2 * chips * rows, columns, size), BF16))
        if up and linked:
            scratch.append(pltpu.VMEM((2 * chips * rows, columns, size), F32))
        dots = rows * ((fanout if linked else 0) + 1) * (int(down) + int(up))
        return pl.pallas_call(
            functools.partial(level_kernel, config),
            in_specs=[SMEM] + [VMEM] * (len(args) - 1),
            out_specs=[VMEM] * len(shapes),
            out_shape=shapes,
            scratch_shapes=scratch,
            compiler_params=params(),
            cost_estimate=pl.CostEstimate(
                flops=2 * dots * columns * size * size,
                bytes_accessed=dots * size * size * 2,
                transcendentals=0,
            ),
        )(*args)

    def exchange(value):
        other = shift(value, 0, 2)
        near = [shift(value, 2 * d, 0) for d in range(1, chips)]
        far = [shift(other, 2 * d, 0) for d in range(1, chips)]
        return near[-1], [value, other] + [x for pair in zip(near, far) for x in pair]

    stored = []
    arrived = ()
    tiles = [tiles_of(0)]
    fetch(1, first_near)
    for level in range(levels - 1):
        (value,) = run(level, tiles[level], True, False, arrived=arrived)
        stored.append(value)
        landed, arrived = exchange(value)
        tiles.append(tiles_of(level + 1, value))
        fetch(level + 2, landed)
    results = [None] * levels
    one, two, *sent = run(levels - 1, tiles[-1], True, True, arrived=arrived)
    results[levels - 1] = (one, two)
    for level in range(levels - 2, -1, -1):
        kept, summed = sent[0], sent[1]
        for d in range(1, chips):
            summed = summed + shift(sent[2 * d + 1], 2 * d, 0).astype(F32)
        crossed = shift(summed.astype(BF16), 0, 2)
        returned = [shift(sent[2 * d], 2 * d, 0) for d in range(1, chips)]
        one, two, *sent = run(
            level,
            tiles[level],
            False,
            True,
            stored=stored[level],
            kept=kept,
            crossed=crossed,
            returned=returned,
        )
        results[level] = (one, two)

    def home(wanted):
        one = jnp.stack([results[x][0] for x in wanted])
        two = jnp.stack([results[x][1] for x in wanted])
        return turn(one, 0, True), turn(two, 1, True)

    groups = [list(range(levels - 1, 1, -1)), [1], [0]]
    early = []
    for wanted in groups[:-1]:
        early += home(wanted)
    final = home(groups[-1])
    return pl.pallas_call(
        functools.partial(finish_kernel, groups),
        in_specs=[VMEM] * (2 * len(groups)),
        out_specs=VMEM,
        out_shape=jax.ShapeDtypeStruct(right_side.shape, F32),
        compiler_params=params(),
    )(*early, *final)


def solution(mesh):
    placed = (
        P("rhs", None, "node", None),
        P(None, ("node", "rhs"), None, None),
        P(None, ("node", "rhs"), None, None, None),
        P(None, "node", None),
        P(None, "node", None),
    )
    return jax.shard_map(
        on_device,
        mesh=mesh,
        in_specs=placed,
        out_specs=P("rhs", None, "node", None),
        check_vma=False,
    )
```

```python
import functools

import jax
import jax.numpy as jnp
from jax import lax
from jax.experimental import pallas as pl
from jax.experimental.pallas import tpu as pltpu
from jax.sharding import PartitionSpec as P

F32 = jnp.float32
BF16 = jnp.bfloat16
NT = (((1,), (1,)), ((), ()))
NN = (((1,), (0,)), ((), ()))


def dot(a, b, dims):
    return lax.dot_general(a, b, dims, preferred_element_type=F32)


def position():
    node, z = lax.axis_index("node"), lax.axis_index("rhs")
    return node >> 1, node & 1, z >> 1, z & 1


def prep_kernel(first, right, one, two):
    _, core, _, near = position()
    half = right.shape[2] // 2
    upper = core == 1
    for i in range(one.shape[0]):
        for t in range(half):
            low = right[:, first + i, t, :]
            high = right[:, first + i, t + half, :]
            at = t ^ (near * 2)
            one[i, at] = jnp.where(upper, high, low).astype(one.dtype)
            two[i, at] = jnp.where(upper, low, high).astype(two.dtype)


def places(link, v, rows, fanout, sources):
    chip, core, far, near = position()
    half = rows // 2
    row = far * half + ((v & (half - 1)) ^ (near * 2))
    part, slot = sources[:2] if v < half else sources[2:]
    found = []
    for k in range(fanout):
        p, s = part[link, row, k], slot[link, row, k]
        unit = (p >> 1) * 2 + ((s >> 2) ^ far)
        inner = ((p & 1) ^ core) * half + ((s & (half - 1)) ^ (near * 2))
        found.append(unit * rows + inner)
    return found


def tile_of(refs, level, v):
    per = refs[0].shape[-4]
    ref = refs[v // per]
    if len(ref.shape) == 5:
        return lambda k: ref[level - 1, v % per, k]
    return lambda k: ref[v % per, k]


def level_kernel(config, *refs):
    refs = list(refs)
    take = lambda n: [refs.pop(0) for _ in range(n)]
    rows, fanout, chips = config["rows"], config["fanout"], config["chips"]
    level, down, up = config["level"], config["down"], config["up"]
    half = rows // 2
    linked = level > 0
    last = fanout if linked else 0
    sources = take(4)
    tiles = take(4)
    if down:
        one, two = take(2)
        solved = take(1)[0] if linked else None
    else:
        stored, crossed, returned = take(3)
    out_f = take(1)[0] if not up else None
    if up:
        result = take(2)
        sent = take(1)[0] if linked else None
    total = take(1)[0] if up and linked else None
    _, core, far, _ = position()
    straight = (core ^ far) == 0
    at = [tile_of(tiles, level, v) for v in range(rows)]
    if total is not None:
        total[...] = jnp.zeros_like(total)
    if down:
        values = []
        for v in range(rows):
            mine, other = (one, two) if v < half else (two, one)
            index = (max(level - 1, 0), v % half)
            current = jnp.where(straight, mine[index], other[index]).astype(F32)
            if linked:
                picked = [solved[at_block] for at_block in places(level - 1, v, rows, fanout, sources)]
                coupled = dot(
                    jnp.concatenate(picked, axis=1),
                    jnp.concatenate([at[v](k) for k in range(fanout)], axis=1),
                    NT,
                )
                current = current - coupled
            values.append(current.astype(BF16))
        values = [dot(values[v], at[v](last), NT).astype(BF16) for v in range(rows)]
        if not up:
            for v in range(rows):
                out_f[v] = values[v]
            return
    else:
        values = []
        for v in range(rows):
            incoming = crossed[v].astype(F32)
            for c in range(chips):
                incoming = incoming + returned[c, 0, v].astype(F32)
            values.append((stored[v].astype(F32) - incoming).astype(BF16))
    answers = [dot(values[v], at[v](last), NN) for v in range(rows)]
    for v in range(half):
        result[0][v] = jnp.where(straight, answers[v], answers[v + half])
        result[1][v] = jnp.where(straight, answers[v + half], answers[v])
    if not linked:
        return
    size = answers[0].shape[1]
    for v in range(rows):
        terms = dot(
            answers[v].astype(BF16),
            jnp.concatenate([at[v](k) for k in range(fanout)], axis=1),
            NN,
        )
        for k, at_block in enumerate(places(level - 1, v, rows, fanout, sources)):
            total[at_block] += terms[:, k * size : (k + 1) * size]
    for c in range(chips):
        for h in range(2):
            base = (2 * c + h) * rows
            sent[c, h] = total[base : base + rows].astype(BF16)


def finish_kernel(spans, *refs):
    _, core, _, near = position()
    refs, out = refs[: 2 * len(spans)], refs[-1]
    upper = core == 1
    for j, levels in enumerate(spans):
        one, two = refs[2 * j], refs[2 * j + 1]
        half = one.shape[1]
        for i, place in enumerate(levels):
            for t in range(half):
                at = t ^ (near * 2)
                a, b = one[i, at], two[i, at]
                out[:, place, t, :] = jnp.where(upper, b, a)
                out[:, place, t + half, :] = jnp.where(upper, a, b)


VMEM = pl.BlockSpec(memory_space=pltpu.VMEM)
SMEM = pl.BlockSpec(memory_space=pltpu.SMEM)


def params():
    return pltpu.CompilerParams(vmem_limit_bytes=32 * 1024 * 1024)


def on_device(right_side, diag_tiles, off_tiles, src_part, src_slot):
    columns, levels, rows, size = right_side.shape
    fanout = src_part.shape[2]
    links = levels - 1
    half = rows // 2
    nodes = lax.axis_size("node")
    group = lax.axis_size("rhs")
    chips = nodes // 2
    both = ("node", "rhs")

    def shift(x, node_bits, z_bits):
        pairs = [
            (n * group + z, (n ^ node_bits) * group + (z ^ z_bits))
            for n in range(nodes)
            for z in range(group)
        ]
        return lax.ppermute(x, both, pairs)

    def turn(x, flip, back):
        pairs = []
        for n in range(nodes):
            for z in range(group):
                a, b = n & 1, z >> 1
                target = ((n & ~1) | b) * group + (((a ^ flip) << 1) | (z & 1))
                pairs.append((n * group + z, target))
        if back:
            pairs = [(b, a) for a, b in pairs]
        return lax.ppermute(x, both, pairs)

    def after(x, *others):
        return lax.optimization_barrier((x, *others))[0]

    first = diag_tiles[0][:, None]
    first_near = shift(first, 0, 1)
    first_tiles = [first, first_near, shift(first, 1, 0), shift(first_near, 1, 0)]

    def prepare(first, count, narrow, right):
        shape = jax.ShapeDtypeStruct((count, half, columns, size), narrow)
        pair = pl.pallas_call(
            functools.partial(prep_kernel, first),
            in_specs=[VMEM],
            out_specs=[VMEM, VMEM],
            out_shape=[shape, shape],
            compiler_params=params(),
        )(right)
        return [turn(pair[0], 0, False), turn(pair[1], 1, False)]

    first_right = prepare(0, 1, BF16, right_side)
    own = jnp.concatenate([off_tiles, diag_tiles[1:, :, None]], axis=2)
    own_swapped = shift(after(own, first_near), 1, 0)
    near = {}

    def fetch(level, *others):
        if level < levels:
            near[level] = shift(after(own[level - 1], *others), 0, 1)

    def tiles_of(level, *others):
        if level == 0:
            return first_tiles
        return [own, near[level], own_swapped, shift(after(near[level], *others), 1, 0)]

    sources = [src_part, src_slot, shift(src_part, 1, 0), shift(src_slot, 1, 0)]
    vec = (rows, columns, size)

    def run(level, tiles, down, up, inputs):
        linked = level > 0
        config = dict(rows=rows, fanout=fanout, chips=chips, level=level, down=down, up=up)
        args = sources + list(tiles) + list(inputs)
        shapes, scratch = [], []
        if not up:
            shapes.append(jax.ShapeDtypeStruct(vec, BF16))
        else:
            shapes += [jax.ShapeDtypeStruct((half, columns, size), F32)] * 2
            if linked:
                shapes.append(jax.ShapeDtypeStruct((chips, 2) + vec, BF16))
                scratch.append(pltpu.VMEM((2 * chips * rows, columns, size), F32))
        dots = rows * ((fanout if linked else 0) + 1) * (int(down) + int(up))
        return pl.pallas_call(
            functools.partial(level_kernel, config),
            in_specs=[SMEM] * 4 + [VMEM] * (len(args) - 4),
            out_specs=[VMEM] * len(shapes),
            out_shape=shapes,
            scratch_shapes=scratch,
            compiler_params=params(),
            cost_estimate=pl.CostEstimate(
                flops=2 * dots * columns * size * size,
                bytes_accessed=dots * size * size * 2,
                transcendentals=0,
            ),
        )(*args)

    lanes = [[2 * c + k for c in range(chips)] for k in range(2)]

    def swap(x):
        return lax.all_to_all(x, "node", 0, 0, tiled=True, axis_index_groups=lanes)

    def exchange(value):
        other = shift(value, 0, 2)
        pair = jnp.stack([value, other])
        spread = swap(jnp.broadcast_to(pair[None], (chips,) + pair.shape))
        return other, spread.reshape((2 * chips * rows,) + vec[1:])

    stored = []
    tiles = [tiles_of(0)]
    fetch(1, first_near)
    inputs = first_right
    for level in range(levels - 1):
        (value,) = run(level, tiles[level], True, False, inputs)
        stored.append(value)
        other, arrived = exchange(value)
        if level == 0:
            rest_right = prepare(1, links, F32, after(right_side, other))
        inputs = rest_right + [arrived]
        tiles.append(tiles_of(level + 1, value))
        fetch(level + 2, other)
    results = [None] * levels
    one, two, sent = run(levels - 1, tiles[-1], True, True, inputs)
    results[levels - 1] = (one, two)
    for level in range(levels - 2, -1, -1):
        returned = swap(sent)
        crossed = shift(jnp.sum(returned[:, 1].astype(F32), axis=0).astype(BF16), 0, 2)
        inputs = [stored[level], crossed, returned]
        one, two, *sent = run(level, tiles[level], False, True, inputs)
        sent = sent[0] if sent else None
        results[level] = (one, two)

    def home(wanted):
        one = jnp.stack([results[x][0] for x in wanted])
        two = jnp.stack([results[x][1] for x in wanted])
        return turn(one, 0, True), turn(two, 1, True)

    groups = [list(range(levels - 1, 1, -1)), [1], [0]]
    early = []
    for wanted in groups[:-1]:
        early += home(wanted)
    final = home(groups[-1])
    return pl.pallas_call(
        functools.partial(finish_kernel, groups),
        in_specs=[VMEM] * (2 * len(groups)),
        out_specs=VMEM,
        out_shape=jax.ShapeDtypeStruct(right_side.shape, F32),
        compiler_params=params(),
    )(*early, *final)


def solution(mesh):
    placed = (
        P("rhs", None, "node", None),
        P(None, ("node", "rhs"), None, None),
        P(None, ("node", "rhs"), None, None, None),
        P(None, "node", None),
        P(None, "node", None),
    )
    return jax.shard_map(
        on_device,
        mesh=mesh,
        in_specs=placed,
        out_specs=P("rhs", None, "node", None),
        check_vma=False,
    )
```

```python
import functools

import jax
import jax.numpy as jnp
from jax import lax
from jax.experimental import pallas as pl
from jax.experimental.pallas import tpu as pltpu
from jax.sharding import PartitionSpec as P

F32 = jnp.float32
BF16 = jnp.bfloat16
NT = (((1,), (1,)), ((), ()))
NN = (((1,), (0,)), ((), ()))

FAR, NEAR = 1, 0
TWIN = 2


def dot(a, b, dims):
    return lax.dot_general(a, b, dims, preferred_element_type=F32)


def position():
    node, z = lax.axis_index("node"), lax.axis_index("rhs")
    return (node >> 1) & 1, (z >> FAR) & 1, (z >> NEAR) & 1


def row_of(far, t):
    return 2 * ((far << FAR) | ((t >> 1) << NEAR)) + (t & 1)


def prep_kernel(first, right, one, two):
    twin, _, near = position()
    upper = twin == 1
    for i in range(one.shape[0]):
        for t in range(one.shape[1]):
            low = right[:, first + i, row_of(0, t), :]
            high = right[:, first + i, row_of(1, t), :]
            at = t ^ (near * 2)
            one[i, at] = jnp.where(upper, high, low).astype(one.dtype)
            two[i, at] = jnp.where(upper, low, high).astype(two.dtype)


def level_kernel(config, *refs):
    refs = list(refs)
    take = lambda n: [refs.pop(0) for _ in range(n)]
    rows, fanout, links = config["rows"], config["fanout"], config["links"]
    level, down, up = config["level"], config["down"], config["up"]
    half = rows // 2
    linked = level > 0
    last = fanout if linked else 0
    place = take(1)[0] if linked else None
    tiles = take(4)
    if down:
        one, two = take(2)
        solved = take(1)[0] if linked else None
    else:
        stored, kept, returned = take(3)
    out_f = take(1)[0] if not up else None
    if up:
        result = take(2)
        keep, sent = take(2) if linked else (None, None)
    total = take(1)[0] if up and linked else None
    twin, far, near = position()
    straight = (twin ^ far) == 0

    def tile(v, k):
        ref, at = tiles[v // 2], config["at"][v // 2]
        return ref[v % 2, k] if at is None else ref[at, v % 2, k]

    def wide(v):
        return jnp.concatenate([tile(v, k) for k in range(fanout)], axis=1)

    def places(v):
        t = v % half
        row = ((far << FAR) | (((t >> 1) ^ near) << NEAR)) * 2 + (t & 1)
        base = (((v // half) * links + level - 1) * rows + row) * fanout
        return [place[base + k] for k in range(fanout)]

    if total is not None:
        total[...] = jnp.zeros_like(total)
    if down:
        values = []
        for v in range(rows):
            mine, other = (one, two) if v < half else (two, one)
            index = (max(level - 1, 0), v % half)
            current = jnp.where(straight, mine[index], other[index]).astype(F32)
            if linked:
                picked = jnp.concatenate([solved[at] for at in places(v)], axis=1)
                current = current - dot(picked, wide(v), NT)
            values.append(current.astype(BF16))
        values = [dot(values[v], tile(v, last), NT).astype(BF16) for v in range(rows)]
        if not up:
            for v in range(rows):
                out_f[v] = values[v]
            return
    else:
        values = []
        for v in range(rows):
            incoming = kept[v] + returned[v].astype(F32)
            values.append((stored[v].astype(F32) - incoming).astype(BF16))
    answers = [dot(values[v], tile(v, last), NN) for v in range(rows)]
    for v in range(half):
        result[0][v] = jnp.where(straight, answers[v], answers[v + half])
        result[1][v] = jnp.where(straight, answers[v + half], answers[v])
    if not linked:
        return
    size = answers[0].shape[1]
    for v in range(rows):
        terms = dot(answers[v].astype(BF16), wide(v), NN)
        for k, at in enumerate(places(v)):
            total[at] += terms[:, k * size : (k + 1) * size]
    middle = total.shape[0] // 2
    keep[...] = total[:middle]
    sent[...] = total[middle:].astype(BF16)


def finish_kernel(spans, *refs):
    twin, _, near = position()
    refs, out = refs[: 2 * len(spans)], refs[-1]
    upper = twin == 1
    for j, levels in enumerate(spans):
        one, two = refs[2 * j], refs[2 * j + 1]
        for i, place in enumerate(levels):
            for t in range(one.shape[1]):
                at = t ^ (near * 2)
                a, b = one[i, at], two[i, at]
                out[:, place, row_of(0, t), :] = jnp.where(upper, b, a)
                out[:, place, row_of(1, t), :] = jnp.where(upper, a, b)


VMEM = pl.BlockSpec(memory_space=pltpu.VMEM)
SMEM = pl.BlockSpec(memory_space=pltpu.SMEM)


def params():
    return pltpu.CompilerParams(vmem_limit_bytes=32 * 1024 * 1024)


def on_device(right_side, diag_tiles, off_tiles, src_part, src_slot):
    columns, levels, rows, size = right_side.shape
    fanout = src_part.shape[2]
    links = levels - 1
    half = rows // 2
    nodes = lax.axis_size("node")
    group = lax.axis_size("rhs")
    node, z = lax.axis_index("node"), lax.axis_index("rhs")
    both = ("node", "rhs")
    far_bit, near_bit = 1 << FAR, 1 << NEAR
    bits = [b for b in (1 << i for i in range(2, nodes.bit_length() - 1))] + [1]
    blocks = nodes * rows

    def shift(x, node_bits, z_bits):
        pairs = [
            (n * group + q, (n ^ node_bits) * group + (q ^ z_bits))
            for n in range(nodes)
            for q in range(group)
        ]
        return lax.ppermute(x, both, pairs)

    def turn(x, flip, back):
        pairs = []
        for n in range(nodes):
            for q in range(group):
                a, b = (n >> 1) & 1, (q >> FAR) & 1
                target = ((n & ~TWIN) | (b << 1)) * group + ((q & ~far_bit) | ((a ^ flip) << FAR))
                pairs.append((n * group + q, target))
        if back:
            pairs = [(b, a) for a, b in pairs]
        return lax.ppermute(x, both, pairs)

    def after(x, *others):
        return lax.optimization_barrier((x, *others))[0]

    def prepare(first, count, narrow, right):
        shape = jax.ShapeDtypeStruct((count, half, columns, size), narrow)
        pair = pl.pallas_call(
            functools.partial(prep_kernel, first),
            in_specs=[VMEM],
            out_specs=[VMEM, VMEM],
            out_shape=[shape, shape],
            compiler_params=params(),
        )(right)
        return [turn(pair[0], 0, False), turn(pair[1], 1, False)]

    first_right = prepare(0, 1, BF16, right_side)
    first = diag_tiles[0][:, None]
    first_near = shift(first, 0, near_bit)
    first_tiles = [first, first_near, shift(first, TWIN, 0), shift(first_near, TWIN, 0)]

    own = jnp.concatenate([off_tiles, diag_tiles[1:, :, None]], axis=2)
    held = {}

    def fetch(level, *others):
        if level < levels:
            piece = after(own[level - 1], *others)
            near = shift(piece, 0, near_bit)
            across = shift(piece, TWIN, 0)
            if level < links:
                corner = shift(near, TWIN, 0)
            else:
                corner = shift(across, 0, near_bit)
            held[level] = [own, near, across, corner]

    coded = src_part * rows + src_slot
    codes = jnp.stack([coded, shift(coded, TWIN, 0)])
    part, slot = codes // rows, codes % rows
    rel = part ^ node
    unit = ((slot >> 1 >> FAR) ^ (z >> FAR)) & 1
    for i, bit in enumerate(bits):
        unit = unit + (((rel & bit) != 0).astype(jnp.int32) << (i + 1))
    inner = (((slot >> 1 >> NEAR) ^ (z >> NEAR)) & 1) * 2 + (slot & 1) + ((rel >> 1) & 1) * half
    place = (unit * rows + inner).reshape(-1)

    vec = (rows, columns, size)

    def run(level, down, up, inputs):
        linked = level > 0
        tiles = held[level] if linked else first_tiles
        at = [level - 1, None, None, None] if linked else [None] * 4
        config = dict(
            rows=rows, fanout=fanout, links=links, level=level, down=down, up=up, at=at
        )
        args = ([place] if linked else []) + list(tiles) + list(inputs)
        shapes, scratch = [], []
        if not up:
            shapes.append(jax.ShapeDtypeStruct(vec, BF16))
        else:
            shapes += [jax.ShapeDtypeStruct((half, columns, size), F32)] * 2
            if linked:
                part_shape = (blocks // 2,) + vec[1:]
                shapes += [jax.ShapeDtypeStruct(part_shape, t) for t in (F32, BF16)]
                scratch.append(pltpu.VMEM((blocks,) + vec[1:], F32))
        dots = rows * ((fanout if linked else 0) + 1) * (int(down) + int(up))
        return pl.pallas_call(
            functools.partial(level_kernel, config),
            in_specs=([SMEM] if linked else []) + [VMEM] * (len(args) - int(linked)),
            out_specs=[VMEM] * len(shapes),
            out_shape=shapes,
            scratch_shapes=scratch,
            compiler_params=params(),
            cost_estimate=pl.CostEstimate(
                flops=2 * dots * columns * size * size,
                bytes_accessed=dots * size * size * 2,
                transcendentals=0,
            ),
        )(*args)

    def gather(value):
        crossed = shift(value, 0, far_bit)
        gathered = jnp.concatenate([value, crossed])
        for bit in bits:
            gathered = jnp.concatenate([gathered, shift(gathered, bit, 0)])
        return crossed, gathered

    def scatter(keep, sent):
        for i, bit in enumerate(bits[::-1]):
            summed = keep + shift(sent, bit, 0).astype(F32)
            middle = summed.shape[0] // 2
            keep, sent = summed[:middle], summed[middle:].astype(BF16)
        return [keep, shift(sent, 0, far_bit)]

    stored = []
    fetch(1, *first_right)
    inputs = first_right
    for level in range(levels - 1):
        (value,) = run(level, True, False, inputs)
        stored.append(value)
        crossed, gathered = gather(value)
        if level == 0:
            rest_right = prepare(1, links, F32, after(right_side, crossed))
        inputs = rest_right + [gathered]
        fetch(level + 2, crossed)
    results = [None] * levels
    one, two, *sums = run(levels - 1, True, True, inputs)
    results[levels - 1] = (one, two)
    for level in range(levels - 2, -1, -1):
        one, two, *sums = run(level, False, True, [stored[level]] + scatter(*sums))
        results[level] = (one, two)

    def home(wanted):
        one = jnp.stack([results[x][0] for x in wanted])
        two = jnp.stack([results[x][1] for x in wanted])
        return turn(one, 0, True), turn(two, 1, True)

    groups = [list(range(levels - 1, 1, -1)), [1], [0]]
    early = []
    for wanted in groups[:-1]:
        early += home(wanted)
    final = home(groups[-1])
    return pl.pallas_call(
        functools.partial(finish_kernel, groups),
        in_specs=[VMEM] * (2 * len(groups)),
        out_specs=VMEM,
        out_shape=jax.ShapeDtypeStruct(right_side.shape, F32),
        compiler_params=params(),
    )(*early, *final)


def solution(mesh):
    placed = (
        P("rhs", None, "node", None),
        P(None, ("node", "rhs"), None, None),
        P(None, ("node", "rhs"), None, None, None),
        P(None, "node", None),
        P(None, "node", None),
    )
    return jax.shard_map(
        on_device,
        mesh=mesh,
        in_specs=placed,
        out_specs=P("rhs", None, "node", None),
        check_vma=False,
    )
```

```python
import functools

import jax
import jax.numpy as jnp
from jax import lax
from jax.experimental import pallas as pl
from jax.experimental.pallas import tpu as pltpu
from jax.sharding import PartitionSpec as P

F32 = jnp.float32
BF16 = jnp.bfloat16
NT = (((1,), (1,)), ((), ()))
NN = (((1,), (0,)), ((), ()))

FAR, NEAR = 0, 1
TWIN = 2


def dot(a, b, dims):
    return lax.dot_general(a, b, dims, preferred_element_type=F32)


def position():
    node, z = lax.axis_index("node"), lax.axis_index("rhs")
    return (node >> 1) & 1, (z >> FAR) & 1, (z >> NEAR) & 1


def row_of(far, t):
    return 2 * ((far << FAR) | ((t >> 1) << NEAR)) + (t & 1)


def prep_kernel(first, right, one, two):
    twin, _, near = position()
    upper = twin == 1
    for i in range(one.shape[0]):
        for t in range(one.shape[1]):
            low = right[:, first + i, row_of(0, t), :]
            high = right[:, first + i, row_of(1, t), :]
            at = t ^ (near * 2)
            one[i, at] = jnp.where(upper, high, low).astype(one.dtype)
            two[i, at] = jnp.where(upper, low, high).astype(two.dtype)


def level_kernel(config, *refs):
    refs = list(refs)
    take = lambda n: [refs.pop(0) for _ in range(n)]
    rows, fanout, links = config["rows"], config["fanout"], config["links"]
    level, down, up = config["level"], config["down"], config["up"]
    half = rows // 2
    linked = level > 0
    last = fanout if linked else 0
    place = take(1)[0] if linked else None
    tiles = take(4)
    if down:
        one, two = take(2)
        solved = take(1)[0] if linked else None
    else:
        stored, kept, returned = take(3)
    out_f = take(1)[0] if not up else None
    if up:
        result = take(2)
        keep, sent = take(2) if linked else (None, None)
    total = take(1)[0] if up and linked else None
    twin, far, near = position()
    straight = (twin ^ far) == 0

    def tile(v, k):
        return tiles[v // 2][v % 2, k]

    def wide(v):
        return jnp.concatenate([tile(v, k) for k in range(fanout)], axis=1)

    def places(v):
        t = v % half
        row = ((far << FAR) | (((t >> 1) ^ near) << NEAR)) * 2 + (t & 1)
        base = (((v // half) * links + level - 1) * rows + row) * fanout
        return [place[base + k] for k in range(fanout)]

    if total is not None:
        total[...] = jnp.zeros_like(total)
    if down:
        values = []
        for v in range(rows):
            mine, other = (one, two) if v < half else (two, one)
            index = (max(level - 1, 0), v % half)
            current = jnp.where(straight, mine[index], other[index]).astype(F32)
            if linked:
                picked = jnp.concatenate([solved[at] for at in places(v)], axis=1)
                current = current - dot(picked, wide(v), NT)
            values.append(current.astype(BF16))
        values = [dot(values[v], tile(v, last), NT).astype(BF16) for v in range(rows)]
        if not up:
            for v in range(rows):
                out_f[v] = values[v]
            return
    else:
        values = []
        for v in range(rows):
            incoming = kept[v] + returned[v].astype(F32)
            values.append((stored[v].astype(F32) - incoming).astype(BF16))
    answers = [dot(values[v], tile(v, last), NN) for v in range(rows)]
    for v in range(half):
        result[0][v] = jnp.where(straight, answers[v], answers[v + half])
        result[1][v] = jnp.where(straight, answers[v + half], answers[v])
    if not linked:
        return
    size = answers[0].shape[1]
    for v in range(rows):
        terms = dot(answers[v].astype(BF16), wide(v), NN)
        for k, at in enumerate(places(v)):
            total[at] += terms[:, k * size : (k + 1) * size]
    middle = total.shape[0] // 2
    keep[...] = total[:middle]
    sent[...] = total[middle:].astype(BF16)


def finish_kernel(spans, *refs):
    twin, _, near = position()
    refs, out = refs[: 2 * len(spans)], refs[-1]
    upper = twin == 1
    for j, levels in enumerate(spans):
        one, two = refs[2 * j], refs[2 * j + 1]
        for i, place in enumerate(levels):
            for t in range(one.shape[1]):
                at = t ^ (near * 2)
                a, b = one[i, at], two[i, at]
                out[:, place, row_of(0, t), :] = jnp.where(upper, b, a)
                out[:, place, row_of(1, t), :] = jnp.where(upper, a, b)


VMEM = pl.BlockSpec(memory_space=pltpu.VMEM)
SMEM = pl.BlockSpec(memory_space=pltpu.SMEM)


def params():
    return pltpu.CompilerParams(vmem_limit_bytes=32 * 1024 * 1024)


def on_device(right_side, diag_tiles, off_tiles, src_part, src_slot):
    columns, levels, rows, size = right_side.shape
    fanout = src_part.shape[2]
    links = levels - 1
    half = rows // 2
    nodes = lax.axis_size("node")
    group = lax.axis_size("rhs")
    node, z = lax.axis_index("node"), lax.axis_index("rhs")
    both = ("node", "rhs")
    far_bit, near_bit = 1 << FAR, 1 << NEAR
    bits = [b for b in (1 << i for i in range(2, nodes.bit_length() - 1))] + [1]
    blocks = nodes * rows

    def shift(x, node_bits, z_bits):
        pairs = [
            (n * group + q, (n ^ node_bits) * group + (q ^ z_bits))
            for n in range(nodes)
            for q in range(group)
        ]
        return lax.ppermute(x, both, pairs)

    def turn(x, flip, back):
        pairs = []
        for n in range(nodes):
            for q in range(group):
                a, b = (n >> 1) & 1, (q >> FAR) & 1
                target = ((n & ~TWIN) | (b << 1)) * group + ((q & ~far_bit) | ((a ^ flip) << FAR))
                pairs.append((n * group + q, target))
        if back:
            pairs = [(b, a) for a, b in pairs]
        return lax.ppermute(x, both, pairs)

    def after(x, *others):
        return lax.optimization_barrier((x, *others))[0]

    def prepare(first, count, narrow, right):
        shape = jax.ShapeDtypeStruct((count, half, columns, size), narrow)
        pair = pl.pallas_call(
            functools.partial(prep_kernel, first),
            in_specs=[VMEM],
            out_specs=[VMEM, VMEM],
            out_shape=[shape, shape],
            compiler_params=params(),
        )(right)
        return [turn(pair[0], 0, False), turn(pair[1], 1, False)]

    first_right = prepare(0, 1, BF16, right_side)
    first = diag_tiles[0][:, None]
    first_near = shift(first, 0, near_bit)
    first_tiles = [first, first_near, shift(first, TWIN, 0), shift(first_near, TWIN, 0)]

    held = {}

    def fetch(level, *others):
        if level < levels:
            piece = jnp.concatenate([off_tiles[level - 1], diag_tiles[level][:, None]], axis=1)
            piece = after(piece, *others)
            near = shift(piece, 0, near_bit)
            across = shift(piece, TWIN, 0)
            held[level] = [piece, near, across]
            return [near, across]
        return []

    coded = src_part * rows + src_slot
    codes = jnp.stack([coded, shift(coded, TWIN, 0)])
    part, slot = codes // rows, codes % rows
    rel = part ^ node
    unit = ((slot >> 1 >> FAR) ^ (z >> FAR)) & 1
    for i, bit in enumerate(bits):
        unit = unit + (((rel & bit) != 0).astype(jnp.int32) << (i + 1))
    inner = (((slot >> 1 >> NEAR) ^ (z >> NEAR)) & 1) * 2 + (slot & 1) + ((rel >> 1) & 1) * half
    place = (unit * rows + inner).reshape(-1)

    vec = (rows, columns, size)

    def run(level, down, up, inputs):
        linked = level > 0
        tiles = held[level] if linked else first_tiles
        config = dict(rows=rows, fanout=fanout, links=links, level=level, down=down, up=up)
        args = ([place] if linked else []) + list(tiles) + list(inputs)
        shapes, scratch = [], []
        if not up:
            shapes.append(jax.ShapeDtypeStruct(vec, BF16))
        else:
            shapes += [jax.ShapeDtypeStruct((half, columns, size), F32)] * 2
            if linked:
                part_shape = (blocks // 2,) + vec[1:]
                shapes += [jax.ShapeDtypeStruct(part_shape, t) for t in (F32, BF16)]
                scratch.append(pltpu.VMEM((blocks,) + vec[1:], F32))
        dots = rows * ((fanout if linked else 0) + 1) * (int(down) + int(up))
        return pl.pallas_call(
            functools.partial(level_kernel, config),
            in_specs=([SMEM] if linked else []) + [VMEM] * (len(args) - int(linked)),
            out_specs=[VMEM] * len(shapes),
            out_shape=shapes,
            scratch_shapes=scratch,
            compiler_params=params(),
            cost_estimate=pl.CostEstimate(
                flops=2 * dots * columns * size * size,
                bytes_accessed=dots * size * size * 2,
                transcendentals=0,
            ),
        )(*args)

    def gather(value, level, *others):
        crossed = shift(value, 0, far_bit)
        if level + 1 < levels:
            crossed = after(crossed, *others)
            held[level + 1].append(shift(held[level + 1][1], TWIN, 0))
        gathered = jnp.concatenate([value, crossed])
        for bit in bits:
            gathered = jnp.concatenate([gathered, shift(gathered, bit, 0)])
        return crossed, gathered

    def scatter(keep, sent):
        for i, bit in enumerate(bits[::-1]):
            summed = keep + shift(sent, bit, 0).astype(F32)
            middle = summed.shape[0] // 2
            keep, sent = summed[:middle], summed[middle:].astype(BF16)
        return [keep, shift(sent, 0, far_bit)]

    stored = []
    owned = fetch(1, first_near)
    rest_right = prepare(1, links, F32, after(right_side, *first_right))
    inputs = first_right
    for level in range(levels - 1):
        (value,) = run(level, True, False, inputs)
        stored.append(value)
        crossed, gathered = gather(value, level, *owned, *(rest_right if level == 0 else []))
        owned = fetch(level + 2, *owned)
        inputs = rest_right + [gathered]
    results = [None] * levels
    one, two, *sums = run(levels - 1, True, True, inputs)
    results[levels - 1] = (one, two)
    for level in range(levels - 2, -1, -1):
        one, two, *sums = run(level, False, True, [stored[level]] + scatter(*sums))
        results[level] = (one, two)

    def home(wanted):
        one = jnp.stack([results[x][0] for x in wanted])
        two = jnp.stack([results[x][1] for x in wanted])
        return turn(one, 0, True), turn(two, 1, True)

    groups = [list(range(levels - 1, 1, -1)), [1, 0]]
    early = []
    for wanted in groups[:-1]:
        early += home(wanted)
    final = home(groups[-1])
    return pl.pallas_call(
        functools.partial(finish_kernel, groups),
        in_specs=[VMEM] * (2 * len(groups)),
        out_specs=VMEM,
        out_shape=jax.ShapeDtypeStruct(right_side.shape, F32),
        compiler_params=params(),
    )(*early, *final)


def solution(mesh):
    placed = (
        P("rhs", None, "node", None),
        P(None, ("node", "rhs"), None, None),
        P(None, ("node", "rhs"), None, None, None),
        P(None, "node", None),
        P(None, "node", None),
    )
    return jax.shard_map(
        on_device,
        mesh=mesh,
        in_specs=placed,
        out_specs=P("rhs", None, "node", None),
        check_vma=False,
    )
```

```python
import functools

import jax
import jax.numpy as jnp
from jax import lax
from jax.experimental import pallas as pl
from jax.experimental.pallas import tpu as pltpu
from jax.sharding import PartitionSpec as P

F32 = jnp.float32
BF16 = jnp.bfloat16
NT = (((1,), (1,)), ((), ()))
NN = (((1,), (0,)), ((), ()))

FAR, NEAR = 1, 0
TWIN = 2


def dot(a, b, dims):
    return lax.dot_general(a, b, dims, preferred_element_type=F32)


def position():
    node, z = lax.axis_index("node"), lax.axis_index("rhs")
    return (node >> 1) & 1, (z >> FAR) & 1, (z >> NEAR) & 1


def row_of(far, t):
    return 2 * ((far << FAR) | ((t >> 1) << NEAR)) + (t & 1)


def prep_kernel(first, right, one, two):
    twin, _, near = position()
    upper = twin == 1
    for i in range(one.shape[0]):
        for t in range(one.shape[1]):
            low = right[:, first + i, row_of(0, t), :]
            high = right[:, first + i, row_of(1, t), :]
            at = t ^ (near * 2)
            one[i, at] = jnp.where(upper, high, low).astype(one.dtype)
            two[i, at] = jnp.where(upper, low, high).astype(two.dtype)


def level_kernel(config, *refs):
    refs = list(refs)
    take = lambda n: [refs.pop(0) for _ in range(n)]
    rows, fanout, links = config["rows"], config["fanout"], config["links"]
    level, down, up = config["level"], config["down"], config["up"]
    half = rows // 2
    linked = level > 0
    last = fanout if linked else 0
    place = take(1)[0] if linked else None
    tiles = take(4)
    if down:
        one, two = take(2)
        solved = take(1)[0] if linked else None
    else:
        stored, kept = take(2)
        returned = take(config["partners"])
    out_f = take(1)[0] if not up else None
    if up:
        result = take(2)
        keep, sent = take(2) if linked else (None, None)
    total = take(1)[0] if up and linked else None
    twin, far, near = position()
    straight = (twin ^ far) == 0

    def tile(v, k):
        return tiles[v // 2][v % 2, k]

    def wide(v):
        return jnp.concatenate([tile(v, k) for k in range(fanout)], axis=1)

    def places(v):
        t = v % half
        row = ((far << FAR) | (((t >> 1) ^ near) << NEAR)) * 2 + (t & 1)
        base = (((v // half) * links + level - 1) * rows + row) * fanout
        return [place[base + k] for k in range(fanout)]

    if total is not None:
        total[...] = jnp.zeros_like(total)
    if down:
        values = []
        for v in range(rows):
            mine, other = (one, two) if v < half else (two, one)
            index = (max(level - 1, 0), v % half)
            current = jnp.where(straight, mine[index], other[index]).astype(F32)
            if linked:
                picked = jnp.concatenate([solved[at] for at in places(v)], axis=1)
                current = current - dot(picked, wide(v), NT)
            values.append(current.astype(BF16))
        values = [dot(values[v], tile(v, last), NT).astype(BF16) for v in range(rows)]
        if not up:
            for v in range(rows):
                out_f[v] = values[v]
            return
    else:
        values = []
        for v in range(rows):
            incoming = kept[v]
            for block in returned:
                incoming = incoming + block[v].astype(F32)
            values.append((stored[v].astype(F32) - incoming).astype(BF16))
    answers = [dot(values[v], tile(v, last), NN) for v in range(rows)]
    for v in range(half):
        result[0][v] = jnp.where(straight, answers[v], answers[v + half])
        result[1][v] = jnp.where(straight, answers[v + half], answers[v])
    if not linked:
        return
    size = answers[0].shape[1]
    for v in range(rows):
        terms = dot(answers[v].astype(BF16), wide(v), NN)
        for k, at in enumerate(places(v)):
            total[at] += terms[:, k * size : (k + 1) * size]
    middle = total.shape[0] // 2
    keep[...] = total[:middle]
    sent[...] = total[middle:].astype(BF16)


def finish_kernel(spans, *refs):
    twin, _, near = position()
    refs, out = refs[: 2 * len(spans)], refs[-1]
    upper = twin == 1
    for j, levels in enumerate(spans):
        one, two = refs[2 * j], refs[2 * j + 1]
        for i, place in enumerate(levels):
            for t in range(one.shape[1]):
                at = t ^ (near * 2)
                a, b = one[i, at], two[i, at]
                out[:, place, row_of(0, t), :] = jnp.where(upper, b, a)
                out[:, place, row_of(1, t), :] = jnp.where(upper, a, b)


VMEM = pl.BlockSpec(memory_space=pltpu.VMEM)
SMEM = pl.BlockSpec(memory_space=pltpu.SMEM)


def params():
    return pltpu.CompilerParams(vmem_limit_bytes=32 * 1024 * 1024)


def on_device(right_side, diag_tiles, off_tiles, src_part, src_slot):
    columns, levels, rows, size = right_side.shape
    fanout = src_part.shape[2]
    links = levels - 1
    half = rows // 2
    nodes = lax.axis_size("node")
    group = lax.axis_size("rhs")
    node, z = lax.axis_index("node"), lax.axis_index("rhs")
    both = ("node", "rhs")
    far_bit, near_bit = 1 << FAR, 1 << NEAR
    bits = [1 << i for i in range(2, nodes.bit_length() - 1)]
    partners = nodes // 2
    blocks = nodes * rows

    def shift(x, node_bits, z_bits):
        pairs = [
            (n * group + q, (n ^ node_bits) * group + (q ^ z_bits))
            for n in range(nodes)
            for q in range(group)
        ]
        return lax.ppermute(x, both, pairs)

    def turn(x, flip, back):
        pairs = []
        for n in range(nodes):
            for q in range(group):
                a, b = (n >> 1) & 1, (q >> FAR) & 1
                target = ((n & ~TWIN) | (b << 1)) * group + ((q & ~far_bit) | ((a ^ flip) << FAR))
                pairs.append((n * group + q, target))
        if back:
            pairs = [(b, a) for a, b in pairs]
        return lax.ppermute(x, both, pairs)

    def after(x, *others):
        return lax.optimization_barrier((x, *others))[0]

    def prepare(first, count, narrow, right):
        shape = jax.ShapeDtypeStruct((count, half, columns, size), narrow)
        pair = pl.pallas_call(
            functools.partial(prep_kernel, first),
            in_specs=[VMEM],
            out_specs=[VMEM, VMEM],
            out_shape=[shape, shape],
            compiler_params=params(),
        )(right)
        return [turn(pair[0], 0, False), turn(pair[1], 1, False)]

    first_right = prepare(0, 1, BF16, right_side)
    first = diag_tiles[0][:, None]
    first_near = shift(first, 0, near_bit)
    first_tiles = [first, first_near, shift(first, TWIN, 0), shift(first_near, TWIN, 0)]
    near, across, corner, pieces = {}, {}, {}, {}

    def piece_of(level):
        if level not in pieces:
            pieces[level] = jnp.concatenate(
                [off_tiles[level - 1], diag_tiles[level][:, None]], axis=1
            )
        return pieces[level]

    def fetch_near(level, *others):
        if level < levels:
            near[level] = shift(after(piece_of(level), *others), 0, near_bit)

    def fetch_across(level, *others):
        if level < levels:
            across[level] = shift(after(piece_of(level), *others), TWIN, 0)

    def fetch_corner(level):
        if level % 2:
            corner[level] = shift(after(near[level], across[level]), TWIN, 0)
        else:
            corner[level] = shift(after(across[level], near[level]), 0, near_bit)

    coded = src_part * rows + src_slot
    codes = jnp.stack([coded, shift(coded, TWIN, 0)])
    part, slot = codes // rows, codes % rows
    rel = part ^ node
    unit = ((slot >> 1 >> FAR) ^ (z >> FAR)) & 1
    for i, bit in enumerate(bits + [1]):
        unit = unit + (((rel & bit) != 0).astype(jnp.int32) << (i + 1))
    inner = (((slot >> 1 >> NEAR) ^ (z >> NEAR)) & 1) * 2 + (slot & 1) + ((rel >> 1) & 1) * half
    place = (unit * rows + inner).reshape(-1)

    vec = (rows, columns, size)

    def run(level, down, up, inputs):
        linked = level > 0
        tiles = first_tiles
        if linked:
            tiles = [pieces[level], near[level], across[level], corner[level]]
        config = dict(rows=rows, fanout=fanout, links=links, level=level, down=down, up=up, partners=partners - 1)
        args = ([place] if linked else []) + list(tiles) + list(inputs)
        shapes, scratch = [], []
        if not up:
            shapes.append(jax.ShapeDtypeStruct(vec, BF16))
        else:
            shapes += [jax.ShapeDtypeStruct((half, columns, size), F32)] * 2
            if linked:
                part_shape = (blocks // 2,) + vec[1:]
                shapes += [jax.ShapeDtypeStruct(part_shape, t) for t in (F32, BF16)]
                scratch.append(pltpu.VMEM((blocks,) + vec[1:], F32))
        dots = rows * ((fanout if linked else 0) + 1) * (int(down) + int(up))
        return pl.pallas_call(
            functools.partial(level_kernel, config),
            in_specs=([SMEM] if linked else []) + [VMEM] * (len(args) - int(linked)),
            out_specs=[VMEM] * len(shapes),
            out_shape=shapes,
            scratch_shapes=scratch,
            compiler_params=params(),
            cost_estimate=pl.CostEstimate(
                flops=2 * dots * columns * size * size,
                bytes_accessed=dots * size * size * 2,
                transcendentals=0,
            ),
        )(*args)

    def flip(x, d):
        node_bits = sum(bit for i, bit in enumerate(bits) if (d >> (i + 1)) & 1)
        return shift(x, node_bits, far_bit if d & 1 else 0)

    def gather(value, *early):
        met = jnp.concatenate([value] + [flip(value, d) for d in range(1, partners)])
        met = after(met, *early)
        return jnp.concatenate([met, shift(met, 1, 0)])

    def scatter(keep, sent):
        summed = keep + shift(sent, 1, 0).astype(F32)
        pieces = [summed[d * rows : (d + 1) * rows] for d in range(partners)]
        return pieces[:1] + [flip(x.astype(BF16), d) for d, x in enumerate(pieces) if d > 0]

    stored = []
    fetch_near(1, first_near)
    fetch_across(1, first_tiles[3])
    inputs = first_right
    for level in range(levels - 1):
        (value,) = run(level, True, False, inputs)
        stored.append(value)
        after_next = level + 2
        if level == 0:
            rest_right = prepare(1, links, F32, after(right_side, value))
            fetch_near(2, near[1], value)
            early, late = [near[1], across[1]], [near[2]]
        else:
            if level == 1:
                fetch_across(2, value)
            fetch_near(after_next, near[level + 1], value)
            fetch_across(after_next, across[level + 1], *([value] if level > 1 else []))
            early = [across[level + 1], near[level + 1]]
            late = [near[after_next], across[after_next]] if after_next < levels else []
        fetch_corner(level + 1)
        inputs = rest_right + [after(gather(value, *early), *late)]
    results = [None] * levels
    one, two, *sums = run(levels - 1, True, True, inputs)
    results[levels - 1] = (one, two)
    for level in range(levels - 2, -1, -1):
        one, two, *sums = run(level, False, True, [stored[level]] + scatter(*sums))
        results[level] = (one, two)

    def home(wanted):
        one = jnp.stack([results[x][0] for x in wanted])
        two = jnp.stack([results[x][1] for x in wanted])
        return turn(one, 0, True), turn(two, 1, True)

    groups = [list(range(levels - 1, 1, -1)), [1, 0]]
    early = []
    for wanted in groups[:-1]:
        early += home(wanted)
    final = home(groups[-1])
    return pl.pallas_call(
        functools.partial(finish_kernel, groups),
        in_specs=[VMEM] * (2 * len(groups)),
        out_specs=VMEM,
        out_shape=jax.ShapeDtypeStruct(right_side.shape, F32),
        compiler_params=params(),
    )(*early, *final)


def solution(mesh):
    placed = (
        P("rhs", None, "node", None),
        P(None, ("node", "rhs"), None, None),
        P(None, ("node", "rhs"), None, None, None),
        P(None, "node", None),
        P(None, "node", None),
    )
    return jax.shard_map(
        on_device,
        mesh=mesh,
        in_specs=placed,
        out_specs=P("rhs", None, "node", None),
        check_vma=False,
    )
```

```python
import functools

import jax
import jax.numpy as jnp
from jax import lax
from jax.experimental import pallas as pl
from jax.experimental.pallas import tpu as pltpu
from jax.sharding import PartitionSpec as P

F32 = jnp.float32
BF16 = jnp.bfloat16
NT = (((1,), (1,)), ((), ()))
NN = (((1,), (0,)), ((), ()))

FAR, NEAR = 1, 0
TWIN = 2


def dot(a, b, dims):
    return lax.dot_general(a, b, dims, preferred_element_type=F32)


def position():
    node, z = lax.axis_index("node"), lax.axis_index("rhs")
    return (node >> 1) & 1, (z >> FAR) & 1, (z >> NEAR) & 1


def row_of(far, t):
    return 2 * ((far << FAR) | ((t >> 1) << NEAR)) + (t & 1)


def prep_kernel(right, one, two):
    twin, _, near = position()
    upper = twin == 1
    for i in range(one.shape[0]):
        for t in range(one.shape[1]):
            low = right[:, i, row_of(0, t), :]
            high = right[:, i, row_of(1, t), :]
            at = t ^ (near * 2)
            one[i, at] = jnp.where(upper, high, low)
            two[i, at] = jnp.where(upper, low, high)


def level_kernel(config, *refs):
    refs = list(refs)
    take = lambda n: [refs.pop(0) for _ in range(n)]
    rows, fanout, links = config["rows"], config["fanout"], config["links"]
    level, down, up = config["level"], config["down"], config["up"]
    half = rows // 2
    linked = level > 0
    last = fanout if linked else 0
    place = take(1)[0] if linked else None
    tiles = take(max(ref for ref, _ in config["tiles"]) + 1)
    tiles = [(tiles[ref], at) for ref, at in config["tiles"]]
    if down:
        one, two = take(2)
        solved = take(1)[0] if linked else None
    else:
        stored, kept = take(2)
        returned = take(config["partners"])
    out_f = take(1)[0] if not up else None
    if up:
        result = take(2)
        keep, sent = take(2) if linked else (None, None)
    total = take(1)[0] if up and linked else None
    twin, far, near = position()
    straight = (twin ^ far) == 0

    def tile(v, k):
        ref, at = tiles[v // 2]
        return ref[v % 2, k] if at is None else ref[at, v % 2, k]

    def wide(v):
        return jnp.concatenate([tile(v, k) for k in range(fanout)], axis=1)

    def places(v):
        t = v % half
        row = ((far << FAR) | (((t >> 1) ^ near) << NEAR)) * 2 + (t & 1)
        base = (((v // half) * links + level - 1) * rows + row) * fanout
        return [place[base + k] for k in range(fanout)]

    if total is not None:
        total[...] = jnp.zeros_like(total)
    if down:
        values = []
        for v in range(rows):
            mine, other = (one, two) if v < half else (two, one)
            current = jnp.where(straight, mine[level, v % half], other[level, v % half])
            if linked:
                picked = jnp.concatenate([solved[at] for at in places(v)], axis=1)
                current = current - dot(picked, wide(v), NT)
            values.append(current.astype(BF16))
        values = [dot(values[v], tile(v, last), NT).astype(BF16) for v in range(rows)]
        if not up:
            for v in range(rows):
                out_f[v] = values[v]
            return
    else:
        values = []
        for v in range(rows):
            incoming = kept[v]
            for block in returned:
                incoming = incoming + block[v].astype(F32)
            values.append((stored[v].astype(F32) - incoming).astype(BF16))
    answers = [dot(values[v], tile(v, last), NN) for v in range(rows)]
    for v in range(half):
        result[0][v] = jnp.where(straight, answers[v], answers[v + half])
        result[1][v] = jnp.where(straight, answers[v + half], answers[v])
    if not linked:
        return
    size = answers[0].shape[1]
    for v in range(rows):
        terms = dot(answers[v].astype(BF16), wide(v), NN)
        for k, at in enumerate(places(v)):
            total[at] += terms[:, k * size : (k + 1) * size]
    middle = total.shape[0] // 2
    keep[...] = total[:middle]
    sent[...] = total[middle:].astype(BF16)


def finish_kernel(spans, *refs):
    twin, _, near = position()
    refs, out = refs[: 2 * len(spans)], refs[-1]
    upper = twin == 1
    for j, levels in enumerate(spans):
        one, two = refs[2 * j], refs[2 * j + 1]
        for i, place in enumerate(levels):
            for t in range(one.shape[1]):
                at = t ^ (near * 2)
                a, b = one[i, at].astype(F32), two[i, at].astype(F32)
                out[:, place, row_of(0, t), :] = jnp.where(upper, b, a)
                out[:, place, row_of(1, t), :] = jnp.where(upper, a, b)


VMEM = pl.BlockSpec(memory_space=pltpu.VMEM)
SMEM = pl.BlockSpec(memory_space=pltpu.SMEM)


def params():
    return pltpu.CompilerParams(vmem_limit_bytes=32 * 1024 * 1024)


def on_device(right_side, diag_tiles, off_tiles, src_part, src_slot):
    columns, levels, rows, size = right_side.shape
    fanout = src_part.shape[2]
    links = levels - 1
    half = rows // 2
    nodes = lax.axis_size("node")
    group = lax.axis_size("rhs")
    node, z = lax.axis_index("node"), lax.axis_index("rhs")
    both = ("node", "rhs")
    far_bit, near_bit = 1 << FAR, 1 << NEAR
    bits = [1 << i for i in range(2, nodes.bit_length() - 1)]
    partners = nodes // 2
    blocks = nodes * rows

    def shift(x, node_bits, z_bits):
        pairs = [
            (n * group + q, (n ^ node_bits) * group + (q ^ z_bits))
            for n in range(nodes)
            for q in range(group)
        ]
        return lax.ppermute(x, both, pairs)

    def turn(x, flip, back):
        pairs = []
        for n in range(nodes):
            for q in range(group):
                a, b = (n >> 1) & 1, (q >> FAR) & 1
                target = ((n & ~TWIN) | (b << 1)) * group + ((q & ~far_bit) | ((a ^ flip) << FAR))
                pairs.append((n * group + q, target))
        if back:
            pairs = [(b, a) for a, b in pairs]
        return lax.ppermute(x, both, pairs)

    def after(x, *others):
        return lax.optimization_barrier((x, *others))[0]

    shape = jax.ShapeDtypeStruct((levels, half, columns, size), F32)
    pair = pl.pallas_call(
        prep_kernel,
        in_specs=[VMEM],
        out_specs=[VMEM, VMEM],
        out_shape=[shape, shape],
        compiler_params=params(),
    )(right_side)
    right = [turn(pair[0], 0, False), turn(pair[1], 1, False)]
    first = diag_tiles[0][:, None]
    first_near = shift(first, 0, near_bit)
    first_tiles = [first, first_near, shift(first, TWIN, 0), shift(first_near, TWIN, 0)]
    pieces = [None] + [
        jnp.concatenate([off_tiles[level - 1], diag_tiles[level][:, None]], axis=1)
        for level in range(1, levels)
    ]

    def near_of(x, *others):
        return shift(after(x, *others), 0, near_bit)

    def across_of(x, *others):
        return shift(after(x, *others), TWIN, 0)

    coded = src_part * rows + src_slot
    codes = jnp.stack([coded, shift(coded, TWIN, 0)])
    part, slot = codes // rows, codes % rows
    rel = part ^ node
    unit = ((slot >> 1 >> FAR) ^ (z >> FAR)) & 1
    for i, bit in enumerate(bits + [1]):
        unit = unit + (((rel & bit) != 0).astype(jnp.int32) << (i + 1))
    inner = (((slot >> 1 >> NEAR) ^ (z >> NEAR)) & 1) * 2 + (slot & 1) + ((rel >> 1) & 1) * half
    place = (unit * rows + inner).reshape(-1)

    vec = (rows, columns, size)

    def run(level, down, up, inputs):
        linked = level > 0
        config = dict(
            rows=rows,
            fanout=fanout,
            links=links,
            level=level,
            down=down,
            up=up,
            partners=partners - 1,
            tiles=where[level],
        )
        args = ([place] if linked else []) + list(held[level]) + list(inputs)
        shapes, scratch = [], []
        if not up:
            shapes.append(jax.ShapeDtypeStruct(vec, BF16))
        else:
            shapes += [jax.ShapeDtypeStruct((half, columns, size), F32)] * 2
            if linked:
                part_shape = (blocks // 2,) + vec[1:]
                shapes += [jax.ShapeDtypeStruct(part_shape, t) for t in (F32, BF16)]
                scratch.append(pltpu.VMEM((blocks,) + vec[1:], F32))
        dots = rows * ((fanout if linked else 0) + 1) * (int(down) + int(up))
        return pl.pallas_call(
            functools.partial(level_kernel, config),
            in_specs=([SMEM] if linked else []) + [VMEM] * (len(args) - int(linked)),
            out_specs=[VMEM] * len(shapes),
            out_shape=shapes,
            scratch_shapes=scratch,
            compiler_params=params(),
            cost_estimate=pl.CostEstimate(
                flops=2 * dots * columns * size * size,
                bytes_accessed=dots * size * size * 2,
                transcendentals=0,
            ),
        )(*args)

    def flip(x, d):
        node_bits = sum(bit for i, bit in enumerate(bits) if (d >> (i + 1)) & 1)
        return shift(x, node_bits, far_bit if d & 1 else 0)

    def gather(value, *early):
        met = jnp.concatenate([value] + [flip(value, d) for d in range(1, partners)])
        met = after(met, *early)
        return jnp.concatenate([met, shift(met, 1, 0)])

    def scatter(keep, sent):
        summed = keep + shift(sent, 1, 0).astype(F32)
        pieces = [summed[d * rows : (d + 1) * rows] for d in range(partners)]
        return pieces[:1] + [flip(x.astype(BF16), d) for d, x in enumerate(pieces) if d > 0]

    held, where = {0: first_tiles}, {0: [(i, None) for i in range(4)]}
    near = {1: near_of(pieces[1], first_tiles[1])}
    across = across_of(pieces[1], first_tiles[3])
    stored = []
    inputs = right
    for level in range(levels - 1):
        (value,) = run(level, True, False, inputs)
        stored.append(value)
        early = []
        if level == 0:
            near[2] = near_of(pieces[2], near[1], value)
            held[1] = [pieces[1], near[1], across, across_of(near[1], across)]
            where[1] = [(i, None) for i in range(4)]
            early, late = [near[1], across], [near[2]]
        elif level == 1:
            rest = near_of(jnp.stack(pieces[3:]), near[2], value)
            for i, other in enumerate(range(3, levels)):
                near[other] = rest[i]
            late = [rest]
        else:
            late = []
        gathered = gather(value, *early)
        inputs = right + [after(gathered, *late)]
        later = level + 2
        if later < levels:
            pair = jnp.stack([pieces[later], near[later]])
            held[later] = [pieces[later], near[later], across_of(pair, gathered)]
            where[later] = [(0, None), (1, None), (2, 0), (2, 1)]
    results = [None] * levels
    one, two, *sums = run(levels - 1, True, True, inputs)
    results[levels - 1] = (one, two)
    for level in range(levels - 2, -1, -1):
        one, two, *sums = run(level, False, True, [stored[level]] + scatter(*sums))
        results[level] = (one, two)

    def home(wanted):
        one = jnp.stack([results[x][0] for x in wanted]).astype(BF16)
        two = jnp.stack([results[x][1] for x in wanted]).astype(BF16)
        return turn(one, 0, True), turn(two, 1, True)

    groups = [list(range(levels - 1, 1, -1)), [1, 0]]
    early = []
    for wanted in groups[:-1]:
        early += home(wanted)
    final = home(groups[-1])
    return pl.pallas_call(
        functools.partial(finish_kernel, groups),
        in_specs=[VMEM] * (2 * len(groups)),
        out_specs=VMEM,
        out_shape=jax.ShapeDtypeStruct(right_side.shape, F32),
        compiler_params=params(),
    )(*early, *final)


def solution(mesh):
    placed = (
        P("rhs", None, "node", None),
        P(None, ("node", "rhs"), None, None),
        P(None, ("node", "rhs"), None, None, None),
        P(None, "node", None),
        P(None, "node", None),
    )
    return jax.shard_map(
        on_device,
        mesh=mesh,
        in_specs=placed,
        out_specs=P("rhs", None, "node", None),
        check_vma=False,
    )
```

```python
import functools

import jax
import jax.numpy as jnp
from jax import lax
from jax.experimental import pallas as pl
from jax.experimental.pallas import tpu as pltpu
from jax.sharding import PartitionSpec as P

F32 = jnp.float32
BF16 = jnp.bfloat16
NT = (((1,), (1,)), ((), ()))
NN = (((1,), (0,)), ((), ()))

ORDER = (0, 1, 3, 2)


def dot(a, b, dims):
    return lax.dot_general(a, b, dims, preferred_element_type=F32)


def slot_of(v, z):
    return (ORDER[v // 2] ^ z) * 2 + v % 2


def level_kernel(config, *refs):
    refs = list(refs)
    take = lambda n: [refs.pop(0) for _ in range(n)]
    rows, fanout = config["rows"], config["fanout"]
    level, down, up = config["level"], config["down"], config["up"]
    linked = level > 0
    last = fanout if linked else 0
    z = lax.axis_index("rhs")
    place = take(1)[0] if linked else None
    tiles = take(max(ref for ref, _ in config["tiles"]) + 1)
    tiles = [(tiles[ref], at) for ref, at in config["tiles"]]
    if down:
        mine, other = take(2)
        solved = take(1)[0] if linked else None
    else:
        stored, kept = take(2)
        returned = take(config["partners"])
    out_f = take(1)[0] if not up else None
    if up:
        result_mine, result_other = take(2)
        keep, sent = take(2) if linked else (None, None)
    right = take(1)[0] if down else None
    total = take(1)[0] if up and linked else None

    def tile(v, k):
        ref, at = tiles[v // 2]
        return ref[v % 2, k] if at is None else ref[at, v % 2, k]

    def wide(v):
        return jnp.concatenate([tile(v, k) for k in range(fanout)], axis=1)

    def places(v):
        base = ((level - 1) * rows + slot_of(v, z)) * fanout
        return [place[base + k] for k in range(fanout)]

    if total is not None:
        total[...] = jnp.zeros_like(total)
    if down:
        columns = mine.shape[0]
        for s in range(rows):
            right[s, :columns] = mine[:, level, s, :]
            late = other[:, level - 1, s, :] if linked else other[:, s, :]
            right[s, columns:] = late.astype(F32)
        values = []
        for v in range(rows):
            current = right[slot_of(v, z)]
            if linked:
                picked = jnp.concatenate([solved[at] for at in places(v)], axis=1)
                current = current - dot(picked, wide(v), NT)
            values.append(current.astype(BF16))
        values = [dot(values[v], tile(v, last), NT).astype(BF16) for v in range(rows)]
        if not up:
            for v in range(rows):
                out_f[v] = values[v]
            return
    else:
        values = []
        for v in range(rows):
            incoming = kept[v]
            for block in returned:
                incoming = incoming + block[v].astype(F32)
            values.append((stored[v].astype(F32) - incoming).astype(BF16))
    answers = [dot(values[v], tile(v, last), NN) for v in range(rows)]
    columns = result_mine.shape[1]
    for v in range(rows):
        result_mine[slot_of(v, z)] = answers[v][:columns]
        result_other[slot_of(v, z)] = answers[v][columns:].astype(result_other.dtype)
    if not linked:
        return
    size = answers[0].shape[1]
    for v in range(rows):
        terms = dot(answers[v].astype(BF16), wide(v), NN)
        for k, at in enumerate(places(v)):
            total[at] += terms[:, k * size : (k + 1) * size]
    middle = total.shape[0] // 2
    keep[...] = total[:middle]
    sent[...] = total[middle:].astype(BF16)


def finish_kernel(spans, *refs):
    z = lax.axis_index("rhs")
    inner = (z == 1) | (z == 2)
    refs, out = list(refs[:-1]), refs[-1]
    for span in spans:
        home = refs.pop(0)
        for i, level in enumerate(span):
            mine = refs.pop(0)
            for s in range(mine.shape[0]):
                out[:, level, s, :] = jnp.where(inner, mine[s], home[i, s].astype(F32))


VMEM = pl.BlockSpec(memory_space=pltpu.VMEM)
SMEM = pl.BlockSpec(memory_space=pltpu.SMEM)


def params():
    return pltpu.CompilerParams(vmem_limit_bytes=32 * 1024 * 1024)


def on_device(right_side, diag_tiles, off_tiles, src_part, src_slot):
    columns, levels, rows, size = right_side.shape
    fanout = src_part.shape[2]
    nodes = lax.axis_size("node")
    chips = nodes // 2
    node, z = lax.axis_index("node"), lax.axis_index("rhs")

    def inward(x):
        return lax.ppermute(x, "rhs", [(0, 1), (3, 2)])

    def outward(x):
        return lax.ppermute(x, "rhs", [(1, 0), (2, 3)])

    def between(x):
        return lax.ppermute(x, "rhs", [(1, 2), (2, 1)])

    def shift(x, d):
        return lax.ppermute(x, "node", [(n, n ^ d) for n in range(nodes)])

    def after(x, *others):
        return lax.optimization_barrier((x, *others))[0]

    held, where = {}, {}

    def hold(level, mine, near, at, both):
        held[level] = [mine, near, both]
        where[level] = [(0, None), (1, at), (2, 0), (2, 1)]

    first = diag_tiles[0][:, None]
    first_near = inward(first)
    first_both = between(jnp.stack([first, first_near]))
    hold(0, first, first_near, None, first_both)
    first_right = inward(right_side[:, 0].astype(BF16))
    pieces = [None] + [
        jnp.concatenate([off_tiles[level - 1], diag_tiles[level][:, None]], axis=1)
        for level in range(1, levels)
    ]
    near = {1: inward(after(pieces[1], first_near))}

    rel = src_part ^ node
    pair = (src_slot >> 1) ^ z
    inner = (pair ^ (pair >> 1)) * 2 + (src_slot & 1)
    place = (((rel >> 1) + (rel & 1) * chips) * rows + inner).reshape(-1)

    vec = (rows, 2 * columns, size)
    own = (rows, columns, size)

    def run(level, down, up, inputs):
        linked = level > 0
        config = dict(
            rows=rows,
            fanout=fanout,
            level=level,
            down=down,
            up=up,
            partners=chips - 1,
            tiles=where[level],
        )
        args = ([place] if linked else []) + list(held[level]) + list(inputs)
        shapes, scratch = [], []
        if down:
            scratch.append(pltpu.VMEM(vec, F32))
        if not up:
            shapes.append(jax.ShapeDtypeStruct(vec, BF16))
        else:
            shapes += [jax.ShapeDtypeStruct(own, t) for t in (F32, BF16)]
            if linked:
                shapes += [jax.ShapeDtypeStruct((chips * rows,) + vec[1:], t) for t in (F32, BF16)]
                scratch.append(pltpu.VMEM((nodes * rows,) + vec[1:], F32))
        dots = rows * ((fanout if linked else 0) + 1) * (int(down) + int(up))
        return pl.pallas_call(
            functools.partial(level_kernel, config),
            in_specs=([SMEM] if linked else []) + [VMEM] * (len(args) - int(linked)),
            out_specs=[VMEM] * len(shapes),
            out_shape=shapes,
            scratch_shapes=scratch,
            compiler_params=params(),
            cost_estimate=pl.CostEstimate(
                flops=4 * dots * columns * size * size,
                bytes_accessed=dots * size * size * 2,
                transcendentals=0,
            ),
        )(*args)

    def gather(value, *early):
        met = jnp.concatenate([value] + [shift(value, 2 * d) for d in range(1, chips)])
        met = after(met, *early)
        return jnp.concatenate([met, shift(met, 1)])

    def scatter(keep, sent):
        summed = keep + shift(sent, 1).astype(F32)
        parts = [summed[d * rows : (d + 1) * rows] for d in range(chips)]
        return parts[:1] + [shift(x.astype(BF16), 2 * d) for d, x in enumerate(parts) if d > 0]

    stored = []
    inputs = [right_side, first_right]
    for level in range(levels - 1):
        (value,) = run(level, True, False, inputs)
        stored.append(value)
        early, late = [], []
        if level == 0:
            rest_right = inward(after(right_side[:, 1:], near[1], value))
            near[2] = inward(after(pieces[2], near[1], value))
            hold(1, pieces[1], near[1], None, between(jnp.stack([pieces[1], near[1]])))
            early = [near[1]]
        elif level == 1:
            rest = inward(after(jnp.stack(pieces[3:]), near[2], value))
            late = [rest]
        gathered = gather(value, *early)
        inputs = [right_side, rest_right, after(gathered, *late)]
        later = level + 2
        if later < levels:
            at = None if later == 2 else later - 3
            block = near[2] if at is None else rest
            pair = jnp.stack([pieces[later], block if at is None else block[at]])
            hold(later, pieces[later], block, at, between(after(pair, gathered)))
    mine, others = [None] * levels, [None] * levels
    mine[-1], others[-1], *sums = run(levels - 1, True, True, inputs)
    for level in range(levels - 2, -1, -1):
        outs = run(level, False, True, [stored[level]] + scatter(*sums))
        mine[level], others[level], *sums = outs
    spans = [list(range(levels - 1, 0, -1)), [0]]
    args = []
    for span in spans:
        args += [outward(jnp.stack([others[x] for x in span]))] + [mine[x] for x in span]
    return pl.pallas_call(
        functools.partial(finish_kernel, spans),
        in_specs=[VMEM] * len(args),
        out_specs=VMEM,
        out_shape=jax.ShapeDtypeStruct(right_side.shape, F32),
        compiler_params=params(),
    )(*args)


def solution(mesh):
    placed = (
        P("rhs", None, "node", None),
        P(None, ("node", "rhs"), None, None),
        P(None, ("node", "rhs"), None, None, None),
        P(None, "node", None),
        P(None, "node", None),
    )
    return jax.shard_map(
        on_device,
        mesh=mesh,
        in_specs=placed,
        out_specs=P("rhs", None, "node", None),
        check_vma=False,
    )
```

```python
import functools

import jax
import jax.numpy as jnp
from jax import lax
from jax.experimental import pallas as pl
from jax.experimental.pallas import tpu as pltpu
from jax.sharding import PartitionSpec as P

F32 = jnp.float32
BF16 = jnp.bfloat16
NT = (((1,), (1,)), ((), ()))
NN = (((1,), (0,)), ((), ()))

ORDER = (0, 1, 3, 2)


def dot(a, b, dims):
    return lax.dot_general(a, b, dims, preferred_element_type=F32)


def slot_of(v, z):
    return (ORDER[v // 2] ^ z) * 2 + v % 2


def level_kernel(config, *refs):
    refs = list(refs)
    take = lambda n: [refs.pop(0) for _ in range(n)]
    rows, fanout = config["rows"], config["fanout"]
    level, down, up = config["level"], config["down"], config["up"]
    linked = level > 0
    last = fanout if linked else 0
    z = lax.axis_index("rhs")
    place = take(1)[0] if linked else None
    tiles = take(max(ref for ref, _ in config["tiles"]) + 1)
    tiles = [(tiles[ref], at) for ref, at in config["tiles"]]
    if down:
        mine, other = take(2)
        solved = take(1)[0] if linked else None
    else:
        stored, incoming = take(2)
    out_f = take(1)[0] if not up else None
    if up:
        result_mine, result_other = take(2)
        keep, sent = take(2) if linked else (None, None)
    right = take(1)[0] if down else None
    total = take(1)[0] if up and linked else None

    def tile(v, k):
        ref, at = tiles[v // 2]
        return ref[v % 2, k] if at is None else ref[at, v % 2, k]

    def wide(v):
        return jnp.concatenate([tile(v, k) for k in range(fanout)], axis=1)

    def places(v):
        base = ((level - 1) * rows + slot_of(v, z)) * fanout
        return [place[base + k] for k in range(fanout)]

    if total is not None:
        total[...] = jnp.zeros_like(total)
    if down:
        columns = mine.shape[0]
        for s in range(rows):
            right[s, :columns] = mine[:, level, s, :]
            late = other[:, level - 1, s, :] if linked else other[:, s, :]
            right[s, columns:] = late.astype(F32)
        values = []
        for v in range(rows):
            current = right[slot_of(v, z)]
            if linked:
                picked = jnp.concatenate([solved[at] for at in places(v)], axis=1)
                current = current - dot(picked, wide(v), NT)
            values.append(current.astype(BF16))
        values = [dot(values[v], tile(v, last), NT).astype(BF16) for v in range(rows)]
        if not up:
            for v in range(rows):
                out_f[v] = values[v]
            return
    else:
        values = []
        for v in range(rows):
            values.append((stored[v].astype(F32) - incoming[v]).astype(BF16))
    answers = [dot(values[v], tile(v, last), NN) for v in range(rows)]
    columns = result_mine.shape[1]
    for v in range(rows):
        result_mine[slot_of(v, z)] = answers[v][:columns]
        result_other[slot_of(v, z)] = answers[v][columns:].astype(result_other.dtype)
    if not linked:
        return
    size = answers[0].shape[1]
    for v in range(rows):
        terms = dot(answers[v].astype(BF16), wide(v), NN)
        for k, at in enumerate(places(v)):
            total[at] += terms[:, k * size : (k + 1) * size]
    middle = total.shape[0] // 2
    keep[...] = total[:middle]
    sent[...] = total[middle:].astype(BF16)


def finish_kernel(spans, *refs):
    z = lax.axis_index("rhs")
    inner = (z == 1) | (z == 2)
    refs, out = list(refs[:-1]), refs[-1]
    for span in spans:
        home = refs.pop(0)
        for i, level in enumerate(span):
            mine = refs.pop(0)
            for s in range(mine.shape[0]):
                out[:, level, s, :] = jnp.where(inner, mine[s], home[i, s].astype(F32))


VMEM = pl.BlockSpec(memory_space=pltpu.VMEM)
SMEM = pl.BlockSpec(memory_space=pltpu.SMEM)


def params():
    return pltpu.CompilerParams(vmem_limit_bytes=32 * 1024 * 1024)


def on_device(right_side, diag_tiles, off_tiles, src_part, src_slot):
    columns, levels, rows, size = right_side.shape
    fanout = src_part.shape[2]
    nodes = lax.axis_size("node")
    chips = nodes // 2
    node, z = lax.axis_index("node"), lax.axis_index("rhs")

    def inward(x):
        return lax.ppermute(x, "rhs", [(0, 1), (3, 2)])

    def outward(x):
        return lax.ppermute(x, "rhs", [(1, 0), (2, 3)])

    def between(x):
        return lax.ppermute(x, "rhs", [(1, 2), (2, 1)])

    def shift(x, d):
        return lax.ppermute(x, "node", [(n, n ^ d) for n in range(nodes)])

    def after(x, *others):
        return lax.optimization_barrier((x, *others))[0]

    held, where = {}, {}

    def hold(level, arrays, places):
        held[level], where[level] = arrays, places

    apart = [(i, None) for i in range(4)]
    pieces = [diag_tiles[0][:, None]] + [
        jnp.concatenate([off_tiles[level - 1], diag_tiles[level][:, None]], axis=1)
        for level in range(1, levels)
    ]
    near = {0: inward(pieces[0]), 1: inward(pieces[1])}
    facing = {0: between(pieces[0]), 1: between(pieces[1])}
    corner = {0: between(near[0])}
    near[2] = inward(after(pieces[2], corner[0]))
    facing[2] = between(after(pieces[2], corner[0]))
    for level in (1, 2):
        corner[level] = between(near[level])
    for level in range(3):
        hold(level, [pieces[level], near[level], facing[level], corner[level]], apart)
    first_right = inward(right_side[:, 0].astype(BF16))
    rest_right = inward(after(right_side[:, 1:], near[1]))

    rel = src_part ^ node
    pair = (src_slot >> 1) ^ z
    inner = (pair ^ (pair >> 1)) * 2 + (src_slot & 1)
    place = (((rel >> 1) + (rel & 1) * chips) * rows + inner).reshape(-1)

    vec = (rows, 2 * columns, size)
    own = (rows, columns, size)

    def run(level, down, up, inputs):
        linked = level > 0
        config = dict(
            rows=rows,
            fanout=fanout,
            level=level,
            down=down,
            up=up,
            tiles=where[level],
        )
        args = ([place] if linked else []) + list(held[level]) + list(inputs)
        shapes, scratch = [], []
        if down:
            scratch.append(pltpu.VMEM(vec, F32))
        if not up:
            shapes.append(jax.ShapeDtypeStruct(vec, BF16))
        else:
            shapes += [jax.ShapeDtypeStruct(own, t) for t in (F32, BF16)]
            if linked:
                shapes += [jax.ShapeDtypeStruct((chips * rows,) + vec[1:], t) for t in (F32, BF16)]
                scratch.append(pltpu.VMEM((nodes * rows,) + vec[1:], F32))
        dots = rows * ((fanout if linked else 0) + 1) * (int(down) + int(up))
        return pl.pallas_call(
            functools.partial(level_kernel, config),
            in_specs=([SMEM] if linked else []) + [VMEM] * (len(args) - int(linked)),
            out_specs=[VMEM] * len(shapes),
            out_shape=shapes,
            scratch_shapes=scratch,
            compiler_params=params(),
            cost_estimate=pl.CostEstimate(
                flops=4 * dots * columns * size * size,
                bytes_accessed=dots * size * size * 2,
                transcendentals=0,
            ),
        )(*args)

    def gather(value, *early):
        met = jnp.concatenate([value] + [shift(value, 2 * d) for d in range(1, chips)])
        met = after(met, *early)
        return jnp.concatenate([met, shift(met, 1)])

    def scatter(keep, sent):
        summed = keep + shift(sent, 1).astype(F32)
        parts = [summed[d * rows : (d + 1) * rows] for d in range(chips)]
        incoming = parts[0]
        for d in range(chips - 1, 0, -1):
            incoming = incoming + shift(parts[d].astype(BF16), 2 * d).astype(F32)
        return incoming

    stored = []
    inputs = [right_side, first_right]
    deadlines = {0: [near[2], facing[1], facing[2]], 1: [corner[2]]}
    for level in range(levels - 1):
        (value,) = run(level, True, False, inputs)
        stored.append(value)
        later = level + 3
        if later < levels:
            near[later] = inward(after(pieces[later], near[later - 1], value))
        gathered = gather(value, *deadlines.get(level, []))
        inputs = [right_side, rest_right, gathered]
        later = level + 2
        if 3 <= later < levels:
            pair = jnp.stack([pieces[later], near[later]])
            both = between(after(pair, value))
            hold(later, [pieces[later], near[later], both], [(0, None), (1, None), (2, 0), (2, 1)])
    mine, others = [None] * levels, [None] * levels
    mine[-1], others[-1], *sums = run(levels - 1, True, True, inputs)
    for level in range(levels - 2, -1, -1):
        outs = run(level, False, True, [stored[level], scatter(*sums)])
        mine[level], others[level], *sums = outs
    spans = [list(range(levels - 1, 0, -1)), [0]]
    args = []
    for span in spans:
        args += [outward(jnp.stack([others[x] for x in span]))] + [mine[x] for x in span]
    return pl.pallas_call(
        functools.partial(finish_kernel, spans),
        in_specs=[VMEM] * len(args),
        out_specs=VMEM,
        out_shape=jax.ShapeDtypeStruct(right_side.shape, F32),
        compiler_params=params(),
    )(*args)


def solution(mesh):
    placed = (
        P("rhs", None, "node", None),
        P(None, ("node", "rhs"), None, None),
        P(None, ("node", "rhs"), None, None, None),
        P(None, "node", None),
        P(None, "node", None),
    )
    return jax.shard_map(
        on_device,
        mesh=mesh,
        in_specs=placed,
        out_specs=P("rhs", None, "node", None),
        check_vma=False,
    )
```

```python
import functools

import jax
import jax.numpy as jnp
from jax import lax
from jax.experimental import pallas as pl
from jax.experimental.pallas import tpu as pltpu
from jax.sharding import PartitionSpec as P

F32 = jnp.float32
BF16 = jnp.bfloat16
NT = (((1,), (1,)), ((), ()))
NN = (((1,), (0,)), ((), ()))

ORDER = (0, 1, 3, 2)


def dot(a, b, dims):
    return lax.dot_general(a, b, dims, preferred_element_type=F32)


def slot_of(v, z):
    return (ORDER[v // 2] ^ z) * 2 + v % 2


def level_kernel(config, *refs):
    refs = list(refs)
    take = lambda n: [refs.pop(0) for _ in range(n)]
    rows, fanout = config["rows"], config["fanout"]
    level, down, up = config["level"], config["down"], config["up"]
    linked = level > 0
    last = fanout if linked else 0
    z = lax.axis_index("rhs")
    place = take(1)[0] if linked else None
    tiles = take(max(ref for ref, _ in config["tiles"]) + 1)
    tiles = [(tiles[ref], at) for ref, at in config["tiles"]]
    if down:
        mine, other = take(2)
        solved = take(1)[0] if linked else None
    else:
        stored, incoming = take(2)
    out_f = take(1)[0] if not up else None
    if up:
        result_mine, result_other = take(2)
        keep, sent = take(2) if linked else (None, None)
    right = take(1)[0] if down else None
    total = take(1)[0] if up and linked else None

    def tile(v, k):
        ref, at = tiles[v // 2]
        return ref[v % 2, k] if at is None else ref[at, v % 2, k]

    def wide(v):
        return jnp.concatenate([tile(v, k) for k in range(fanout)], axis=1)

    def places(v):
        base = ((level - 1) * rows + slot_of(v, z)) * fanout
        return [place[base + k] for k in range(fanout)]

    if total is not None:
        total[...] = jnp.zeros_like(total)
    if down:
        columns = mine.shape[0]
        for s in range(rows):
            right[s, :columns] = mine[:, level, s, :]
            late = other[:, level - 1, s, :] if linked else other[:, s, :]
            right[s, columns:] = late.astype(F32)
        values = []
        for v in range(rows):
            current = right[slot_of(v, z)]
            if linked:
                picked = jnp.concatenate([solved[at] for at in places(v)], axis=1)
                current = current - dot(picked, wide(v), NT)
            values.append(current.astype(BF16))
        values = [dot(values[v], tile(v, last), NT).astype(BF16) for v in range(rows)]
        if not up:
            for v in range(rows):
                out_f[v] = values[v]
            return
    else:
        values = []
        for v in range(rows):
            values.append((stored[v].astype(F32) - incoming[v]).astype(BF16))
    answers = [dot(values[v], tile(v, last), NN) for v in range(rows)]
    columns = result_mine.shape[1]
    for v in range(rows):
        result_mine[slot_of(v, z)] = answers[v][:columns]
        result_other[slot_of(v, z)] = answers[v][columns:].astype(result_other.dtype)
    if not linked:
        return
    size = answers[0].shape[1]
    for v in range(rows):
        terms = dot(answers[v].astype(BF16), wide(v), NN)
        for k, at in enumerate(places(v)):
            total[at] += terms[:, k * size : (k + 1) * size]
    middle = total.shape[0] // 2
    keep[...] = total[:middle]
    sent[...] = total[middle:].astype(BF16)


def finish_kernel(spans, *refs):
    z = lax.axis_index("rhs")
    inner = (z == 1) | (z == 2)
    refs, out = list(refs[:-1]), refs[-1]
    for span in spans:
        home = refs.pop(0)
        for i, level in enumerate(span):
            mine = refs.pop(0)
            for s in range(mine.shape[0]):
                out[:, level, s, :] = jnp.where(inner, mine[s], home[i, s].astype(F32))


VMEM = pl.BlockSpec(memory_space=pltpu.VMEM)
SMEM = pl.BlockSpec(memory_space=pltpu.SMEM)


def params():
    return pltpu.CompilerParams(vmem_limit_bytes=32 * 1024 * 1024)


def on_device(right_side, diag_tiles, off_tiles, src_part, src_slot):
    columns, levels, rows, size = right_side.shape
    fanout = src_part.shape[2]
    nodes = lax.axis_size("node")
    chips = nodes // 2
    node, z = lax.axis_index("node"), lax.axis_index("rhs")

    def inward(x):
        return lax.ppermute(x, "rhs", [(0, 1), (3, 2)])

    def outward(x):
        return lax.ppermute(x, "rhs", [(1, 0), (2, 3)])

    def between(x):
        return lax.ppermute(x, "rhs", [(1, 2), (2, 1)])

    def shift(x, d):
        return lax.ppermute(x, "node", [(n, n ^ d) for n in range(nodes)])

    def after(x, *others):
        return lax.optimization_barrier((x, *others))[0]

    held, where = {}, {}

    def hold(level, arrays, places):
        held[level], where[level] = arrays, places

    apart = [(i, None) for i in range(4)]
    pieces = [diag_tiles[0][:, None]] + [
        jnp.concatenate([off_tiles[level - 1], diag_tiles[level][:, None]], axis=1)
        for level in range(1, levels)
    ]
    near, facing, corner = {0: inward(pieces[0])}, {0: between(pieces[0])}, {}

    def join(level):
        corner[level] = between(near[level])
        hold(level, [pieces[level], near[level], facing[level], corner[level]], apart)

    join(0)
    near[1] = inward(after(pieces[1], near[0]))
    facing[1] = between(after(pieces[1], corner[0]))
    join(1)
    first_right = inward(right_side[:, 0].astype(BF16))

    rel = src_part ^ node
    pair = (src_slot >> 1) ^ z
    inner = (pair ^ (pair >> 1)) * 2 + (src_slot & 1)
    place = (((rel >> 1) + (rel & 1) * chips) * rows + inner).reshape(-1)

    vec = (rows, 2 * columns, size)
    own = (rows, columns, size)

    def run(level, down, up, inputs):
        linked = level > 0
        config = dict(
            rows=rows,
            fanout=fanout,
            level=level,
            down=down,
            up=up,
            tiles=where[level],
        )
        args = ([place] if linked else []) + list(held[level]) + list(inputs)
        shapes, scratch = [], []
        if down:
            scratch.append(pltpu.VMEM(vec, F32))
        if not up:
            shapes.append(jax.ShapeDtypeStruct(vec, BF16))
        else:
            shapes += [jax.ShapeDtypeStruct(own, t) for t in (F32, BF16)]
            if linked:
                shapes += [jax.ShapeDtypeStruct((chips * rows,) + vec[1:], t) for t in (F32, BF16)]
                scratch.append(pltpu.VMEM((nodes * rows,) + vec[1:], F32))
        dots = rows * ((fanout if linked else 0) + 1) * (int(down) + int(up))
        return pl.pallas_call(
            functools.partial(level_kernel, config),
            in_specs=([SMEM] if linked else []) + [VMEM] * (len(args) - int(linked)),
            out_specs=[VMEM] * len(shapes),
            out_shape=shapes,
            scratch_shapes=scratch,
            compiler_params=params(),
            cost_estimate=pl.CostEstimate(
                flops=4 * dots * columns * size * size,
                bytes_accessed=dots * size * size * 2,
                transcendentals=0,
            ),
        )(*args)

    def gather(value, *early):
        met = jnp.concatenate([value] + [shift(value, 2 * d) for d in range(1, chips)])
        met = after(met, *early)
        return met, jnp.concatenate([met, shift(met, 1)])

    def scatter(keep, sent):
        summed = keep + shift(sent, 1).astype(F32)
        parts = [summed[d * rows : (d + 1) * rows] for d in range(chips)]
        incoming = parts[0]
        for d in range(chips - 1, 0, -1):
            incoming = incoming + shift(parts[d].astype(BF16), 2 * d).astype(F32)
        return incoming

    stored = []
    inputs = [right_side, after(first_right, place)]
    for level in range(levels - 1):
        (value,) = run(level, True, False, inputs)
        stored.append(value)
        early = []
        if level == 0:
            near[2] = inward(after(pieces[2], near[1], value))
            rest_right = inward(after(right_side[:, 1:], near[1], value))
            early = [near[1], facing[1]]
        elif level == 1:
            early = [facing[2], corner[2]]
        later = level + 3
        if later < levels:
            near[later] = inward(after(pieces[later], near[later - 1], value))
        met, gathered = gather(value, *early)
        if level == 0:
            facing[2] = between(after(pieces[2], met))
            join(2)
        inputs = [right_side, rest_right, gathered]
        later = level + 2
        if 3 <= later < levels:
            pair = jnp.stack([pieces[later], near[later]])
            both = between(after(pair, value))
            hold(later, [pieces[later], near[later], both], [(0, None), (1, None), (2, 0), (2, 1)])
    mine, others = [None] * levels, [None] * levels
    mine[-1], others[-1], *sums = run(levels - 1, True, True, inputs)
    for level in range(levels - 2, -1, -1):
        outs = run(level, False, True, [stored[level], scatter(*sums)])
        mine[level], others[level], *sums = outs
    spans = [list(range(levels - 1, 0, -1)), [0]]
    args = []
    for span in spans:
        args += [outward(jnp.stack([others[x] for x in span]))] + [mine[x] for x in span]
    return pl.pallas_call(
        functools.partial(finish_kernel, spans),
        in_specs=[VMEM] * len(args),
        out_specs=VMEM,
        out_shape=jax.ShapeDtypeStruct(right_side.shape, F32),
        compiler_params=params(),
    )(*args)


def solution(mesh):
    placed = (
        P("rhs", None, "node", None),
        P(None, ("node", "rhs"), None, None),
        P(None, ("node", "rhs"), None, None, None),
        P(None, "node", None),
        P(None, "node", None),
    )
    return jax.shard_map(
        on_device,
        mesh=mesh,
        in_specs=placed,
        out_specs=P("rhs", None, "node", None),
        check_vma=False,
    )
```

```python
import functools

import jax
import jax.numpy as jnp
from jax import lax
from jax.experimental import pallas as pl
from jax.experimental.pallas import tpu as pltpu
from jax.sharding import PartitionSpec as P

F32 = jnp.float32
BF16 = jnp.bfloat16
NT = (((1,), (1,)), ((), ()))
NN = (((1,), (0,)), ((), ()))

ORDER = (0, 1, 3, 2)


def dot(a, b, dims):
    return lax.dot_general(a, b, dims, preferred_element_type=F32)


def slot_of(v, z):
    return (ORDER[v // 2] ^ z) * 2 + v % 2


def level_kernel(config, *refs):
    refs = list(refs)
    take = lambda n: [refs.pop(0) for _ in range(n)]
    rows, fanout = config["rows"], config["fanout"]
    level, down, up = config["level"], config["down"], config["up"]
    linked = level > 0
    last = fanout if linked else 0
    z = lax.axis_index("rhs")
    place = take(1)[0] if linked else None
    tiles = take(max(ref for ref, _ in config["tiles"]) + 1)
    tiles = [(tiles[ref], at) for ref, at in config["tiles"]]
    if down:
        mine, other = take(2)
        solved = take(1)[0] if linked else None
    else:
        stored, incoming = take(2)
    out_f = take(1)[0] if not up else None
    if up:
        result_mine, result_other = take(2)
        keep, sent = take(2) if linked else (None, None)
    right = take(1)[0] if down else None
    total = take(1)[0] if up and linked else None

    def tile(v, k):
        ref, at = tiles[v // 2]
        return ref[v % 2, k] if at is None else ref[at, v % 2, k]

    def wide(v):
        return jnp.concatenate([tile(v, k) for k in range(fanout)], axis=1)

    def places(v):
        base = ((level - 1) * rows + slot_of(v, z)) * fanout
        return [place[base + k] for k in range(fanout)]

    if total is not None:
        total[...] = jnp.zeros_like(total)
    if down:
        columns = mine.shape[0]
        for s in range(rows):
            right[s, :columns] = mine[:, level, s, :]
            right[s, columns:] = other[:, level, s, :]
        values = []
        for v in range(rows):
            current = right[slot_of(v, z)]
            if linked:
                picked = jnp.concatenate([solved[at] for at in places(v)], axis=1)
                current = current - dot(picked, wide(v), NT)
            values.append(current.astype(BF16))
        values = [dot(values[v], tile(v, last), NT).astype(BF16) for v in range(rows)]
        if not up:
            for v in range(rows):
                out_f[v] = values[v]
            return
    else:
        values = []
        for v in range(rows):
            values.append((stored[v].astype(F32) - incoming[v]).astype(BF16))
    answers = [dot(values[v], tile(v, last), NN) for v in range(rows)]
    columns = result_mine.shape[1]
    for v in range(rows):
        result_mine[slot_of(v, z)] = answers[v][:columns]
        result_other[slot_of(v, z)] = answers[v][columns:].astype(result_other.dtype)
    if not linked:
        return
    size = answers[0].shape[1]
    for v in range(rows):
        terms = dot(answers[v].astype(BF16), wide(v), NN)
        for k, at in enumerate(places(v)):
            total[at] += terms[:, k * size : (k + 1) * size]
    middle = total.shape[0] // 2
    keep[...] = total[:middle]
    sent[...] = total[middle:].astype(BF16)


def finish_kernel(spans, *refs):
    z = lax.axis_index("rhs")
    inner = (z == 1) | (z == 2)
    refs, out = list(refs[:-1]), refs[-1]
    for span in spans:
        home = refs.pop(0)
        for i, level in enumerate(span):
            mine = refs.pop(0)
            for s in range(mine.shape[0]):
                out[:, level, s, :] = jnp.where(inner, mine[s], home[i, s].astype(F32))


VMEM = pl.BlockSpec(memory_space=pltpu.VMEM)
SMEM = pl.BlockSpec(memory_space=pltpu.SMEM)


def params():
    return pltpu.CompilerParams(vmem_limit_bytes=32 * 1024 * 1024)


def on_device(right_side, diag_tiles, off_tiles, src_part, src_slot):
    columns, levels, rows, size = right_side.shape
    fanout = src_part.shape[2]
    nodes = lax.axis_size("node")
    chips = nodes // 2
    node, z = lax.axis_index("node"), lax.axis_index("rhs")

    def inward(x):
        return lax.ppermute(x, "rhs", [(0, 1), (3, 2)])

    def outward(x):
        return lax.ppermute(x, "rhs", [(1, 0), (2, 3)])

    def between(x):
        return lax.ppermute(x, "rhs", [(1, 2), (2, 1)])

    def shift(x, d):
        return lax.ppermute(x, "node", [(n, n ^ d) for n in range(nodes)])

    def after(x, *others):
        return lax.optimization_barrier((x, *others))[0]

    held, where = {}, {}

    def hold(level, arrays, places):
        held[level], where[level] = arrays, places

    pieces = [diag_tiles[0][:, None]] + [
        jnp.concatenate([off_tiles[level - 1], diag_tiles[level][:, None]], axis=1)
        for level in range(1, levels)
    ]
    near, both = {}, {}

    def join(level, *others):
        block, at = near[level]
        pair = jnp.stack([pieces[level], block if at is None else block[at]])
        both[level] = between(after(pair, *others))
        places = [(0, None), (1, at), (2, 0), (2, 1)]
        hold(level, [pieces[level], block, both[level]], places)

    near[0] = inward(pieces[0]), None
    other_right = inward(right_side)
    join(0)
    lower = inward(after(jnp.stack(pieces[1:3]), other_right))
    near[1], near[2] = (lower, 0), (lower, 1)
    facing = between(after(pieces[1], both[0]))
    corner = between(lower[0])
    hold(1, [pieces[1], lower, facing, corner], [(0, None), (1, 0), (2, None), (3, None)])

    rel = src_part ^ node
    pair = (src_slot >> 1) ^ z
    inner = (pair ^ (pair >> 1)) * 2 + (src_slot & 1)
    place = (((rel >> 1) + (rel & 1) * chips) * rows + inner).reshape(-1)

    vec = (rows, 2 * columns, size)
    own = (rows, columns, size)

    def run(level, down, up, inputs):
        linked = level > 0
        config = dict(
            rows=rows,
            fanout=fanout,
            level=level,
            down=down,
            up=up,
            tiles=where[level],
        )
        args = ([place] if linked else []) + list(held[level]) + list(inputs)
        shapes, scratch = [], []
        if down:
            scratch.append(pltpu.VMEM(vec, F32))
        if not up:
            shapes.append(jax.ShapeDtypeStruct(vec, BF16))
        else:
            shapes += [jax.ShapeDtypeStruct(own, t) for t in (F32, BF16)]
            if linked:
                shapes += [jax.ShapeDtypeStruct((chips * rows,) + vec[1:], t) for t in (F32, BF16)]
                scratch.append(pltpu.VMEM((nodes * rows,) + vec[1:], F32))
        dots = rows * ((fanout if linked else 0) + 1) * (int(down) + int(up))
        return pl.pallas_call(
            functools.partial(level_kernel, config),
            in_specs=([SMEM] if linked else []) + [VMEM] * (len(args) - int(linked)),
            out_specs=[VMEM] * len(shapes),
            out_shape=shapes,
            scratch_shapes=scratch,
            compiler_params=params(),
            cost_estimate=pl.CostEstimate(
                flops=4 * dots * columns * size * size,
                bytes_accessed=dots * size * size * 2,
                transcendentals=0,
            ),
        )(*args)

    def gather(value, *early):
        met = jnp.concatenate([value] + [shift(value, 2 * d) for d in range(1, chips)])
        core = after(met, *early)
        return jnp.concatenate([core, shift(core, 1)])

    def scatter(keep, sent):
        summed = keep + shift(sent, 1).astype(F32)
        parts = [summed[d * rows : (d + 1) * rows] for d in range(chips)]
        incoming = parts[0]
        for d in range(chips - 1, 0, -1):
            incoming = incoming + shift(parts[d].astype(BF16), 2 * d).astype(F32)
        return incoming

    stored = []
    inputs = [right_side, after(other_right, place)]
    for level in range(levels - 1):
        (value,) = run(level, True, False, inputs)
        stored.append(value)
        if level == 0:
            rest = inward(after(jnp.stack(pieces[3:]), lower, value))
            for i in range(3, levels):
                near[i] = rest, i - 3
        gathered = gather(value, *([both[level + 1]] if level > 0 else [facing]))
        if level + 2 < levels:
            join(level + 2, value)
        inputs = [right_side, other_right, gathered]
    mine, others = [None] * levels, [None] * levels
    mine[-1], others[-1], *sums = run(levels - 1, True, True, inputs)
    for level in range(levels - 2, -1, -1):
        outs = run(level, False, True, [stored[level], scatter(*sums)])
        mine[level], others[level], *sums = outs
    spans = [list(range(levels - 1, 0, -1)), [0]]
    args = []
    for span in spans:
        args += [outward(jnp.stack([others[x] for x in span]))] + [mine[x] for x in span]
    return pl.pallas_call(
        functools.partial(finish_kernel, spans),
        in_specs=[VMEM] * len(args),
        out_specs=VMEM,
        out_shape=jax.ShapeDtypeStruct(right_side.shape, F32),
        compiler_params=params(),
    )(*args)


def solution(mesh):
    placed = (
        P("rhs", None, "node", None),
        P(None, ("node", "rhs"), None, None),
        P(None, ("node", "rhs"), None, None, None),
        P(None, "node", None),
        P(None, "node", None),
    )
    return jax.shard_map(
        on_device,
        mesh=mesh,
        in_specs=placed,
        out_specs=P("rhs", None, "node", None),
        check_vma=False,
    )
```

```python
import functools

import jax
import jax.numpy as jnp
from jax import lax
from jax.experimental import pallas as pl
from jax.experimental.pallas import tpu as pltpu
from jax.sharding import PartitionSpec as P

F32 = jnp.float32
BF16 = jnp.bfloat16
NT = (((1,), (1,)), ((), ()))
NN = (((1,), (0,)), ((), ()))

ORDER = (0, 1, 3, 2)


def dot(a, b, dims):
    return lax.dot_general(a, b, dims, preferred_element_type=F32)


def slot_of(v, z):
    return (ORDER[v // 2] ^ z) * 2 + v % 2


def level_kernel(config, *refs):
    refs = list(refs)
    take = lambda n: [refs.pop(0) for _ in range(n)]
    rows, fanout = config["rows"], config["fanout"]
    level, down, up = config["level"], config["down"], config["up"]
    linked = level > 0
    last = fanout if linked else 0
    z = lax.axis_index("rhs")
    place = take(1)[0] if linked else None
    tiles = take(max(spec[0] for spec in config["tiles"]) + 1)
    tiles = [(tiles[ref], at, skip) for ref, at, skip in config["tiles"]]
    if down:
        mine, other = take(2)
        solved = take(1)[0] if linked else None
    else:
        stored, incoming = take(2)
    out_f = take(1)[0] if not up else None
    if up:
        result_mine, result_other = take(2)
        keep, sent = take(2) if linked else (None, None)
    right = take(1)[0] if down else None
    total = take(1)[0] if up and linked else None

    def tile(v, k):
        ref, at, skip = tiles[v // 2]
        return ref[v % 2, skip + k] if at is None else ref[at, v % 2, skip + k]

    def wide(v):
        return jnp.concatenate([tile(v, k) for k in range(fanout)], axis=1)

    def places(v):
        base = ((level - 1) * rows + slot_of(v, z)) * fanout
        return [place[base + k] for k in range(fanout)]

    if total is not None:
        total[...] = jnp.zeros_like(total)
    if down:
        columns = mine.shape[0]
        for s in range(rows):
            right[s, :columns] = mine[:, level, s, :]
            right[s, columns:] = other[:, level, s, :]
        values = []
        for v in range(rows):
            current = right[slot_of(v, z)]
            if linked:
                picked = jnp.concatenate([solved[at] for at in places(v)], axis=1)
                current = current - dot(picked, wide(v), NT)
            values.append(current.astype(BF16))
        values = [dot(values[v], tile(v, last), NT).astype(BF16) for v in range(rows)]
        if not up:
            for v in range(rows):
                out_f[v] = values[v]
            return
    else:
        values = []
        for v in range(rows):
            values.append((stored[v].astype(F32) - incoming[v]).astype(BF16))
    answers = [dot(values[v], tile(v, last), NN) for v in range(rows)]
    columns = result_mine.shape[1]
    for v in range(rows):
        result_mine[slot_of(v, z)] = answers[v][:columns]
        result_other[slot_of(v, z)] = answers[v][columns:].astype(result_other.dtype)
    if not linked:
        return
    size = answers[0].shape[1]
    for v in range(rows):
        terms = dot(answers[v].astype(BF16), wide(v), NN)
        for k, at in enumerate(places(v)):
            total[at] += terms[:, k * size : (k + 1) * size]
    middle = total.shape[0] // 2
    keep[...] = total[:middle]
    sent[...] = total[middle:].astype(BF16)


def finish_kernel(spans, *refs):
    z = lax.axis_index("rhs")
    inner = (z == 1) | (z == 2)
    refs, out = list(refs[:-1]), refs[-1]
    for span in spans:
        home = refs.pop(0)
        for i, level in enumerate(span):
            mine = refs.pop(0)
            for s in range(mine.shape[0]):
                out[:, level, s, :] = jnp.where(inner, mine[s], home[i, s].astype(F32))


VMEM = pl.BlockSpec(memory_space=pltpu.VMEM)
SMEM = pl.BlockSpec(memory_space=pltpu.SMEM)


def params():
    return pltpu.CompilerParams(vmem_limit_bytes=32 * 1024 * 1024)


def on_device(right_side, diag_tiles, off_tiles, src_part, src_slot):
    columns, levels, rows, size = right_side.shape
    fanout = src_part.shape[2]
    nodes = lax.axis_size("node")
    chips = nodes // 2
    node, z = lax.axis_index("node"), lax.axis_index("rhs")

    def inward(x):
        return lax.ppermute(x, "rhs", [(0, 1), (3, 2)])

    def outward(x):
        return lax.ppermute(x, "rhs", [(1, 0), (2, 3)])

    def between(x):
        return lax.ppermute(x, "rhs", [(1, 2), (2, 1)])

    def shift(x, d):
        return lax.ppermute(x, "node", [(n, n ^ d) for n in range(nodes)])

    def after(x, *others):
        return lax.optimization_barrier((x, *others))[0]

    held, where = {}, {}

    def hold(level, arrays, places):
        held[level], where[level] = arrays, places

    pieces = [diag_tiles[0][:, None]] + [
        jnp.concatenate([off_tiles[level - 1], diag_tiles[level][:, None]], axis=1)
        for level in range(1, levels)
    ]
    rel = src_part ^ node
    pair = (src_slot >> 1) ^ z
    inner = (pair ^ (pair >> 1)) * 2 + (src_slot & 1)
    place = (((rel >> 1) + (rel & 1) * chips) * rows + inner).reshape(-1)

    near, both = {}, {}

    def join(level, *others):
        block, at = near[level]
        pair = jnp.stack([pieces[level], block if at is None else block[at]])
        both[level] = between(after(pair, *others))
        places = [(0, None, 0), (1, at, 0), (2, 0, 0), (2, 1, 0)]
        hold(level, [pieces[level], block, both[level]], places)

    facing = between(jnp.concatenate(pieces[:2], axis=1))
    other_right = inward(right_side)
    near[0] = inward(pieces[0]), None
    near[1] = inward(after(pieces[1], other_right, near[0][0])), None

    def meet(level, *others):
        block = near[level][0]
        corner = between(after(block, *others))
        places = [(0, None, 0), (1, None, 0), (2, None, level), (3, None, 0)]
        hold(level, [pieces[level], block, facing, corner], places)
        return corner

    meet(0, place, facing)

    vec = (rows, 2 * columns, size)
    own = (rows, columns, size)

    def run(level, down, up, inputs):
        linked = level > 0
        config = dict(
            rows=rows,
            fanout=fanout,
            level=level,
            down=down,
            up=up,
            tiles=where[level],
        )
        args = ([place] if linked else []) + list(held[level]) + list(inputs)
        shapes, scratch = [], []
        if down:
            scratch.append(pltpu.VMEM(vec, F32))
        if not up:
            shapes.append(jax.ShapeDtypeStruct(vec, BF16))
        else:
            shapes += [jax.ShapeDtypeStruct(own, t) for t in (F32, BF16)]
            if linked:
                shapes += [jax.ShapeDtypeStruct((chips * rows,) + vec[1:], t) for t in (F32, BF16)]
                scratch.append(pltpu.VMEM((nodes * rows,) + vec[1:], F32))
        dots = rows * ((fanout if linked else 0) + 1) * (int(down) + int(up))
        return pl.pallas_call(
            functools.partial(level_kernel, config),
            in_specs=([SMEM] if linked else []) + [VMEM] * (len(args) - int(linked)),
            out_specs=[VMEM] * len(shapes),
            out_shape=shapes,
            scratch_shapes=scratch,
            compiler_params=params(),
            cost_estimate=pl.CostEstimate(
                flops=4 * dots * columns * size * size,
                bytes_accessed=dots * size * size * 2,
                transcendentals=0,
            ),
        )(*args)

    def gather(value, *early):
        met = jnp.concatenate([value] + [shift(value, 2 * d) for d in range(1, chips)])
        core = after(met, *early)
        return jnp.concatenate([core, shift(core, 1)])

    def scatter(keep, sent):
        summed = keep + shift(sent, 1).astype(F32)
        parts = [summed[d * rows : (d + 1) * rows] for d in range(chips)]
        incoming = parts[0]
        for d in range(chips - 1, 0, -1):
            incoming = incoming + shift(parts[d].astype(BF16), 2 * d).astype(F32)
        return incoming

    stored = []
    inputs = [right_side, other_right]
    for level in range(levels - 1):
        (value,) = run(level, True, False, inputs)
        stored.append(value)
        if level == 0:
            near[2] = inward(after(pieces[2], value)), None
        gathered = gather(value, *([both[level + 1]] if level > 0 else [meet(1, value), near[2][0]]))
        if level == 0:
            rest = inward(after(jnp.stack(pieces[3:]), near[2][0], gathered))
            for i in range(3, levels):
                near[i] = rest, i - 3
        if level + 2 < levels:
            join(level + 2, value if level > 0 else gathered)
        inputs = [right_side, other_right, gathered]
    mine, others = [None] * levels, [None] * levels
    mine[-1], others[-1], *sums = run(levels - 1, True, True, inputs)
    for level in range(levels - 2, -1, -1):
        outs = run(level, False, True, [stored[level], scatter(*sums)])
        mine[level], others[level], *sums = outs
    spans = [list(range(levels - 1, 0, -1)), [0]]
    args = []
    for span in spans:
        args += [outward(jnp.stack([others[x] for x in span]))] + [mine[x] for x in span]
    return pl.pallas_call(
        functools.partial(finish_kernel, spans),
        in_specs=[VMEM] * len(args),
        out_specs=VMEM,
        out_shape=jax.ShapeDtypeStruct(right_side.shape, F32),
        compiler_params=params(),
    )(*args)


def solution(mesh):
    placed = (
        P("rhs", None, "node", None),
        P(None, ("node", "rhs"), None, None),
        P(None, ("node", "rhs"), None, None, None),
        P(None, "node", None),
        P(None, "node", None),
    )
    return jax.shard_map(
        on_device,
        mesh=mesh,
        in_specs=placed,
        out_specs=P("rhs", None, "node", None),
        check_vma=False,
    )
```

```python
import functools

import jax
import jax.numpy as jnp
from jax import lax
from jax.experimental import pallas as pl
from jax.experimental.pallas import tpu as pltpu
from jax.sharding import PartitionSpec as P

F32 = jnp.float32
BF16 = jnp.bfloat16
NT = (((1,), (1,)), ((), ()))
NN = (((1,), (0,)), ((), ()))

ORDER = (0, 1, 3, 2)


def dot(a, b, dims):
    return lax.dot_general(a, b, dims, preferred_element_type=F32)


def slot_of(v, z):
    return (ORDER[v // 2] ^ z) * 2 + v % 2


def level_kernel(config, *refs):
    refs = list(refs)
    take = lambda n: [refs.pop(0) for _ in range(n)]
    rows, fanout = config["rows"], config["fanout"]
    level, down, up = config["level"], config["down"], config["up"]
    linked = level > 0
    last = fanout if linked else 0
    z = lax.axis_index("rhs")
    place = take(1)[0] if linked else None
    tiles = take(max(spec[0] for spec in config["tiles"]) + 1)
    tiles = [(tiles[ref], at, skip) for ref, at, skip in config["tiles"]]
    if down:
        mine, other = take(2)
        solved = take(1)[0] if linked else None
    else:
        stored, incoming = take(2)
    out_f = take(1)[0] if not up else None
    if up:
        result_mine, result_other = take(2)
        keep, sent = take(2) if linked else (None, None)
    right = take(1)[0] if down else None
    total = take(1)[0] if up and linked else None

    def tile(v, k):
        ref, at, skip = tiles[v // 2]
        return ref[v % 2, skip + k] if at is None else ref[at, v % 2, skip + k]

    def wide(v):
        return jnp.concatenate([tile(v, k) for k in range(fanout)], axis=1)

    def places(v):
        base = ((level - 1) * rows + slot_of(v, z)) * fanout
        return [place[base + k] for k in range(fanout)]

    if total is not None:
        total[...] = jnp.zeros_like(total)
    if down:
        columns = mine.shape[0]
        for s in range(rows):
            right[s, :columns] = mine[:, level, s, :]
            right[s, columns:] = other[:, level, s, :]
        values = []
        for v in range(rows):
            current = right[slot_of(v, z)]
            if linked:
                picked = jnp.concatenate([solved[at] for at in places(v)], axis=1)
                current = current - dot(picked, wide(v), NT)
            values.append(current.astype(BF16))
        values = [dot(values[v], tile(v, last), NT).astype(BF16) for v in range(rows)]
        if not up:
            for v in range(rows):
                out_f[v] = values[v]
            return
    else:
        values = []
        for v in range(rows):
            values.append((stored[v].astype(F32) - incoming[v]).astype(BF16))
    answers = [dot(values[v], tile(v, last), NN) for v in range(rows)]
    columns = result_mine.shape[1]
    for v in range(rows):
        result_mine[slot_of(v, z)] = answers[v][:columns]
        result_other[slot_of(v, z)] = answers[v][columns:].astype(result_other.dtype)
    if not linked:
        return
    size = answers[0].shape[1]
    for v in range(rows):
        terms = dot(answers[v].astype(BF16), wide(v), NN)
        for k, at in enumerate(places(v)):
            total[at] += terms[:, k * size : (k + 1) * size]
    middle = total.shape[0] // 2
    keep[...] = total[:middle]
    sent[...] = total[middle:].astype(BF16)


def finish_kernel(spans, *refs):
    z = lax.axis_index("rhs")
    inner = (z == 1) | (z == 2)
    refs, out = list(refs[:-1]), refs[-1]
    for span in spans:
        home = refs.pop(0)
        for i, level in enumerate(span):
            mine = refs.pop(0)
            for s in range(mine.shape[0]):
                out[:, level, s, :] = jnp.where(inner, mine[s], home[i, s].astype(F32))


VMEM = pl.BlockSpec(memory_space=pltpu.VMEM)
SMEM = pl.BlockSpec(memory_space=pltpu.SMEM)


def params():
    return pltpu.CompilerParams(vmem_limit_bytes=32 * 1024 * 1024)


def on_device(right_side, diag_tiles, off_tiles, src_part, src_slot):
    columns, levels, rows, size = right_side.shape
    fanout = src_part.shape[2]
    nodes = lax.axis_size("node")
    chips = nodes // 2
    node, z = lax.axis_index("node"), lax.axis_index("rhs")

    def inward(x):
        return lax.ppermute(x, "rhs", [(0, 1), (3, 2)])

    def outward(x):
        return lax.ppermute(x, "rhs", [(1, 0), (2, 3)])

    def between(x):
        return lax.ppermute(x, "rhs", [(1, 2), (2, 1)])

    def shift(x, d):
        return lax.ppermute(x, "node", [(n, n ^ d) for n in range(nodes)])

    def after(x, *others):
        return lax.optimization_barrier((x, *others))[0]

    held, where = {}, {}

    def hold(level, arrays, places):
        held[level], where[level] = arrays, places

    pieces = [diag_tiles[0][:, None]] + [
        jnp.concatenate([off_tiles[level - 1], diag_tiles[level][:, None]], axis=1)
        for level in range(1, levels)
    ]
    rel = src_part ^ node
    pair = (src_slot >> 1) ^ z
    inner = (pair ^ (pair >> 1)) * 2 + (src_slot & 1)
    place = (((rel >> 1) + (rel & 1) * chips) * rows + inner).reshape(-1)

    near, both = {}, {}

    def join(level, *others):
        block, at = near[level]
        pair = jnp.stack([pieces[level], block if at is None else block[at]])
        both[level] = between(after(pair, *others))
        places = [(0, None, 0), (1, at, 0), (2, 0, 0), (2, 1, 0)]
        hold(level, [pieces[level], block, both[level]], places)

    facing = between(jnp.concatenate(pieces[:2], axis=1))
    other_right = inward(right_side)
    near[0] = inward(pieces[0]), None
    near[1] = inward(after(pieces[1], other_right, near[0][0])), None

    def meet(level, *others):
        block = near[level][0]
        corner = between(after(block, *others))
        places = [(0, None, 0), (1, None, 0), (2, None, level), (3, None, 0)]
        hold(level, [pieces[level], block, facing, corner], places)
        return corner

    middle = inward(after(jnp.stack(pieces[2:4]), other_right, meet(0, place)))
    near[2], near[3] = (middle, 0), (middle, 1)

    vec = (rows, 2 * columns, size)
    own = (rows, columns, size)

    def run(level, down, up, inputs):
        linked = level > 0
        config = dict(
            rows=rows,
            fanout=fanout,
            level=level,
            down=down,
            up=up,
            tiles=where[level],
        )
        args = ([place] if linked else []) + list(held[level]) + list(inputs)
        shapes, scratch = [], []
        if down:
            scratch.append(pltpu.VMEM(vec, F32))
        if not up:
            shapes.append(jax.ShapeDtypeStruct(vec, BF16))
        else:
            shapes += [jax.ShapeDtypeStruct(own, t) for t in (F32, BF16)]
            if linked:
                shapes += [jax.ShapeDtypeStruct((chips * rows,) + vec[1:], t) for t in (F32, BF16)]
                scratch.append(pltpu.VMEM((nodes * rows,) + vec[1:], F32))
        dots = rows * ((fanout if linked else 0) + 1) * (int(down) + int(up))
        return pl.pallas_call(
            functools.partial(level_kernel, config),
            in_specs=([SMEM] if linked else []) + [VMEM] * (len(args) - int(linked)),
            out_specs=[VMEM] * len(shapes),
            out_shape=shapes,
            scratch_shapes=scratch,
            compiler_params=params(),
            cost_estimate=pl.CostEstimate(
                flops=4 * dots * columns * size * size,
                bytes_accessed=dots * size * size * 2,
                transcendentals=0,
            ),
        )(*args)

    def gather(value, *early):
        met = jnp.concatenate([value] + [shift(value, 2 * d) for d in range(1, chips)])
        core = after(met, *early)
        return jnp.concatenate([core, shift(core, 1)])

    def scatter(keep, sent):
        summed = keep + shift(sent, 1).astype(F32)
        parts = [summed[d * rows : (d + 1) * rows] for d in range(chips)]
        incoming = parts[0]
        for d in range(chips - 1, 0, -1):
            incoming = incoming + shift(parts[d].astype(BF16), 2 * d).astype(F32)
        return incoming

    stored = []
    inputs = [right_side, other_right]
    for level in range(levels - 1):
        (value,) = run(level, True, False, inputs)
        stored.append(value)
        gathered = gather(value, *([both[level + 1]] if level > 0 else [meet(1, value), middle]))
        if level == 0:
            near[4] = inward(after(pieces[4], gathered)), None
        if level + 2 < levels:
            join(level + 2, value if level > 0 else gathered)
        inputs = [right_side, other_right, gathered]
    mine, others = [None] * levels, [None] * levels
    mine[-1], others[-1], *sums = run(levels - 1, True, True, inputs)
    for level in range(levels - 2, -1, -1):
        outs = run(level, False, True, [stored[level], scatter(*sums)])
        mine[level], others[level], *sums = outs
    spans = [list(range(levels - 1, 0, -1)), [0]]
    args = []
    for span in spans:
        args += [outward(jnp.stack([others[x] for x in span]))] + [mine[x] for x in span]
    return pl.pallas_call(
        functools.partial(finish_kernel, spans),
        in_specs=[VMEM] * len(args),
        out_specs=VMEM,
        out_shape=jax.ShapeDtypeStruct(right_side.shape, F32),
        compiler_params=params(),
    )(*args)


def solution(mesh):
    placed = (
        P("rhs", None, "node", None),
        P(None, ("node", "rhs"), None, None),
        P(None, ("node", "rhs"), None, None, None),
        P(None, "node", None),
        P(None, "node", None),
    )
    return jax.shard_map(
        on_device,
        mesh=mesh,
        in_specs=placed,
        out_specs=P("rhs", None, "node", None),
        check_vma=False,
    )
```

```python
import functools

import jax
import jax.numpy as jnp
from jax import lax
from jax.experimental import pallas as pl
from jax.experimental.pallas import tpu as pltpu
from jax.sharding import PartitionSpec as P

F32 = jnp.float32
BF16 = jnp.bfloat16
NT = (((1,), (1,)), ((), ()))
NN = (((1,), (0,)), ((), ()))

ORDER = (0, 1, 3, 2)


def dot(a, b, dims):
    return lax.dot_general(a, b, dims, preferred_element_type=F32)


def slot_of(v, z):
    return (ORDER[v // 2] ^ z) * 2 + v % 2


def level_kernel(config, *refs):
    refs = list(refs)
    take = lambda n: [refs.pop(0) for _ in range(n)]
    rows, fanout = config["rows"], config["fanout"]
    level, down, up = config["level"], config["down"], config["up"]
    linked = level > 0
    last = fanout if linked else 0
    z = lax.axis_index("rhs")
    place = take(1)[0] if linked else None
    tiles = take(max(spec[0] for spec in config["tiles"]) + 1)
    tiles = [(tiles[ref], at, skip) for ref, at, skip in config["tiles"]]
    if down:
        mine, other = take(2)
        solved = take(1)[0] if linked else None
    else:
        stored, incoming = take(2)
    out_f = take(1)[0] if not up else None
    if up:
        result_mine, result_other = take(2)
        keep, sent = take(2) if linked else (None, None)
    right = take(1)[0] if down else None
    total = take(1)[0] if up and linked else None

    def tile(v, k):
        ref, at, skip = tiles[v // 2]
        return ref[v % 2, skip + k] if at is None else ref[at, v % 2, skip + k]

    def wide(v):
        return jnp.concatenate([tile(v, k) for k in range(fanout)], axis=1)

    def places(v):
        base = ((level - 1) * rows + slot_of(v, z)) * fanout
        return [place[base + k] for k in range(fanout)]

    if total is not None:
        total[...] = jnp.zeros_like(total)
    if down:
        columns = mine.shape[0]
        for s in range(rows):
            right[s, :columns] = mine[:, level, s, :]
            right[s, columns:] = other[:, level, s, :]
        values = []
        for v in range(rows):
            current = right[slot_of(v, z)]
            if linked:
                picked = jnp.concatenate([solved[at] for at in places(v)], axis=1)
                current = current - dot(picked, wide(v), NT)
            values.append(current.astype(BF16))
        values = [dot(values[v], tile(v, last), NT).astype(BF16) for v in range(rows)]
        if not up:
            for v in range(rows):
                out_f[v] = values[v]
            return
    else:
        values = []
        for v in range(rows):
            values.append((stored[v].astype(F32) - incoming[v]).astype(BF16))
    answers = [dot(values[v], tile(v, last), NN) for v in range(rows)]
    columns = result_mine.shape[1]
    for v in range(rows):
        result_mine[slot_of(v, z)] = answers[v][:columns]
        result_other[slot_of(v, z)] = answers[v][columns:].astype(result_other.dtype)
    if not linked:
        return
    size = answers[0].shape[1]
    for v in range(rows):
        terms = dot(answers[v].astype(BF16), wide(v), NN)
        for k, at in enumerate(places(v)):
            total[at] += terms[:, k * size : (k + 1) * size]
    middle = total.shape[0] // 2
    keep[...] = total[:middle]
    sent[...] = total[middle:].astype(BF16)


def finish_kernel(spans, *refs):
    z = lax.axis_index("rhs")
    inner = (z == 1) | (z == 2)
    refs, out = list(refs[:-1]), refs[-1]
    for span in spans:
        home = refs.pop(0)
        for i, level in enumerate(span):
            mine = refs.pop(0)
            for s in range(mine.shape[0]):
                out[:, level, s, :] = jnp.where(inner, mine[s], home[i, s].astype(F32))


VMEM = pl.BlockSpec(memory_space=pltpu.VMEM)
SMEM = pl.BlockSpec(memory_space=pltpu.SMEM)


def params():
    return pltpu.CompilerParams(vmem_limit_bytes=32 * 1024 * 1024)


def on_device(right_side, diag_tiles, off_tiles, src_part, src_slot):
    columns, levels, rows, size = right_side.shape
    fanout = src_part.shape[2]
    nodes = lax.axis_size("node")
    chips = nodes // 2
    node, z = lax.axis_index("node"), lax.axis_index("rhs")

    def inward(x):
        return lax.ppermute(x, "rhs", [(0, 1), (3, 2)])

    def outward(x):
        return lax.ppermute(x, "rhs", [(1, 0), (2, 3)])

    def between(x):
        return lax.ppermute(x, "rhs", [(1, 2), (2, 1)])

    def shift(x, d):
        return lax.ppermute(x, "node", [(n, n ^ d) for n in range(nodes)])

    def after(x, *others):
        return lax.optimization_barrier((x, *others))[0]

    held, where = {}, {}

    def hold(level, arrays, places):
        held[level], where[level] = arrays, places

    pieces = [diag_tiles[0][:, None]] + [
        jnp.concatenate([off_tiles[level - 1], diag_tiles[level][:, None]], axis=1)
        for level in range(1, levels)
    ]
    rel = src_part ^ node
    pair = (src_slot >> 1) ^ z
    inner = (pair ^ (pair >> 1)) * 2 + (src_slot & 1)
    place = (((rel >> 1) + (rel & 1) * chips) * rows + inner).reshape(-1)

    near, both = {}, {}

    def join(level, *others):
        block, at = near[level]
        pair = jnp.stack([pieces[level], block if at is None else block[at]])
        both[level] = between(after(pair, *others))
        places = [(0, None, 0), (1, at, 0), (2, 0, 0), (2, 1, 0)]
        hold(level, [pieces[level], block, both[level]], places)

    facing = between(jnp.concatenate(pieces[:2], axis=1))
    other_right = inward(right_side)
    near[0] = inward(pieces[0]), None
    near[1] = inward(after(pieces[1], near[0][0])), None

    def meet(level, *others):
        block = near[level][0]
        corner = between(after(block, *others))
        places = [(0, None, 0), (1, None, 0), (2, None, level), (3, None, 0)]
        hold(level, [pieces[level], block, facing, corner], places)
        return corner

    middle = inward(after(jnp.stack(pieces[2:4]), other_right, meet(0, place)))
    near[2], near[3] = (middle, 0), (middle, 1)

    vec = (rows, 2 * columns, size)
    own = (rows, columns, size)

    def run(level, down, up, inputs):
        linked = level > 0
        config = dict(
            rows=rows,
            fanout=fanout,
            level=level,
            down=down,
            up=up,
            tiles=where[level],
        )
        args = ([place] if linked else []) + list(held[level]) + list(inputs)
        shapes, scratch = [], []
        if down:
            scratch.append(pltpu.VMEM(vec, F32))
        if not up:
            shapes.append(jax.ShapeDtypeStruct(vec, BF16))
        else:
            shapes += [jax.ShapeDtypeStruct(own, t) for t in (F32, BF16)]
            if linked:
                shapes += [jax.ShapeDtypeStruct((chips * rows,) + vec[1:], t) for t in (F32, BF16)]
                scratch.append(pltpu.VMEM((nodes * rows,) + vec[1:], F32))
        dots = rows * ((fanout if linked else 0) + 1) * (int(down) + int(up))
        return pl.pallas_call(
            functools.partial(level_kernel, config),
            in_specs=([SMEM] if linked else []) + [VMEM] * (len(args) - int(linked)),
            out_specs=[VMEM] * len(shapes),
            out_shape=shapes,
            scratch_shapes=scratch,
            compiler_params=params(),
            cost_estimate=pl.CostEstimate(
                flops=4 * dots * columns * size * size,
                bytes_accessed=dots * size * size * 2,
                transcendentals=0,
            ),
        )(*args)

    def gather(value, *early):
        met = jnp.concatenate([value] + [shift(value, 2 * d) for d in range(1, chips)])
        core = after(met, *early)
        return jnp.concatenate([core, shift(core, 1)])

    def scatter(keep, sent):
        summed = keep + shift(sent, 1).astype(F32)
        parts = [summed[d * rows : (d + 1) * rows] for d in range(chips)]
        incoming = parts[0]
        for d in range(chips - 1, 0, -1):
            incoming = incoming + shift(parts[d].astype(BF16), 2 * d).astype(F32)
        return incoming

    stored = []
    inputs = [right_side, other_right]
    for level in range(levels - 1):
        (value,) = run(level, True, False, inputs)
        stored.append(value)
        early = [meet(1, value), middle] if level == 0 else [both[level + 1]]
        if level == 1:
            early.append(near[4][0])
        gathered = gather(value, *early)
        if level == 0:
            near[4] = inward(after(pieces[4], gathered)), None
        if level + 2 < levels:
            join(level + 2, value if level > 0 else gathered)
        inputs = [right_side, other_right, gathered]
    mine, others = [None] * levels, [None] * levels
    mine[-1], others[-1], *sums = run(levels - 1, True, True, inputs)
    for level in range(levels - 2, -1, -1):
        outs = run(level, False, True, [stored[level], scatter(*sums)])
        mine[level], others[level], *sums = outs
    spans = [list(range(levels - 1, 0, -1)), [0]]
    args = []
    for span in spans:
        args += [outward(jnp.stack([others[x] for x in span]))] + [mine[x] for x in span]
    return pl.pallas_call(
        functools.partial(finish_kernel, spans),
        in_specs=[VMEM] * len(args),
        out_specs=VMEM,
        out_shape=jax.ShapeDtypeStruct(right_side.shape, F32),
        compiler_params=params(),
    )(*args)


def solution(mesh):
    placed = (
        P("rhs", None, "node", None),
        P(None, ("node", "rhs"), None, None),
        P(None, ("node", "rhs"), None, None, None),
        P(None, "node", None),
        P(None, "node", None),
    )
    return jax.shard_map(
        on_device,
        mesh=mesh,
        in_specs=placed,
        out_specs=P("rhs", None, "node", None),
        check_vma=False,
    )
```

```python
import functools

import jax
import jax.numpy as jnp
from jax import lax
from jax.experimental import pallas as pl
from jax.experimental.pallas import tpu as pltpu
from jax.sharding import PartitionSpec as P

F32 = jnp.float32
BF16 = jnp.bfloat16
NT = (((1,), (1,)), ((), ()))
NN = (((1,), (0,)), ((), ()))

ORDER = (0, 1, 3, 2)


def dot(a, b, dims):
    return lax.dot_general(a, b, dims, preferred_element_type=F32)


def slot_of(v, z):
    return (ORDER[v // 2] ^ z) * 2 + v % 2


def level_kernel(config, *refs):
    refs = list(refs)
    take = lambda n: [refs.pop(0) for _ in range(n)]
    rows, fanout = config["rows"], config["fanout"]
    level, down, up = config["level"], config["down"], config["up"]
    linked = level > 0
    last = fanout if linked else 0
    z = lax.axis_index("rhs")
    place = take(1)[0] if linked else None
    tiles = take(max(spec[0] for spec in config["tiles"]) + 1)
    tiles = [(tiles[ref], at, skip) for ref, at, skip in config["tiles"]]
    if down:
        mine, other = take(2)
        solved = take(1)[0] if linked else None
    else:
        stored, incoming = take(2)
    out_f = take(1)[0] if not up else None
    if up:
        result_mine, result_other = take(2)
        keep, sent = take(2) if linked else (None, None)
    right = take(1)[0] if down else None
    total = take(1)[0] if up and linked else None

    def tile(v, k):
        ref, at, skip = tiles[v // 2]
        return ref[v % 2, skip + k] if at is None else ref[at, v % 2, skip + k]

    def wide(v):
        return jnp.concatenate([tile(v, k) for k in range(fanout)], axis=1)

    def places(v):
        base = ((level - 1) * rows + slot_of(v, z)) * fanout
        return [place[base + k] for k in range(fanout)]

    if total is not None:
        total[...] = jnp.zeros_like(total)
    if down:
        columns = mine.shape[0]
        for s in range(rows):
            right[s, :columns] = mine[:, level, s, :]
            right[s, columns:] = other[:, level, s, :]
        values = []
        for v in range(rows):
            current = right[slot_of(v, z)]
            if linked:
                picked = jnp.concatenate([solved[at] for at in places(v)], axis=1)
                current = current - dot(picked, wide(v), NT)
            values.append(current.astype(BF16))
        values = [dot(values[v], tile(v, last), NT).astype(BF16) for v in range(rows)]
        if not up:
            for v in range(rows):
                out_f[v] = values[v]
            return
    else:
        values = []
        for v in range(rows):
            values.append((stored[v].astype(F32) - incoming[v]).astype(BF16))
    answers = [dot(values[v], tile(v, last), NN) for v in range(rows)]
    columns = result_mine.shape[1]
    for v in range(rows):
        result_mine[slot_of(v, z)] = answers[v][:columns]
        result_other[slot_of(v, z)] = answers[v][columns:].astype(result_other.dtype)
    if not linked:
        return
    size = answers[0].shape[1]
    for v in range(rows):
        terms = dot(answers[v].astype(BF16), wide(v), NN)
        for k, at in enumerate(places(v)):
            total[at] += terms[:, k * size : (k + 1) * size]
    middle = total.shape[0] // 2
    keep[...] = total[:middle]
    sent[...] = total[middle:].astype(BF16)


def finish_kernel(spans, *refs):
    z = lax.axis_index("rhs")
    inner = (z == 1) | (z == 2)
    refs, out = list(refs[:-1]), refs[-1]
    for span in spans:
        home = refs.pop(0)
        for i, level in enumerate(span):
            mine = refs.pop(0)
            for s in range(mine.shape[0]):
                out[:, level, s, :] = jnp.where(inner, mine[s], home[i, s].astype(F32))


VMEM = pl.BlockSpec(memory_space=pltpu.VMEM)
SMEM = pl.BlockSpec(memory_space=pltpu.SMEM)


def params():
    return pltpu.CompilerParams(vmem_limit_bytes=32 * 1024 * 1024)


def on_device(right_side, diag_tiles, off_tiles, src_part, src_slot):
    columns, levels, rows, size = right_side.shape
    fanout = src_part.shape[2]
    nodes = lax.axis_size("node")
    chips = nodes // 2
    node, z = lax.axis_index("node"), lax.axis_index("rhs")

    def inward(x):
        return lax.ppermute(x, "rhs", [(0, 1), (3, 2)])

    def outward(x):
        return lax.ppermute(x, "rhs", [(1, 0), (2, 3)])

    def between(x):
        return lax.ppermute(x, "rhs", [(1, 2), (2, 1)])

    def shift(x, d):
        return lax.ppermute(x, "node", [(n, n ^ d) for n in range(nodes)])

    def after(x, *others):
        return lax.optimization_barrier((x, *others))[0]

    held, where = {}, {}

    def hold(level, arrays, places):
        held[level], where[level] = arrays, places

    pieces = [diag_tiles[0][:, None]] + [
        jnp.concatenate([off_tiles[level - 1], diag_tiles[level][:, None]], axis=1)
        for level in range(1, levels)
    ]
    rel = src_part ^ node
    pair = (src_slot >> 1) ^ z
    inner = (pair ^ (pair >> 1)) * 2 + (src_slot & 1)
    place = (((rel >> 1) + (rel & 1) * chips) * rows + inner).reshape(-1)

    near, both = {}, {}

    def join(level, *others):
        block, at = near[level]
        pair = jnp.stack([pieces[level], block if at is None else block[at]])
        both[level] = between(after(pair, *others))
        places = [(0, None, 0), (1, at, 0), (2, 0, 0), (2, 1, 0)]
        hold(level, [pieces[level], block, both[level]], places)

    def meet(level, *others):
        block = near[level][0]
        corner = between(after(block, *others))
        places = [(i, None, 0) for i in range(4)]
        hold(level, [pieces[level], block, facing[level], corner], places)
        return corner

    near[0] = inward(pieces[0]), None
    facing = {0: between(pieces[0])}
    other_right = inward(right_side)
    near[1] = inward(pieces[1]), None
    middle = inward(after(jnp.stack(pieces[2:4]), near[0][0]))
    near[2], near[3] = (middle, 0), (middle, 1)
    facing[1] = between(after(pieces[1], meet(0, place)))

    vec = (rows, 2 * columns, size)
    own = (rows, columns, size)

    def run(level, down, up, inputs):
        linked = level > 0
        config = dict(
            rows=rows,
            fanout=fanout,
            level=level,
            down=down,
            up=up,
            tiles=where[level],
        )
        args = ([place] if linked else []) + list(held[level]) + list(inputs)
        shapes, scratch = [], []
        if down:
            scratch.append(pltpu.VMEM(vec, F32))
        if not up:
            shapes.append(jax.ShapeDtypeStruct(vec, BF16))
        else:
            shapes += [jax.ShapeDtypeStruct(own, t) for t in (F32, BF16)]
            if linked:
                shapes += [jax.ShapeDtypeStruct((chips * rows,) + vec[1:], t) for t in (F32, BF16)]
                scratch.append(pltpu.VMEM((nodes * rows,) + vec[1:], F32))
        dots = rows * ((fanout if linked else 0) + 1) * (int(down) + int(up))
        return pl.pallas_call(
            functools.partial(level_kernel, config),
            in_specs=([SMEM] if linked else []) + [VMEM] * (len(args) - int(linked)),
            out_specs=[VMEM] * len(shapes),
            out_shape=shapes,
            scratch_shapes=scratch,
            compiler_params=params(),
            cost_estimate=pl.CostEstimate(
                flops=4 * dots * columns * size * size,
                bytes_accessed=dots * size * size * 2,
                transcendentals=0,
            ),
        )(*args)

    def gather(value, *early):
        met = jnp.concatenate([value] + [shift(value, 2 * d) for d in range(1, chips)])
        core = after(met, *early)
        return jnp.concatenate([core, shift(core, 1)])

    def scatter(keep, sent):
        summed = keep + shift(sent, 1).astype(F32)
        parts = [summed[d * rows : (d + 1) * rows] for d in range(chips)]
        incoming = parts[0]
        for d in range(chips - 1, 0, -1):
            incoming = incoming + shift(parts[d].astype(BF16), 2 * d).astype(F32)
        return incoming

    stored = []
    inputs = [right_side, other_right]
    for level in range(levels - 1):
        (value,) = run(level, True, False, inputs)
        stored.append(value)
        early = [meet(1, value, facing[1]), middle] if level == 0 else [both[level + 1]]
        if level == 1:
            early.append(near[4][0])
        gathered = gather(value, *early)
        if level == 0:
            near[4] = inward(after(pieces[4], gathered)), None
        if level + 2 < levels:
            join(level + 2, value if level > 0 else gathered)
        inputs = [right_side, other_right, gathered]
    mine, others = [None] * levels, [None] * levels
    mine[-1], others[-1], *sums = run(levels - 1, True, True, inputs)
    for level in range(levels - 2, -1, -1):
        outs = run(level, False, True, [stored[level], scatter(*sums)])
        mine[level], others[level], *sums = outs
    spans = [list(range(levels - 1, 0, -1)), [0]]
    args = []
    for span in spans:
        args += [outward(jnp.stack([others[x] for x in span]))] + [mine[x] for x in span]
    return pl.pallas_call(
        functools.partial(finish_kernel, spans),
        in_specs=[VMEM] * len(args),
        out_specs=VMEM,
        out_shape=jax.ShapeDtypeStruct(right_side.shape, F32),
        compiler_params=params(),
    )(*args)


def solution(mesh):
    placed = (
        P("rhs", None, "node", None),
        P(None, ("node", "rhs"), None, None),
        P(None, ("node", "rhs"), None, None, None),
        P(None, "node", None),
        P(None, "node", None),
    )
    return jax.shard_map(
        on_device,
        mesh=mesh,
        in_specs=placed,
        out_specs=P("rhs", None, "node", None),
        check_vma=False,
    )
```

```python
import functools

import jax
import jax.numpy as jnp
from jax import lax
from jax.experimental import pallas as pl
from jax.experimental.pallas import tpu as pltpu
from jax.sharding import PartitionSpec as P

F32 = jnp.float32
BF16 = jnp.bfloat16
NT = (((1,), (1,)), ((), ()))
NN = (((1,), (0,)), ((), ()))

ORDER = (0, 1, 3, 2)


def dot(a, b, dims):
    return lax.dot_general(a, b, dims, preferred_element_type=F32)


def slot_of(v, z):
    return (ORDER[v // 2] ^ z) * 2 + v % 2


def level_kernel(config, *refs):
    refs = list(refs)
    take = lambda n: [refs.pop(0) for _ in range(n)]
    rows, fanout = config["rows"], config["fanout"]
    level, down, up = config["level"], config["down"], config["up"]
    linked = level > 0
    last = fanout if linked else 0
    z = lax.axis_index("rhs")
    place = take(1)[0] if linked else None
    tiles = take(max(spec[0] for spec in config["tiles"]) + 1)
    tiles = [(tiles[ref], at, skip) for ref, at, skip in config["tiles"]]
    if down:
        mine, other = take(2)
        solved = take(1)[0] if linked else None
    else:
        stored, incoming = take(2)
    out_f = take(1)[0] if not up else None
    if up:
        result_mine, result_other = take(2)
        keep, sent = take(2) if linked else (None, None)
    right = take(1)[0] if down else None
    total = take(1)[0] if up and linked else None

    def tile(v, k):
        ref, at, skip = tiles[v // 2]
        return ref[v % 2, skip + k] if at is None else ref[at, v % 2, skip + k]

    def wide(v):
        return jnp.concatenate([tile(v, k) for k in range(fanout)], axis=1)

    def places(v):
        base = ((level - 1) * rows + slot_of(v, z)) * fanout
        return [place[base + k] for k in range(fanout)]

    if total is not None:
        total[...] = jnp.zeros_like(total)
    if down:
        columns = mine.shape[0]
        for s in range(rows):
            right[s, :columns] = mine[:, level, s, :]
            right[s, columns:] = other[:, level, s, :]
        values = []
        for v in range(rows):
            current = right[slot_of(v, z)]
            if linked:
                picked = jnp.concatenate([solved[at] for at in places(v)], axis=1)
                current = current - dot(picked, wide(v), NT)
            values.append(current.astype(BF16))
        values = [dot(values[v], tile(v, last), NT).astype(BF16) for v in range(rows)]
        if not up:
            for v in range(rows):
                out_f[v] = values[v]
            return
    else:
        values = []
        for v in range(rows):
            values.append((stored[v].astype(F32) - incoming[v]).astype(BF16))
    answers = [dot(values[v], tile(v, last), NN) for v in range(rows)]
    columns = result_mine.shape[1]
    for v in range(rows):
        result_mine[slot_of(v, z)] = answers[v][:columns]
        result_other[slot_of(v, z)] = answers[v][columns:].astype(result_other.dtype)
    if not linked:
        return
    size = answers[0].shape[1]
    for v in range(rows):
        terms = dot(answers[v].astype(BF16), wide(v), NN)
        for k, at in enumerate(places(v)):
            total[at] += terms[:, k * size : (k + 1) * size]
    middle = total.shape[0] // 2
    keep[...] = total[:middle]
    sent[...] = total[middle:].astype(BF16)


def finish_kernel(spans, *refs):
    z = lax.axis_index("rhs")
    inner = (z == 1) | (z == 2)
    refs, out = list(refs[:-1]), refs[-1]
    for span in spans:
        home = refs.pop(0)
        for i, level in enumerate(span):
            mine = refs.pop(0)
            for s in range(mine.shape[0]):
                out[:, level, s, :] = jnp.where(inner, mine[s], home[i, s].astype(F32))


VMEM = pl.BlockSpec(memory_space=pltpu.VMEM)
SMEM = pl.BlockSpec(memory_space=pltpu.SMEM)


def params():
    return pltpu.CompilerParams(vmem_limit_bytes=32 * 1024 * 1024)


def on_device(right_side, diag_tiles, off_tiles, src_part, src_slot):
    columns, levels, rows, size = right_side.shape
    fanout = src_part.shape[2]
    nodes = lax.axis_size("node")
    chips = nodes // 2
    node, z = lax.axis_index("node"), lax.axis_index("rhs")

    def inward(x):
        return lax.ppermute(x, "rhs", [(0, 1), (3, 2)])

    def outward(x):
        return lax.ppermute(x, "rhs", [(1, 0), (2, 3)])

    def between(x):
        return lax.ppermute(x, "rhs", [(1, 2), (2, 1)])

    def shift(x, d):
        return lax.ppermute(x, "node", [(n, n ^ d) for n in range(nodes)])

    def after(x, *others):
        return lax.optimization_barrier((x, *others))[0]

    held, where = {}, {}

    def hold(level, arrays, places):
        held[level], where[level] = arrays, places

    pieces = [diag_tiles[0][:, None]] + [
        jnp.concatenate([off_tiles[level - 1], diag_tiles[level][:, None]], axis=1)
        for level in range(1, levels)
    ]
    rel = src_part ^ node
    pair = (src_slot >> 1) ^ z
    inner = (pair ^ (pair >> 1)) * 2 + (src_slot & 1)
    place = (((rel >> 1) + (rel & 1) * chips) * rows + inner).reshape(-1)

    near, both = {}, {}

    def join(level, *others):
        block, at = near[level]
        pair = jnp.stack([pieces[level], block if at is None else block[at]])
        both[level] = between(after(pair, *others))
        places = [(0, None, 0), (1, at, 0), (2, 0, 0), (2, 1, 0)]
        hold(level, [pieces[level], block, both[level]], places)

    def meet(level, *others):
        block = near[level][0]
        corner = between(after(block, *others))
        places = [(i, None, 0) for i in range(4)]
        hold(level, [pieces[level], block, facing[level], corner], places)
        return corner

    near[0] = inward(pieces[0]), None
    facing = {0: between(pieces[0])}
    other_right = inward(right_side)
    near[1] = inward(pieces[1]), None
    middle = inward(after(jnp.stack(pieces[2:4]), near[0][0]))
    near[2], near[3] = (middle, 0), (middle, 1)
    facing[1] = between(after(pieces[1], meet(0, place), facing[0]))

    vec = (rows, 2 * columns, size)
    own = (rows, columns, size)

    def run(level, down, up, inputs):
        linked = level > 0
        config = dict(
            rows=rows,
            fanout=fanout,
            level=level,
            down=down,
            up=up,
            tiles=where[level],
        )
        args = ([place] if linked else []) + list(held[level]) + list(inputs)
        shapes, scratch = [], []
        if down:
            scratch.append(pltpu.VMEM(vec, F32))
        if not up:
            shapes.append(jax.ShapeDtypeStruct(vec, BF16))
        else:
            shapes += [jax.ShapeDtypeStruct(own, t) for t in (F32, BF16)]
            if linked:
                shapes += [jax.ShapeDtypeStruct((chips * rows,) + vec[1:], t) for t in (F32, BF16)]
                scratch.append(pltpu.VMEM((nodes * rows,) + vec[1:], F32))
        dots = rows * ((fanout if linked else 0) + 1) * (int(down) + int(up))
        return pl.pallas_call(
            functools.partial(level_kernel, config),
            in_specs=([SMEM] if linked else []) + [VMEM] * (len(args) - int(linked)),
            out_specs=[VMEM] * len(shapes),
            out_shape=shapes,
            scratch_shapes=scratch,
            compiler_params=params(),
            cost_estimate=pl.CostEstimate(
                flops=4 * dots * columns * size * size,
                bytes_accessed=dots * size * size * 2,
                transcendentals=0,
            ),
        )(*args)

    def gather(value, *early):
        met = jnp.concatenate([value] + [shift(value, 2 * d) for d in range(1, chips)])
        core = after(met, *early)
        return jnp.concatenate([core, shift(core, 1)])

    def scatter(keep, sent):
        summed = keep + shift(sent, 1).astype(F32)
        parts = [summed[d * rows : (d + 1) * rows] for d in range(chips)]
        incoming = parts[0]
        for d in range(chips - 1, 0, -1):
            incoming = incoming + shift(parts[d].astype(BF16), 2 * d).astype(F32)
        return incoming

    stored = []
    inputs = [right_side, other_right]
    for level in range(levels - 1):
        (value,) = run(level, True, False, inputs)
        stored.append(value)
        early = [meet(1, value), middle, facing[1]] if level == 0 else [both[level + 1]]
        if level == 1:
            early.append(near[4][0])
        gathered = gather(value, *early)
        if level == 0:
            near[4] = inward(after(pieces[4], gathered)), None
        if level + 2 < levels:
            join(level + 2, value if level > 0 else gathered)
        inputs = [right_side, other_right, gathered]
    mine, others = [None] * levels, [None] * levels
    mine[-1], others[-1], *sums = run(levels - 1, True, True, inputs)
    for level in range(levels - 2, -1, -1):
        outs = run(level, False, True, [stored[level], scatter(*sums)])
        mine[level], others[level], *sums = outs
    spans = [list(range(levels - 1, 0, -1)), [0]]
    args = []
    for span in spans:
        args += [outward(jnp.stack([others[x] for x in span]))] + [mine[x] for x in span]
    return pl.pallas_call(
        functools.partial(finish_kernel, spans),
        in_specs=[VMEM] * len(args),
        out_specs=VMEM,
        out_shape=jax.ShapeDtypeStruct(right_side.shape, F32),
        compiler_params=params(),
    )(*args)


def solution(mesh):
    placed = (
        P("rhs", None, "node", None),
        P(None, ("node", "rhs"), None, None),
        P(None, ("node", "rhs"), None, None, None),
        P(None, "node", None),
        P(None, "node", None),
    )
    return jax.shard_map(
        on_device,
        mesh=mesh,
        in_specs=placed,
        out_specs=P("rhs", None, "node", None),
        check_vma=False,
    )
```

```python
import functools

import jax
import jax.numpy as jnp
from jax import lax
from jax.experimental import pallas as pl
from jax.experimental.pallas import tpu as pltpu
from jax.sharding import PartitionSpec as P

F32 = jnp.float32
BF16 = jnp.bfloat16
NT = (((1,), (1,)), ((), ()))
NN = (((1,), (0,)), ((), ()))

ORDER = (0, 1, 3, 2)


def dot(a, b, dims):
    return lax.dot_general(a, b, dims, preferred_element_type=F32)


def slot_of(v, z):
    return (ORDER[v // 2] ^ z) * 2 + v % 2


def level_kernel(config, *refs):
    refs = list(refs)
    take = lambda n: [refs.pop(0) for _ in range(n)]
    rows, fanout = config["rows"], config["fanout"]
    level, down, up = config["level"], config["down"], config["up"]
    linked = level > 0
    last = fanout if linked else 0
    z = lax.axis_index("rhs")
    place = take(1)[0] if linked else None
    tiles = take(max(spec[0] for spec in config["tiles"]) + 1)
    tiles = [(tiles[ref], at, skip) for ref, at, skip in config["tiles"]]
    if down:
        mine, other = take(2)
        solved = take(1)[0] if linked else None
    else:
        stored, incoming = take(2)
    out_f = take(1)[0] if not up else None
    if up:
        result_mine, result_other = take(2)
        keep, sent = take(2) if linked else (None, None)
    right = take(1)[0] if down else None
    total = take(1)[0] if up and linked else None

    def tile(v, k):
        ref, at, skip = tiles[v // 2]
        return ref[v % 2, skip + k] if at is None else ref[at, v % 2, skip + k]

    def wide(v):
        return jnp.concatenate([tile(v, k) for k in range(fanout)], axis=1)

    def places(v):
        base = ((level - 1) * rows + slot_of(v, z)) * fanout
        return [place[base + k] for k in range(fanout)]

    if total is not None:
        total[...] = jnp.zeros_like(total)
    if down:
        columns = mine.shape[0]
        for s in range(rows):
            right[s, :columns] = mine[:, level, s, :]
            right[s, columns:] = other[:, level, s, :]
        values = []
        for v in range(rows):
            current = right[slot_of(v, z)]
            if linked:
                picked = jnp.concatenate([solved[at] for at in places(v)], axis=1)
                current = current - dot(picked, wide(v), NT)
            values.append(current.astype(BF16))
        values = [dot(values[v], tile(v, last), NT).astype(BF16) for v in range(rows)]
        if not up:
            for v in range(rows):
                out_f[v] = values[v]
            return
    else:
        values = []
        for v in range(rows):
            values.append((stored[v].astype(F32) - incoming[v]).astype(BF16))
    answers = [dot(values[v], tile(v, last), NN) for v in range(rows)]
    columns = result_mine.shape[1]
    for v in range(rows):
        result_mine[slot_of(v, z)] = answers[v][:columns]
        result_other[slot_of(v, z)] = answers[v][columns:].astype(result_other.dtype)
    if not linked:
        return
    size = answers[0].shape[1]
    for v in range(rows):
        terms = dot(answers[v].astype(BF16), wide(v), NN)
        for k, at in enumerate(places(v)):
            total[at] += terms[:, k * size : (k + 1) * size]
    middle = total.shape[0] // 2
    keep[...] = total[:middle]
    sent[...] = total[middle:].astype(BF16)


def finish_kernel(spans, *refs):
    z = lax.axis_index("rhs")
    inner = (z == 1) | (z == 2)
    refs, out = list(refs[:-1]), refs[-1]
    for span in spans:
        home = refs.pop(0)
        for i, level in enumerate(span):
            mine = refs.pop(0)
            for s in range(mine.shape[0]):
                out[:, level, s, :] = jnp.where(inner, mine[s], home[i, s].astype(F32))


VMEM = pl.BlockSpec(memory_space=pltpu.VMEM)
SMEM = pl.BlockSpec(memory_space=pltpu.SMEM)


def params():
    return pltpu.CompilerParams(vmem_limit_bytes=32 * 1024 * 1024)


def on_device(right_side, diag_tiles, off_tiles, src_part, src_slot):
    columns, levels, rows, size = right_side.shape
    fanout = src_part.shape[2]
    nodes = lax.axis_size("node")
    chips = nodes // 2
    node, z = lax.axis_index("node"), lax.axis_index("rhs")

    def inward(x):
        return lax.ppermute(x, "rhs", [(0, 1), (3, 2)])

    def outward(x):
        return lax.ppermute(x, "rhs", [(1, 0), (2, 3)])

    def between(x):
        return lax.ppermute(x, "rhs", [(1, 2), (2, 1)])

    def shift(x, d):
        return lax.ppermute(x, "node", [(n, n ^ d) for n in range(nodes)])

    def after(x, *others):
        return lax.optimization_barrier((x, *others))[0]

    held, where = {}, {}

    def hold(level, arrays, places):
        held[level], where[level] = arrays, places

    pieces = [diag_tiles[0][:, None]] + [
        jnp.concatenate([off_tiles[level - 1], diag_tiles[level][:, None]], axis=1)
        for level in range(1, levels)
    ]
    rel = src_part ^ node
    pair = (src_slot >> 1) ^ z
    inner = (pair ^ (pair >> 1)) * 2 + (src_slot & 1)
    place = (((rel >> 1) + (rel & 1) * chips) * rows + inner).reshape(-1)

    near, both = {}, {}

    def join(level, *others):
        block, at = near[level]
        pair = jnp.stack([pieces[level], block if at is None else block[at]])
        both[level] = between(after(pair, *others))
        places = [(0, None, 0), (1, at, 0), (2, 0, 0), (2, 1, 0)]
        hold(level, [pieces[level], block, both[level]], places)

    facing = between(jnp.concatenate(pieces[:2], axis=1))
    other_right = inward(right_side)
    near[0] = inward(pieces[0]), None
    near[1] = inward(pieces[1]), None
    middle = inward(after(jnp.stack(pieces[2:4]), near[0][0]))
    near[2], near[3] = (middle, 0), (middle, 1)

    def meet(level, *others):
        block, at = near[level]
        corner = between(after(block if at is None else block[at], *others))
        places = [(0, None, 0), (1, at, 0), (2, None, level % 2), (3, None, 0)]
        hold(level, [pieces[level], block, facing if level < 2 else second, corner], places)
        return corner

    meet(0, place)
    second = between(after(pieces[2], facing))

    vec = (rows, 2 * columns, size)
    own = (rows, columns, size)

    def run(level, down, up, inputs):
        linked = level > 0
        config = dict(
            rows=rows,
            fanout=fanout,
            level=level,
            down=down,
            up=up,
            tiles=where[level],
        )
        args = ([place] if linked else []) + list(held[level]) + list(inputs)
        shapes, scratch = [], []
        if down:
            scratch.append(pltpu.VMEM(vec, F32))
        if not up:
            shapes.append(jax.ShapeDtypeStruct(vec, BF16))
        else:
            shapes += [jax.ShapeDtypeStruct(own, t) for t in (F32, BF16)]
            if linked:
                shapes += [jax.ShapeDtypeStruct((chips * rows,) + vec[1:], t) for t in (F32, BF16)]
                scratch.append(pltpu.VMEM((nodes * rows,) + vec[1:], F32))
        dots = rows * ((fanout if linked else 0) + 1) * (int(down) + int(up))
        return pl.pallas_call(
            functools.partial(level_kernel, config),
            in_specs=([SMEM] if linked else []) + [VMEM] * (len(args) - int(linked)),
            out_specs=[VMEM] * len(shapes),
            out_shape=shapes,
            scratch_shapes=scratch,
            compiler_params=params(),
            cost_estimate=pl.CostEstimate(
                flops=4 * dots * columns * size * size,
                bytes_accessed=dots * size * size * 2,
                transcendentals=0,
            ),
        )(*args)

    def gather(value, *early):
        met = jnp.concatenate([value] + [shift(value, 2 * d) for d in range(1, chips)])
        core = after(met, *early)
        return jnp.concatenate([core, shift(core, 1)])

    def scatter(keep, sent):
        summed = keep + shift(sent, 1).astype(F32)
        parts = [summed[d * rows : (d + 1) * rows] for d in range(chips)]
        incoming = parts[0]
        for d in range(chips - 1, 0, -1):
            incoming = incoming + shift(parts[d].astype(BF16), 2 * d).astype(F32)
        return incoming

    stored = []
    inputs = [right_side, other_right]
    for level in range(levels - 1):
        (value,) = run(level, True, False, inputs)
        stored.append(value)
        if level == 0:
            early = [meet(1, value), middle]
        else:
            early = [both[level + 1] if level > 1 else meet(2, stored[0])]
        if level == 1:
            early += [near[4][0], second]
        gathered = gather(value, *early)
        if level == 0:
            near[4] = inward(after(pieces[4], gathered)), None
        if 0 < level < levels - 2:
            join(level + 2, value)
        inputs = [right_side, other_right, gathered]
    mine, others = [None] * levels, [None] * levels
    mine[-1], others[-1], *sums = run(levels - 1, True, True, inputs)
    for level in range(levels - 2, -1, -1):
        outs = run(level, False, True, [stored[level], scatter(*sums)])
        mine[level], others[level], *sums = outs
    spans = [list(range(levels - 1, 0, -1)), [0]]
    args = []
    for span in spans:
        args += [outward(jnp.stack([others[x] for x in span]))] + [mine[x] for x in span]
    return pl.pallas_call(
        functools.partial(finish_kernel, spans),
        in_specs=[VMEM] * len(args),
        out_specs=VMEM,
        out_shape=jax.ShapeDtypeStruct(right_side.shape, F32),
        compiler_params=params(),
    )(*args)


def solution(mesh):
    placed = (
        P("rhs", None, "node", None),
        P(None, ("node", "rhs"), None, None),
        P(None, ("node", "rhs"), None, None, None),
        P(None, "node", None),
        P(None, "node", None),
    )
    return jax.shard_map(
        on_device,
        mesh=mesh,
        in_specs=placed,
        out_specs=P("rhs", None, "node", None),
        check_vma=False,
    )
```

```python
import functools

import jax
import jax.numpy as jnp
from jax import lax
from jax.experimental import pallas as pl
from jax.experimental.pallas import tpu as pltpu
from jax.sharding import PartitionSpec as P

F32 = jnp.float32
BF16 = jnp.bfloat16
NT = (((1,), (1,)), ((), ()))
NN = (((1,), (0,)), ((), ()))

ORDER = (0, 1, 3, 2)


def dot(a, b, dims):
    return lax.dot_general(a, b, dims, preferred_element_type=F32)


def slot_of(v, z):
    return (ORDER[v // 2] ^ z) * 2 + v % 2


def level_kernel(config, *refs):
    refs = list(refs)
    take = lambda n: [refs.pop(0) for _ in range(n)]
    rows, fanout = config["rows"], config["fanout"]
    level, down, up = config["level"], config["down"], config["up"]
    linked = level > 0
    last = fanout if linked else 0
    z = lax.axis_index("rhs")
    place = take(1)[0] if linked else None
    tiles = take(max(spec[0] for spec in config["tiles"]) + 1)
    tiles = [(tiles[ref], at, skip) for ref, at, skip in config["tiles"]]
    if down:
        mine, other = take(2)
        solved = take(1)[0] if linked else None
    else:
        stored, incoming = take(2)
    out_f = take(1)[0] if not up else None
    if up:
        result_mine, result_other = take(2)
        keep, sent = take(2) if linked else (None, None)
    right = take(1)[0] if down else None
    total = take(1)[0] if up and linked else None

    def tile(v, k):
        ref, at, skip = tiles[v // 2]
        return ref[v % 2, skip + k] if at is None else ref[at, v % 2, skip + k]

    def wide(v):
        return jnp.concatenate([tile(v, k) for k in range(fanout)], axis=1)

    def places(v):
        base = ((level - 1) * rows + slot_of(v, z)) * fanout
        return [place[base + k] for k in range(fanout)]

    if total is not None:
        total[...] = jnp.zeros_like(total)
    if down:
        columns = mine.shape[0]
        for s in range(rows):
            right[s, :columns] = mine[:, level, s, :]
            right[s, columns:] = other[:, level, s, :]
        values = []
        for v in range(rows):
            current = right[slot_of(v, z)]
            if linked:
                picked = jnp.concatenate([solved[at] for at in places(v)], axis=1)
                current = current - dot(picked, wide(v), NT)
            values.append(current.astype(BF16))
        values = [dot(values[v], tile(v, last), NT).astype(BF16) for v in range(rows)]
        if not up:
            for v in range(rows):
                out_f[v] = values[v]
            return
    else:
        values = []
        for v in range(rows):
            values.append((stored[v].astype(F32) - incoming[v]).astype(BF16))
    answers = [dot(values[v], tile(v, last), NN) for v in range(rows)]
    columns = result_mine.shape[1]
    for v in range(rows):
        result_mine[slot_of(v, z)] = answers[v][:columns]
        result_other[slot_of(v, z)] = answers[v][columns:].astype(result_other.dtype)
    if not linked:
        return
    size = answers[0].shape[1]
    for v in range(rows):
        terms = dot(answers[v].astype(BF16), wide(v), NN)
        for k, at in enumerate(places(v)):
            total[at] += terms[:, k * size : (k + 1) * size]
    middle = total.shape[0] // 2
    keep[...] = total[:middle]
    sent[...] = total[middle:].astype(BF16)


def finish_kernel(spans, *refs):
    z = lax.axis_index("rhs")
    inner = (z == 1) | (z == 2)
    refs, out = list(refs[:-1]), refs[-1]
    for span in spans:
        home = refs.pop(0)
        for i, level in enumerate(span):
            mine = refs.pop(0)
            for s in range(mine.shape[0]):
                out[:, level, s, :] = jnp.where(inner, mine[s], home[i, s].astype(F32))


VMEM = pl.BlockSpec(memory_space=pltpu.VMEM)
SMEM = pl.BlockSpec(memory_space=pltpu.SMEM)


def params():
    return pltpu.CompilerParams(vmem_limit_bytes=32 * 1024 * 1024)


def on_device(right_side, diag_tiles, off_tiles, src_part, src_slot):
    columns, levels, rows, size = right_side.shape
    fanout = src_part.shape[2]
    nodes = lax.axis_size("node")
    chips = nodes // 2
    node, z = lax.axis_index("node"), lax.axis_index("rhs")

    def inward(x):
        return lax.ppermute(x, "rhs", [(0, 1), (3, 2)])

    def outward(x):
        return lax.ppermute(x, "rhs", [(1, 0), (2, 3)])

    def between(x):
        return lax.ppermute(x, "rhs", [(1, 2), (2, 1)])

    def shift(x, d):
        return lax.ppermute(x, "node", [(n, n ^ d) for n in range(nodes)])

    def after(x, *others):
        return lax.optimization_barrier((x, *others))[0]

    held, where = {}, {}

    def hold(level, arrays, places):
        held[level], where[level] = arrays, places

    pieces = [diag_tiles[0][:, None]] + [
        jnp.concatenate([off_tiles[level - 1], diag_tiles[level][:, None]], axis=1)
        for level in range(1, levels)
    ]
    rel = src_part ^ node
    pair = (src_slot >> 1) ^ z
    inner = (pair ^ (pair >> 1)) * 2 + (src_slot & 1)
    place = (((rel >> 1) + (rel & 1) * chips) * rows + inner).reshape(-1)

    near, both = {}, {}

    def join(level, *others):
        block, at = near[level]
        pair = jnp.stack([pieces[level], block if at is None else block[at]])
        both[level] = between(after(pair, *others))
        places = [(0, None, 0), (1, at, 0), (2, 0, 0), (2, 1, 0)]
        hold(level, [pieces[level], block, both[level]], places)

    facing = between(jnp.concatenate(pieces[:2], axis=1))
    other_right = inward(right_side)
    near[0] = inward(pieces[0]), None
    lower = inward(after(jnp.stack(pieces[1:3]), near[0][0], other_right))
    near[1], near[2] = (lower, 0), (lower, 1)
    def meet(level, *others):
        block, at = near[level]
        corner = between(after(block if at is None else block[at], *others))
        places = [(0, None, 0), (1, at, 0), (2, None, level % 2), (3, None, 0)]
        hold(level, [pieces[level], block, facing if level < 2 else second, corner], places)
        return corner

    upper = inward(after(jnp.stack(pieces[3:]), meet(0)))
    for level in range(3, levels):
        near[level] = upper, level - 3
    second = between(after(pieces[2], facing))

    vec = (rows, 2 * columns, size)
    own = (rows, columns, size)

    def run(level, down, up, inputs):
        linked = level > 0
        config = dict(
            rows=rows,
            fanout=fanout,
            level=level,
            down=down,
            up=up,
            tiles=where[level],
        )
        args = ([place] if linked else []) + list(held[level]) + list(inputs)
        shapes, scratch = [], []
        if down:
            scratch.append(pltpu.VMEM(vec, F32))
        if not up:
            shapes.append(jax.ShapeDtypeStruct(vec, BF16))
        else:
            shapes += [jax.ShapeDtypeStruct(own, t) for t in (F32, BF16)]
            if linked:
                shapes += [jax.ShapeDtypeStruct((chips * rows,) + vec[1:], t) for t in (F32, BF16)]
                scratch.append(pltpu.VMEM((nodes * rows,) + vec[1:], F32))
        dots = rows * ((fanout if linked else 0) + 1) * (int(down) + int(up))
        return pl.pallas_call(
            functools.partial(level_kernel, config),
            in_specs=([SMEM] if linked else []) + [VMEM] * (len(args) - int(linked)),
            out_specs=[VMEM] * len(shapes),
            out_shape=shapes,
            scratch_shapes=scratch,
            compiler_params=params(),
            cost_estimate=pl.CostEstimate(
                flops=4 * dots * columns * size * size,
                bytes_accessed=dots * size * size * 2,
                transcendentals=0,
            ),
        )(*args)

    def gather(value, *early):
        met = jnp.concatenate([value] + [shift(value, 2 * d) for d in range(1, chips)])
        core = after(met, *early)
        return jnp.concatenate([core, shift(core, 1)])

    def scatter(keep, sent):
        summed = keep + shift(sent, 1).astype(F32)
        parts = [summed[d * rows : (d + 1) * rows] for d in range(chips)]
        incoming = parts[0]
        for d in range(chips - 1, 0, -1):
            incoming = incoming + shift(parts[d].astype(BF16), 2 * d).astype(F32)
        return incoming

    stored = []
    inputs = [right_side, other_right]
    for level in range(levels - 1):
        (value,) = run(level, True, False, inputs)
        stored.append(value)
        if level == 0:
            early = [meet(1, value), place]
        else:
            early = [both[level + 1] if level > 1 else meet(2, stored[0])]
        if level == 1:
            early.append(second)
        gathered = gather(value, *early)
        if level < 2:
            join(level + 3, gathered)
        if level == 0:
            gathered = after(gathered, upper)
        inputs = [right_side, other_right, gathered]
    mine, others = [None] * levels, [None] * levels
    mine[-1], others[-1], *sums = run(levels - 1, True, True, inputs)
    for level in range(levels - 2, -1, -1):
        outs = run(level, False, True, [stored[level], scatter(*sums)])
        mine[level], others[level], *sums = outs
    spans = [list(range(levels - 1, 0, -1)), [0]]
    args = []
    for span in spans:
        args += [outward(jnp.stack([others[x] for x in span]))] + [mine[x] for x in span]
    return pl.pallas_call(
        functools.partial(finish_kernel, spans),
        in_specs=[VMEM] * len(args),
        out_specs=VMEM,
        out_shape=jax.ShapeDtypeStruct(right_side.shape, F32),
        compiler_params=params(),
    )(*args)


def solution(mesh):
    placed = (
        P("rhs", None, "node", None),
        P(None, ("node", "rhs"), None, None),
        P(None, ("node", "rhs"), None, None, None),
        P(None, "node", None),
        P(None, "node", None),
    )
    return jax.shard_map(
        on_device,
        mesh=mesh,
        in_specs=placed,
        out_specs=P("rhs", None, "node", None),
        check_vma=False,
    )
```

```python
import functools

import jax
import jax.numpy as jnp
from jax import lax
from jax.experimental import pallas as pl
from jax.experimental.pallas import tpu as pltpu
from jax.sharding import PartitionSpec as P

F32 = jnp.float32
BF16 = jnp.bfloat16
NT = (((1,), (1,)), ((), ()))
NN = (((1,), (0,)), ((), ()))

ORDER = (0, 1, 3, 2)


def dot(a, b, dims):
    return lax.dot_general(a, b, dims, preferred_element_type=F32)


def slot_of(v, z):
    return (ORDER[v // 2] ^ z) * 2 + v % 2


def level_kernel(config, *refs):
    refs = list(refs)
    take = lambda n: [refs.pop(0) for _ in range(n)]
    rows, fanout = config["rows"], config["fanout"]
    level, down, up = config["level"], config["down"], config["up"]
    linked = level > 0
    last = fanout if linked else 0
    z = lax.axis_index("rhs")
    place = take(1)[0] if linked else None
    tiles = take(max(spec[0] for spec in config["tiles"]) + 1)
    tiles = [(tiles[ref], at, skip) for ref, at, skip in config["tiles"]]
    if down:
        mine, other = take(2)
        solved = take(1)[0] if linked else None
    else:
        stored, incoming = take(2)
    out_f = take(1)[0] if not up else None
    if up:
        result_mine, result_other = take(2)
        keep, sent = take(2) if linked else (None, None)
    right = take(1)[0] if down else None
    total = take(1)[0] if up and linked else None

    def tile(v, k):
        ref, at, skip = tiles[v // 2]
        return ref[v % 2, skip + k] if at is None else ref[at, v % 2, skip + k]

    def wide(v):
        return jnp.concatenate([tile(v, k) for k in range(fanout)], axis=1)

    def places(v):
        base = ((level - 1) * rows + slot_of(v, z)) * fanout
        return [place[base + k] for k in range(fanout)]

    if total is not None:
        total[...] = jnp.zeros_like(total)
    if down:
        columns = mine.shape[0]
        for s in range(rows):
            right[s, :columns] = mine[:, level, s, :]
            right[s, columns:] = other[:, level, s, :]
        values = []
        for v in range(rows):
            current = right[slot_of(v, z)]
            if linked:
                picked = jnp.concatenate([solved[at] for at in places(v)], axis=1)
                current = current - dot(picked, wide(v), NT)
            values.append(current.astype(BF16))
        values = [dot(values[v], tile(v, last), NT).astype(BF16) for v in range(rows)]
        if not up:
            for v in range(rows):
                out_f[v] = values[v]
            return
    else:
        values = []
        for v in range(rows):
            values.append((stored[v].astype(F32) - incoming[v]).astype(BF16))
    answers = [dot(values[v], tile(v, last), NN) for v in range(rows)]
    columns = result_mine.shape[1]
    for v in range(rows):
        result_mine[slot_of(v, z)] = answers[v][:columns]
        result_other[slot_of(v, z)] = answers[v][columns:].astype(result_other.dtype)
    if not linked:
        return
    size = answers[0].shape[1]
    for v in range(rows):
        terms = dot(answers[v].astype(BF16), wide(v), NN)
        for k, at in enumerate(places(v)):
            total[at] += terms[:, k * size : (k + 1) * size]
    middle = total.shape[0] // 2
    keep[...] = total[:middle]
    sent[...] = total[middle:].astype(BF16)


def finish_kernel(spans, *refs):
    z = lax.axis_index("rhs")
    inner = (z == 1) | (z == 2)
    refs, out = list(refs[:-1]), refs[-1]
    for span in spans:
        home = refs.pop(0)
        for i, level in enumerate(span):
            mine = refs.pop(0)
            for s in range(mine.shape[0]):
                out[:, level, s, :] = jnp.where(inner, mine[s], home[i, s].astype(F32))


VMEM = pl.BlockSpec(memory_space=pltpu.VMEM)
SMEM = pl.BlockSpec(memory_space=pltpu.SMEM)


def params():
    return pltpu.CompilerParams(vmem_limit_bytes=32 * 1024 * 1024)


def on_device(right_side, diag_tiles, off_tiles, src_part, src_slot):
    columns, levels, rows, size = right_side.shape
    fanout = src_part.shape[2]
    nodes = lax.axis_size("node")
    chips = nodes // 2
    node, z = lax.axis_index("node"), lax.axis_index("rhs")

    def inward(x):
        return lax.ppermute(x, "rhs", [(0, 1), (3, 2)])

    def outward(x):
        return lax.ppermute(x, "rhs", [(1, 0), (2, 3)])

    def between(x):
        return lax.ppermute(x, "rhs", [(1, 2), (2, 1)])

    def shift(x, d):
        return lax.ppermute(x, "node", [(n, n ^ d) for n in range(nodes)])

    def after(x, *others):
        return lax.optimization_barrier((x, *others))[0]

    held, where = {}, {}

    def hold(level, arrays, places):
        held[level], where[level] = arrays, places

    pieces = [diag_tiles[0][:, None]] + [
        jnp.concatenate([off_tiles[level - 1], diag_tiles[level][:, None]], axis=1)
        for level in range(1, levels)
    ]
    rel = src_part ^ node
    pair = (src_slot >> 1) ^ z
    inner = (pair ^ (pair >> 1)) * 2 + (src_slot & 1)
    place = (((rel >> 1) + (rel & 1) * chips) * rows + inner).reshape(-1)

    near, both = {}, {}

    def join(level, *others):
        block, at = near[level]
        pair = jnp.stack([pieces[level], block if at is None else block[at]])
        both[level] = between(after(pair, *others))
        places = [(0, None, 0), (1, at, 0), (2, 0, 0), (2, 1, 0)]
        hold(level, [pieces[level], block, both[level]], places)

    facing = between(jnp.concatenate(pieces[:2], axis=1))
    other_right = inward(right_side)
    near[0] = inward(pieces[0]), None
    near[1] = inward(pieces[1]), None
    middle = inward(after(jnp.stack(pieces[2:4]), near[0][0]))
    near[2], near[3] = (middle, 0), (middle, 1)

    def meet(level, *others):
        block, at = near[level]
        corner = between(after(block if at is None else block[at], *others))
        places = [(0, None, 0), (1, at, 0), (2, None, level % 2), (3, None, 0)]
        hold(level, [pieces[level], block, facing if level < 2 else second, corner], places)
        return corner

    meet(0)
    second = between(after(pieces[2], facing))

    vec = (rows, 2 * columns, size)
    own = (rows, columns, size)

    def run(level, down, up, inputs):
        linked = level > 0
        config = dict(
            rows=rows,
            fanout=fanout,
            level=level,
            down=down,
            up=up,
            tiles=where[level],
        )
        args = ([place] if linked else []) + list(held[level]) + list(inputs)
        shapes, scratch = [], []
        if down:
            scratch.append(pltpu.VMEM(vec, F32))
        if not up:
            shapes.append(jax.ShapeDtypeStruct(vec, BF16))
        else:
            shapes += [jax.ShapeDtypeStruct(own, t) for t in (F32, BF16)]
            if linked:
                shapes += [jax.ShapeDtypeStruct((chips * rows,) + vec[1:], t) for t in (F32, BF16)]
                scratch.append(pltpu.VMEM((nodes * rows,) + vec[1:], F32))
        dots = rows * ((fanout if linked else 0) + 1) * (int(down) + int(up))
        return pl.pallas_call(
            functools.partial(level_kernel, config),
            in_specs=([SMEM] if linked else []) + [VMEM] * (len(args) - int(linked)),
            out_specs=[VMEM] * len(shapes),
            out_shape=shapes,
            scratch_shapes=scratch,
            compiler_params=params(),
            cost_estimate=pl.CostEstimate(
                flops=4 * dots * columns * size * size,
                bytes_accessed=dots * size * size * 2,
                transcendentals=0,
            ),
        )(*args)

    def gather(value, *early):
        met = jnp.concatenate([value] + [shift(value, 2 * d) for d in range(1, chips)])
        core = after(met, *early)
        return jnp.concatenate([core, shift(core, 1)])

    def scatter(keep, sent):
        summed = keep + shift(sent, 1).astype(F32)
        parts = [summed[d * rows : (d + 1) * rows] for d in range(chips)]
        incoming = parts[0]
        for d in range(chips - 1, 0, -1):
            incoming = incoming + shift(parts[d].astype(BF16), 2 * d).astype(F32)
        return incoming

    stored = []
    inputs = [right_side, other_right]
    for level in range(levels - 1):
        (value,) = run(level, True, False, inputs)
        stored.append(value)
        if level == 0:
            near[4] = inward(after(pieces[4], value)), None
            early = [meet(1, value), middle]
        elif level == 1:
            early = [meet(2, stored[0]), second]
        else:
            early = [both[level + 1]]
        gathered = gather(value, *early)
        if level < 2:
            join(level + 3, gathered)
        if level == 0:
            gathered = after(gathered, near[4][0])
        inputs = [right_side, other_right, gathered]
    mine, others = [None] * levels, [None] * levels
    mine[-1], others[-1], *sums = run(levels - 1, True, True, inputs)
    for level in range(levels - 2, -1, -1):
        outs = run(level, False, True, [stored[level], scatter(*sums)])
        mine[level], others[level], *sums = outs
    spans = [list(range(levels - 1, 0, -1)), [0]]
    args = []
    for span in spans:
        args += [outward(jnp.stack([others[x] for x in span]))] + [mine[x] for x in span]
    return pl.pallas_call(
        functools.partial(finish_kernel, spans),
        in_specs=[VMEM] * len(args),
        out_specs=VMEM,
        out_shape=jax.ShapeDtypeStruct(right_side.shape, F32),
        compiler_params=params(),
    )(*args)


def solution(mesh):
    placed = (
        P("rhs", None, "node", None),
        P(None, ("node", "rhs"), None, None),
        P(None, ("node", "rhs"), None, None, None),
        P(None, "node", None),
        P(None, "node", None),
    )
    return jax.shard_map(
        on_device,
        mesh=mesh,
        in_specs=placed,
        out_specs=P("rhs", None, "node", None),
        check_vma=False,
    )
```

```python
import functools

import jax
import jax.numpy as jnp
from jax import lax
from jax.experimental import pallas as pl
from jax.experimental.pallas import tpu as pltpu
from jax.sharding import PartitionSpec as P

F32 = jnp.float32
BF16 = jnp.bfloat16
NT = (((1,), (1,)), ((), ()))
NN = (((1,), (0,)), ((), ()))

ORDER = (0, 1, 3, 2)


def dot(a, b, dims):
    return lax.dot_general(a, b, dims, preferred_element_type=F32)


def slot_of(v, z):
    return (ORDER[v // 2] ^ z) * 2 + v % 2


def level_kernel(config, *refs):
    refs = list(refs)
    take = lambda n: [refs.pop(0) for _ in range(n)]
    rows, fanout = config["rows"], config["fanout"]
    level, down, up = config["level"], config["down"], config["up"]
    linked = level > 0
    last = fanout if linked else 0
    z = lax.axis_index("rhs")
    place = take(1)[0] if linked else None
    tiles = take(max(spec[0] for spec in config["tiles"]) + 1)
    tiles = [(tiles[ref], at, skip) for ref, at, skip in config["tiles"]]
    if down:
        mine, other = take(2)
        solved = take(1)[0] if linked else None
    else:
        stored, incoming = take(2)
    out_f = take(1)[0] if not up else None
    if up:
        result_mine, result_other = take(2)
        keep, sent = take(2) if linked else (None, None)
    right = take(1)[0] if down else None
    total = take(1)[0] if up and linked else None

    def tile(v, k):
        ref, at, skip = tiles[v // 2]
        return ref[v % 2, skip + k] if at is None else ref[at, v % 2, skip + k]

    def wide(v):
        return jnp.concatenate([tile(v, k) for k in range(fanout)], axis=1)

    def places(v):
        base = ((level - 1) * rows + slot_of(v, z)) * fanout
        return [place[base + k] for k in range(fanout)]

    if total is not None:
        total[...] = jnp.zeros_like(total)
    if down:
        columns = mine.shape[0]
        for s in range(rows):
            right[s, :columns] = mine[:, level, s, :]
            right[s, columns:] = other[:, level, s, :]
        values = []
        for v in range(rows):
            current = right[slot_of(v, z)]
            if linked:
                picked = jnp.concatenate([solved[at] for at in places(v)], axis=1)
                current = current - dot(picked, wide(v), NT)
            values.append(current.astype(BF16))
        values = [dot(values[v], tile(v, last), NT).astype(BF16) for v in range(rows)]
        if not up:
            for v in range(rows):
                out_f[v] = values[v]
            return
    else:
        values = []
        for v in range(rows):
            values.append((stored[v].astype(F32) - incoming[v]).astype(BF16))
    answers = [dot(values[v], tile(v, last), NN) for v in range(rows)]
    columns = result_mine.shape[1]
    for v in range(rows):
        result_mine[slot_of(v, z)] = answers[v][:columns]
        result_other[slot_of(v, z)] = answers[v][columns:].astype(result_other.dtype)
    if not linked:
        return
    size = answers[0].shape[1]
    for v in range(rows):
        terms = dot(answers[v].astype(BF16), wide(v), NN)
        for k, at in enumerate(places(v)):
            total[at] += terms[:, k * size : (k + 1) * size]
    middle = total.shape[0] // 2
    keep[...] = total[:middle]
    sent[...] = total[middle:].astype(BF16)


def finish_kernel(spans, *refs):
    z = lax.axis_index("rhs")
    inner = (z == 1) | (z == 2)
    refs, out = list(refs[:-1]), refs[-1]
    for span in spans:
        home = refs.pop(0)
        for i, level in enumerate(span):
            mine = refs.pop(0)
            for s in range(mine.shape[0]):
                out[:, level, s, :] = jnp.where(inner, mine[s], home[i, s].astype(F32))


VMEM = pl.BlockSpec(memory_space=pltpu.VMEM)
SMEM = pl.BlockSpec(memory_space=pltpu.SMEM)


def params():
    return pltpu.CompilerParams(vmem_limit_bytes=32 * 1024 * 1024)


def on_device(right_side, diag_tiles, off_tiles, src_part, src_slot):
    columns, levels, rows, size = right_side.shape
    fanout = src_part.shape[2]
    nodes = lax.axis_size("node")
    chips = nodes // 2
    node, z = lax.axis_index("node"), lax.axis_index("rhs")

    def inward(x):
        return lax.ppermute(x, "rhs", [(0, 1), (3, 2)])

    def outward(x):
        return lax.ppermute(x, "rhs", [(1, 0), (2, 3)])

    def between(x):
        return lax.ppermute(x, "rhs", [(1, 2), (2, 1)])

    def shift(x, d):
        return lax.ppermute(x, "node", [(n, n ^ d) for n in range(nodes)])

    def after(x, *others):
        return lax.optimization_barrier((x, *others))[0]

    held, where = {}, {}

    def hold(level, arrays, places):
        held[level], where[level] = arrays, places

    pieces = [diag_tiles[0][:, None]] + [
        jnp.concatenate([off_tiles[level - 1], diag_tiles[level][:, None]], axis=1)
        for level in range(1, levels)
    ]
    def index_table(part):
        rel = part ^ node
        pair = (src_slot >> 1) ^ z
        inner = (pair ^ (pair >> 1)) * 2 + (src_slot & 1)
        return (((rel >> 1) + (rel & 1) * chips) * rows + inner).reshape(-1)

    near, both = {}, {}

    def join(level, *others):
        block, at = near[level]
        pair = jnp.stack([pieces[level], block if at is None else block[at]])
        both[level] = between(after(pair, *others))
        places = [(0, None, 0), (1, at, 0), (2, 0, 0), (2, 1, 0)]
        hold(level, [pieces[level], block, both[level]], places)

    facing = between(jnp.concatenate(pieces[:2], axis=1))
    other_right = inward(right_side)
    near[0] = inward(pieces[0]), None
    near[1] = inward(pieces[1]), None
    middle = inward(after(jnp.stack(pieces[2:4]), near[0][0]))
    near[2], near[3] = (middle, 0), (middle, 1)

    def meet(level, *others):
        block, at = near[level]
        corner = between(after(block if at is None else block[at], *others))
        places = [(0, None, 0), (1, at, 0), (2, None, level % 2), (3, None, 0)]
        hold(level, [pieces[level], block, facing if level < 2 else second, corner], places)
        return corner

    meet(0)
    second = between(after(pieces[2], facing))

    vec = (rows, 2 * columns, size)
    own = (rows, columns, size)

    def run(level, down, up, inputs, table=None):
        linked = level > 0
        config = dict(
            rows=rows,
            fanout=fanout,
            level=level,
            down=down,
            up=up,
            tiles=where[level],
        )
        args = ([table] if linked else []) + list(held[level]) + list(inputs)
        shapes, scratch = [], []
        if down:
            scratch.append(pltpu.VMEM(vec, F32))
        if not up:
            shapes.append(jax.ShapeDtypeStruct(vec, BF16))
        else:
            shapes += [jax.ShapeDtypeStruct(own, t) for t in (F32, BF16)]
            if linked:
                shapes += [jax.ShapeDtypeStruct((chips * rows,) + vec[1:], t) for t in (F32, BF16)]
                scratch.append(pltpu.VMEM((nodes * rows,) + vec[1:], F32))
        dots = rows * ((fanout if linked else 0) + 1) * (int(down) + int(up))
        return pl.pallas_call(
            functools.partial(level_kernel, config),
            in_specs=([SMEM] if linked else []) + [VMEM] * (len(args) - int(linked)),
            out_specs=[VMEM] * len(shapes),
            out_shape=shapes,
            scratch_shapes=scratch,
            compiler_params=params(),
            cost_estimate=pl.CostEstimate(
                flops=4 * dots * columns * size * size,
                bytes_accessed=dots * size * size * 2,
                transcendentals=0,
            ),
        )(*args)

    def gather(value, *early):
        met = jnp.concatenate([value] + [shift(value, 2 * d) for d in range(1, chips)])
        core = after(met, *early)
        return met, jnp.concatenate([core, shift(core, 1)])

    def scatter(keep, sent):
        summed = keep + shift(sent, 1).astype(F32)
        parts = [summed[d * rows : (d + 1) * rows] for d in range(chips)]
        incoming = parts[0]
        for d in range(chips - 1, 0, -1):
            incoming = incoming + shift(parts[d].astype(BF16), 2 * d).astype(F32)
        return incoming

    stored = []
    inputs, table = [right_side, other_right], None
    for level in range(levels - 1):
        (value,) = run(level, True, False, inputs, table)
        stored.append(value)
        if level == 0:
            near[4] = inward(after(pieces[4], value)), None
            early = [meet(1, value), middle]
        elif level == 1:
            early = [meet(2, stored[0])]
        else:
            early = [both[level + 1]]
        met, gathered = gather(value, *early)
        if level == 0:
            table = index_table(after(src_part, met))
        if level < 2:
            join(level + 3, gathered)
        if level == 0:
            gathered = after(gathered, near[4][0], second)
        inputs = [right_side, other_right, gathered]
    mine, others = [None] * levels, [None] * levels
    mine[-1], others[-1], *sums = run(levels - 1, True, True, inputs, table)
    for level in range(levels - 2, -1, -1):
        outs = run(level, False, True, [stored[level], scatter(*sums)], table)
        mine[level], others[level], *sums = outs
    spans = [list(range(levels - 1, 0, -1)), [0]]
    args = []
    for span in spans:
        args += [outward(jnp.stack([others[x] for x in span]))] + [mine[x] for x in span]
    return pl.pallas_call(
        functools.partial(finish_kernel, spans),
        in_specs=[VMEM] * len(args),
        out_specs=VMEM,
        out_shape=jax.ShapeDtypeStruct(right_side.shape, F32),
        compiler_params=params(),
    )(*args)


def solution(mesh):
    placed = (
        P("rhs", None, "node", None),
        P(None, ("node", "rhs"), None, None),
        P(None, ("node", "rhs"), None, None, None),
        P(None, "node", None),
        P(None, "node", None),
    )
    return jax.shard_map(
        on_device,
        mesh=mesh,
        in_specs=placed,
        out_specs=P("rhs", None, "node", None),
        check_vma=False,
    )
```

```python
import functools

import jax
import jax.numpy as jnp
from jax import lax
from jax.experimental import pallas as pl
from jax.experimental.pallas import tpu as pltpu
from jax.sharding import PartitionSpec as P

F32 = jnp.float32
BF16 = jnp.bfloat16
NT = (((1,), (1,)), ((), ()))
NN = (((1,), (0,)), ((), ()))

ORDER = (0, 1, 3, 2)


def dot(a, b, dims):
    return lax.dot_general(a, b, dims, preferred_element_type=F32)


def slot_of(v, z):
    return (ORDER[v // 2] ^ z) * 2 + v % 2


def level_kernel(config, *refs):
    refs = list(refs)
    take = lambda n: [refs.pop(0) for _ in range(n)]
    rows, fanout = config["rows"], config["fanout"]
    level, down, up = config["level"], config["down"], config["up"]
    linked = level > 0
    last = fanout if linked else 0
    z = lax.axis_index("rhs")
    place = take(1)[0] if linked else None
    tiles = take(max(spec[0] for spec in config["tiles"]) + 1)
    tiles = [(tiles[ref], at, skip) for ref, at, skip in config["tiles"]]
    if down:
        mine, other = take(2)
        solved = take(1)[0] if linked else None
    else:
        stored, incoming = take(2)
    out_f = take(1)[0] if not up else None
    if up:
        result_mine, result_other = take(2)
        keep, sent = take(2) if linked else (None, None)
    right = take(1)[0] if down else None
    total = take(1)[0] if up and linked else None

    def tile(v, k):
        ref, at, skip = tiles[v // 2]
        return ref[v % 2, skip + k] if at is None else ref[at, v % 2, skip + k]

    def wide(v):
        return jnp.concatenate([tile(v, k) for k in range(fanout)], axis=1)

    def places(v):
        base = ((level - 1) * rows + slot_of(v, z)) * fanout
        return [place[base + k] for k in range(fanout)]

    if total is not None:
        total[...] = jnp.zeros_like(total)
    if down:
        columns = mine.shape[0]
        for s in range(rows):
            right[s, :columns] = mine[:, level, s, :]
            right[s, columns:] = other[:, level, s, :]
        values = []
        for v in range(rows):
            current = right[slot_of(v, z)]
            if linked:
                picked = jnp.concatenate([solved[at] for at in places(v)], axis=1)
                current = current - dot(picked, wide(v), NT)
            values.append(current.astype(BF16))
        values = [dot(values[v], tile(v, last), NT).astype(BF16) for v in range(rows)]
        if not up:
            for v in range(rows):
                out_f[v] = values[v]
            return
    else:
        values = []
        for v in range(rows):
            values.append((stored[v].astype(F32) - incoming[v]).astype(BF16))
    answers = [dot(values[v], tile(v, last), NN) for v in range(rows)]
    columns = result_mine.shape[1]
    for v in range(rows):
        result_mine[slot_of(v, z)] = answers[v][:columns]
        result_other[slot_of(v, z)] = answers[v][columns:].astype(result_other.dtype)
    if not linked:
        return
    size = answers[0].shape[1]
    for v in range(rows):
        terms = dot(answers[v].astype(BF16), wide(v), NN)
        for k, at in enumerate(places(v)):
            total[at] += terms[:, k * size : (k + 1) * size]
    middle = total.shape[0] // 2
    keep[...] = total[:middle]
    sent[...] = total[middle:].astype(BF16)


def finish_kernel(spans, *refs):
    z = lax.axis_index("rhs")
    inner = (z == 1) | (z == 2)
    refs, out = list(refs[:-1]), refs[-1]
    for span in spans:
        home = refs.pop(0)
        for i, level in enumerate(span):
            mine = refs.pop(0)
            for s in range(mine.shape[0]):
                out[:, level, s, :] = jnp.where(inner, mine[s], home[i, s].astype(F32))


VMEM = pl.BlockSpec(memory_space=pltpu.VMEM)
SMEM = pl.BlockSpec(memory_space=pltpu.SMEM)


def params():
    return pltpu.CompilerParams(vmem_limit_bytes=32 * 1024 * 1024)


def on_device(right_side, diag_tiles, off_tiles, src_part, src_slot):
    columns, levels, rows, size = right_side.shape
    fanout = src_part.shape[2]
    nodes = lax.axis_size("node")
    chips = nodes // 2
    node, z = lax.axis_index("node"), lax.axis_index("rhs")

    def inward(x):
        return lax.ppermute(x, "rhs", [(0, 1), (3, 2)])

    def outward(x):
        return lax.ppermute(x, "rhs", [(1, 0), (2, 3)])

    def between(x):
        return lax.ppermute(x, "rhs", [(1, 2), (2, 1)])

    def shift(x, d):
        return lax.ppermute(x, "node", [(n, n ^ d) for n in range(nodes)])

    def after(x, *others):
        return lax.optimization_barrier((x, *others))[0]

    held, where = {}, {}

    def hold(level, arrays, places):
        held[level], where[level] = arrays, places

    pieces = [diag_tiles[0][:, None]] + [
        jnp.concatenate([off_tiles[level - 1], diag_tiles[level][:, None]], axis=1)
        for level in range(1, levels)
    ]
    rel = src_part ^ node
    pair = (src_slot >> 1) ^ z
    inner = (pair ^ (pair >> 1)) * 2 + (src_slot & 1)
    place = (((rel >> 1) + (rel & 1) * chips) * rows + inner).reshape(-1)

    near, both = {}, {}

    def join(level, *others):
        block, at = near[level]
        pair = jnp.stack([pieces[level], block if at is None else block[at]])
        both[level] = between(after(pair, *others))
        places = [(0, None, 0), (1, at, 0), (2, 0, 0), (2, 1, 0)]
        hold(level, [pieces[level], block, both[level]], places)

    facing = between(jnp.concatenate(pieces[:2], axis=1))
    other_right = inward(right_side)
    near[0] = inward(pieces[0]), None
    near[1] = inward(pieces[1]), None
    middle = inward(after(jnp.stack(pieces[2:4]), near[0][0]))
    near[2], near[3] = (middle, 0), (middle, 1)

    def meet(level, *others):
        block, at = near[level]
        corner = between(after(block if at is None else block[at], *others))
        places = [(0, None, 0), (1, at, 0), (2, None, level % 2), (3, None, 0)]
        hold(level, [pieces[level], block, facing if level < 2 else second, corner], places)
        return corner

    meet(0)
    second = between(after(pieces[2], facing))

    vec = (rows, 2 * columns, size)
    own = (rows, columns, size)

    def run(level, down, up, inputs):
        linked = level > 0
        config = dict(
            rows=rows,
            fanout=fanout,
            level=level,
            down=down,
            up=up,
            tiles=where[level],
        )
        args = ([place] if linked else []) + list(held[level]) + list(inputs)
        shapes, scratch = [], []
        if down:
            scratch.append(pltpu.VMEM(vec, F32))
        if not up:
            shapes.append(jax.ShapeDtypeStruct(vec, BF16))
        else:
            shapes += [jax.ShapeDtypeStruct(own, t) for t in (F32, BF16)]
            if linked:
                shapes += [jax.ShapeDtypeStruct((chips * rows,) + vec[1:], t) for t in (F32, BF16)]
                scratch.append(pltpu.VMEM((nodes * rows,) + vec[1:], F32))
        dots = rows * ((fanout if linked else 0) + 1) * (int(down) + int(up))
        return pl.pallas_call(
            functools.partial(level_kernel, config),
            in_specs=([SMEM] if linked else []) + [VMEM] * (len(args) - int(linked)),
            out_specs=[VMEM] * len(shapes),
            out_shape=shapes,
            scratch_shapes=scratch,
            compiler_params=params(),
            cost_estimate=pl.CostEstimate(
                flops=4 * dots * columns * size * size,
                bytes_accessed=dots * size * size * 2,
                transcendentals=0,
            ),
        )(*args)

    def gather(value, *early):
        met = jnp.concatenate([value] + [shift(value, 2 * d) for d in range(1, chips)])
        core = after(met, *early)
        return jnp.concatenate([core, shift(core, 1)])

    def scatter(keep, sent):
        summed = keep + shift(sent, 1).astype(F32)
        parts = [summed[d * rows : (d + 1) * rows] for d in range(chips)]
        incoming = parts[0]
        for d in range(chips - 1, 0, -1):
            incoming = incoming + shift(parts[d].astype(BF16), 2 * d).astype(F32)
        return incoming

    stored = []
    inputs = [right_side, other_right]
    for level in range(levels - 1):
        (value,) = run(level, True, False, inputs)
        stored.append(value)
        if level == 0:
            near[4] = inward(after(pieces[4], value)), None
            early = [meet(1, value), middle]
        elif level == 1:
            early = [meet(2, stored[0])]
        else:
            early = [both[level + 1]]
        gathered = gather(value, *early)
        if level < 2:
            join(level + 3, gathered)
        if level == 0:
            gathered = after(gathered, near[4][0], second)
        inputs = [right_side, other_right, gathered]
    mine, others = [None] * levels, [None] * levels
    mine[-1], others[-1], *sums = run(levels - 1, True, True, inputs)
    for level in range(levels - 2, -1, -1):
        outs = run(level, False, True, [stored[level], scatter(*sums)])
        mine[level], others[level], *sums = outs
    spans = [list(range(levels - 1, 0, -1)), [0]]
    args = []
    for span in spans:
        args += [outward(jnp.stack([others[x] for x in span]))] + [mine[x] for x in span]
    return pl.pallas_call(
        functools.partial(finish_kernel, spans),
        in_specs=[VMEM] * len(args),
        out_specs=VMEM,
        out_shape=jax.ShapeDtypeStruct(right_side.shape, F32),
        compiler_params=params(),
    )(*args)


def solution(mesh):
    placed = (
        P("rhs", None, "node", None),
        P(None, ("node", "rhs"), None, None),
        P(None, ("node", "rhs"), None, None, None),
        P(None, "node", None),
        P(None, "node", None),
    )
    return jax.shard_map(
        on_device,
        mesh=mesh,
        in_specs=placed,
        out_specs=P("rhs", None, "node", None),
        check_vma=False,
    )
```

```python
import functools

import jax
import jax.numpy as jnp
from jax import lax
from jax.experimental import pallas as pl
from jax.experimental.pallas import tpu as pltpu
from jax.sharding import PartitionSpec as P

F32 = jnp.float32
BF16 = jnp.bfloat16
NT = (((1,), (1,)), ((), ()))
NN = (((1,), (0,)), ((), ()))

ORDER = (0, 1, 3, 2)


def dot(a, b, dims):
    return lax.dot_general(a, b, dims, preferred_element_type=F32)


def slot_of(v, z):
    return (ORDER[v // 2] ^ z) * 2 + v % 2


def level_kernel(config, *refs):
    refs = list(refs)
    take = lambda n: [refs.pop(0) for _ in range(n)]
    rows, fanout = config["rows"], config["fanout"]
    level, down, up = config["level"], config["down"], config["up"]
    linked = level > 0
    last = fanout if linked else 0
    z = lax.axis_index("rhs")
    place = take(1)[0] if linked else None
    tiles = take(max(spec[0] for spec in config["tiles"]) + 1)
    tiles = [(tiles[ref], at, skip) for ref, at, skip in config["tiles"]]
    if down:
        mine, other = take(2)
        solved = take(1)[0] if linked else None
    else:
        stored, incoming = take(2)
    out_f = take(1)[0] if not up else None
    if up:
        result_mine, result_other = take(2)
        keep, sent = take(2) if linked else (None, None)
    right = take(1)[0] if down else None
    total = take(1)[0] if up and linked else None

    def tile(v, k):
        ref, at, skip = tiles[v // 2]
        return ref[v % 2, skip + k] if at is None else ref[at, v % 2, skip + k]

    def wide(v):
        return jnp.concatenate([tile(v, k) for k in range(fanout)], axis=1)

    def places(v):
        base = ((level - 1) * rows + slot_of(v, z)) * fanout
        return [place[base + k] for k in range(fanout)]

    if total is not None:
        total[...] = jnp.zeros_like(total)
    if down:
        columns = mine.shape[0]
        for s in range(rows):
            right[s, :columns] = mine[:, level, s, :]
            right[s, columns:] = other[:, level, s, :]
        values = []
        for v in range(rows):
            current = right[slot_of(v, z)]
            if linked:
                picked = jnp.concatenate([solved[at] for at in places(v)], axis=1)
                current = current - dot(picked, wide(v), NT)
            values.append(current.astype(BF16))
        values = [dot(values[v], tile(v, last), NT).astype(BF16) for v in range(rows)]
        if not up:
            for v in range(rows):
                out_f[v] = values[v]
            return
    else:
        values = []
        for v in range(rows):
            values.append((stored[v].astype(F32) - incoming[v]).astype(BF16))
    answers = [dot(values[v], tile(v, last), NN) for v in range(rows)]
    columns = result_mine.shape[1]
    for v in range(rows):
        result_mine[slot_of(v, z)] = answers[v][:columns]
        result_other[slot_of(v, z)] = answers[v][columns:].astype(result_other.dtype)
    if not linked:
        return
    size = answers[0].shape[1]
    for v in range(rows):
        terms = dot(answers[v].astype(BF16), wide(v), NN)
        for k, at in enumerate(places(v)):
            total[at] += terms[:, k * size : (k + 1) * size]
    middle = total.shape[0] // 2
    keep[...] = total[:middle]
    sent[...] = total[middle:].astype(BF16)


def finish_kernel(spans, *refs):
    z = lax.axis_index("rhs")
    inner = (z == 1) | (z == 2)
    refs, out = list(refs[:-1]), refs[-1]
    for span in spans:
        home = refs.pop(0)
        for i, level in enumerate(span):
            mine = refs.pop(0)
            for s in range(mine.shape[0]):
                out[:, level, s, :] = jnp.where(inner, mine[s], home[i, s].astype(F32))


VMEM = pl.BlockSpec(memory_space=pltpu.VMEM)
SMEM = pl.BlockSpec(memory_space=pltpu.SMEM)


def params():
    return pltpu.CompilerParams(vmem_limit_bytes=32 * 1024 * 1024)


def on_device(right_side, diag_tiles, off_tiles, src_part, src_slot):
    columns, levels, rows, size = right_side.shape
    fanout = src_part.shape[2]
    nodes = lax.axis_size("node")
    chips = nodes // 2
    node, z = lax.axis_index("node"), lax.axis_index("rhs")

    def inward(x):
        return lax.ppermute(x, "rhs", [(0, 1), (3, 2)])

    def outward(x):
        return lax.ppermute(x, "rhs", [(1, 0), (2, 3)])

    def between(x):
        return lax.ppermute(x, "rhs", [(1, 2), (2, 1)])

    def shift(x, d):
        return lax.ppermute(x, "node", [(n, n ^ d) for n in range(nodes)])

    def after(x, *others):
        return lax.optimization_barrier((x, *others))[0]

    held, where = {}, {}

    def hold(level, arrays, places):
        held[level], where[level] = arrays, places

    pieces = [diag_tiles[0][:, None]] + [
        jnp.concatenate([off_tiles[level - 1], diag_tiles[level][:, None]], axis=1)
        for level in range(1, levels)
    ]
    near, both = {}, {}

    def join(level, *others):
        block, at = near[level]
        pair = jnp.stack([pieces[level], block if at is None else block[at]])
        both[level] = between(after(pair, *others))
        places = [(0, None, 0), (1, at, 0), (2, 0, 0), (2, 1, 0)]
        hold(level, [pieces[level], block, both[level]], places)

    facing = between(jnp.concatenate(pieces[:2], axis=1))
    other_right = inward(right_side)
    near[0] = inward(pieces[0]), None
    near[1] = inward(after(pieces[1], near[0][0])), None
    middle = inward(after(jnp.stack(pieces[2:4]), near[0][0]))
    near[2], near[3] = (middle, 0), (middle, 1)

    def meet(level, *others):
        block, at = near[level]
        corner = between(after(block if at is None else block[at], *others))
        places = [(0, None, 0), (1, at, 0), (2, None, level % 2), (3, None, 0)]
        hold(level, [pieces[level], block, facing if level < 2 else second, corner], places)
        return corner

    meet(0)
    second = between(after(pieces[2], facing))

    rel = after(src_part, facing) ^ node
    pair = (src_slot >> 1) ^ z
    inner = (pair ^ (pair >> 1)) * 2 + (src_slot & 1)
    place = (((rel >> 1) + (rel & 1) * chips) * rows + inner).reshape(-1)

    vec = (rows, 2 * columns, size)
    own = (rows, columns, size)

    def run(level, down, up, inputs):
        linked = level > 0
        config = dict(
            rows=rows,
            fanout=fanout,
            level=level,
            down=down,
            up=up,
            tiles=where[level],
        )
        args = ([place] if linked else []) + list(held[level]) + list(inputs)
        shapes, scratch = [], []
        if down:
            scratch.append(pltpu.VMEM(vec, F32))
        if not up:
            shapes.append(jax.ShapeDtypeStruct(vec, BF16))
        else:
            shapes += [jax.ShapeDtypeStruct(own, t) for t in (F32, BF16)]
            if linked:
                shapes += [jax.ShapeDtypeStruct((chips * rows,) + vec[1:], t) for t in (F32, BF16)]
                scratch.append(pltpu.VMEM((nodes * rows,) + vec[1:], F32))
        dots = rows * ((fanout if linked else 0) + 1) * (int(down) + int(up))
        return pl.pallas_call(
            functools.partial(level_kernel, config),
            in_specs=([SMEM] if linked else []) + [VMEM] * (len(args) - int(linked)),
            out_specs=[VMEM] * len(shapes),
            out_shape=shapes,
            scratch_shapes=scratch,
            compiler_params=params(),
            cost_estimate=pl.CostEstimate(
                flops=4 * dots * columns * size * size,
                bytes_accessed=dots * size * size * 2,
                transcendentals=0,
            ),
        )(*args)

    def gather(value, *early):
        met = jnp.concatenate([value] + [shift(value, 2 * d) for d in range(1, chips)])
        core = after(met, *early)
        return jnp.concatenate([core, shift(core, 1)])

    def scatter(keep, sent):
        summed = keep + shift(sent, 1).astype(F32)
        parts = [summed[d * rows : (d + 1) * rows] for d in range(chips)]
        incoming = parts[0]
        for d in range(chips - 1, 0, -1):
            incoming = incoming + shift(parts[d].astype(BF16), 2 * d).astype(F32)
        return incoming

    stored = []
    inputs = [right_side, after(other_right, place)]
    for level in range(levels - 1):
        (value,) = run(level, True, False, inputs)
        stored.append(value)
        if level == 0:
            near[4] = inward(after(pieces[4], value)), None
            early = [meet(1, value), middle]
        elif level == 1:
            early = [meet(2, stored[0])]
        else:
            early = [both[level + 1]] if level + 1 < levels - 1 else []
        gathered = gather(value, *early)
        if level < 2:
            join(level + 3, gathered)
        if level == 0:
            gathered = after(gathered, near[4][0], second)
        inputs = [right_side, other_right, gathered]
    mine, others = [None] * levels, [None] * levels
    mine[-1], others[-1], *sums = run(levels - 1, True, True, inputs)
    for level in range(levels - 2, -1, -1):
        outs = run(level, False, True, [stored[level], scatter(*sums)])
        mine[level], others[level], *sums = outs
    spans = [list(range(levels - 1, 0, -1)), [0]]
    args = []
    for span in spans:
        args += [outward(jnp.stack([others[x] for x in span]))] + [mine[x] for x in span]
    return pl.pallas_call(
        functools.partial(finish_kernel, spans),
        in_specs=[VMEM] * len(args),
        out_specs=VMEM,
        out_shape=jax.ShapeDtypeStruct(right_side.shape, F32),
        compiler_params=params(),
    )(*args)


def solution(mesh):
    placed = (
        P("rhs", None, "node", None),
        P(None, ("node", "rhs"), None, None),
        P(None, ("node", "rhs"), None, None, None),
        P(None, "node", None),
        P(None, "node", None),
    )
    return jax.shard_map(
        on_device,
        mesh=mesh,
        in_specs=placed,
        out_specs=P("rhs", None, "node", None),
        check_vma=False,
    )
```

```python
import functools

import jax
import jax.numpy as jnp
from jax import lax
from jax.experimental import pallas as pl
from jax.experimental.pallas import tpu as pltpu
from jax.sharding import PartitionSpec as P

F32 = jnp.float32
BF16 = jnp.bfloat16
NT = (((1,), (1,)), ((), ()))
NN = (((1,), (0,)), ((), ()))

ORDER = (0, 1, 3, 2)


def dot(a, b, dims):
    return lax.dot_general(a, b, dims, preferred_element_type=F32)


def slot_of(v, z):
    return (ORDER[v // 2] ^ z) * 2 + v % 2


def level_kernel(config, *refs):
    refs = list(refs)
    take = lambda n: [refs.pop(0) for _ in range(n)]
    rows, fanout = config["rows"], config["fanout"]
    level, down, up = config["level"], config["down"], config["up"]
    linked = level > 0
    last = fanout if linked else 0
    z = lax.axis_index("rhs")
    place = take(1)[0] if linked else None
    tiles = take(max(spec[0] for spec in config["tiles"]) + 1)
    tiles = [(tiles[ref], at, skip) for ref, at, skip in config["tiles"]]
    if down:
        mine, other = take(2)
        solved = take(1)[0] if linked else None
    else:
        stored, incoming = take(2)
    out_f = take(1)[0] if not up else None
    if up:
        result_mine, result_other = take(2)
        keep, sent = take(2) if linked else (None, None)
    right = take(1)[0] if down else None
    total = take(1)[0] if up and linked else None

    def tile(v, k):
        ref, at, skip = tiles[v // 2]
        return ref[v % 2, skip + k] if at is None else ref[at, v % 2, skip + k]

    def wide(v):
        return jnp.concatenate([tile(v, k) for k in range(fanout)], axis=1)

    def places(v):
        base = ((level - 1) * rows + slot_of(v, z)) * fanout
        return [place[base + k] for k in range(fanout)]

    if total is not None:
        total[...] = jnp.zeros_like(total)
    if down:
        columns = mine.shape[0]
        for s in range(rows):
            right[s, :columns] = mine[:, level, s, :]
            right[s, columns:] = other[:, level, s, :]
        values = []
        for v in range(rows):
            current = right[slot_of(v, z)]
            if linked:
                picked = jnp.concatenate([solved[at] for at in places(v)], axis=1)
                current = current - dot(picked, wide(v), NT)
            values.append(current.astype(BF16))
        values = [dot(values[v], tile(v, last), NT).astype(BF16) for v in range(rows)]
        if not up:
            for v in range(rows):
                out_f[v] = values[v]
            return
    else:
        values = []
        for v in range(rows):
            values.append((stored[v].astype(F32) - incoming[v]).astype(BF16))
    answers = [dot(values[v], tile(v, last), NN) for v in range(rows)]
    columns = result_mine.shape[1]
    for v in range(rows):
        result_mine[slot_of(v, z)] = answers[v][:columns]
        result_other[slot_of(v, z)] = answers[v][columns:].astype(result_other.dtype)
    if not linked:
        return
    size = answers[0].shape[1]
    for v in range(rows):
        terms = dot(answers[v].astype(BF16), wide(v), NN)
        for k, at in enumerate(places(v)):
            total[at] += terms[:, k * size : (k + 1) * size]
    middle = total.shape[0] // 2
    keep[...] = total[:middle]
    sent[...] = total[middle:].astype(BF16)


def finish_kernel(spans, *refs):
    z = lax.axis_index("rhs")
    inner = (z == 1) | (z == 2)
    refs, out = list(refs[:-1]), refs[-1]
    for span in spans:
        home = refs.pop(0)
        for i, level in enumerate(span):
            mine = refs.pop(0)
            for s in range(mine.shape[0]):
                out[:, level, s, :] = jnp.where(inner, mine[s], home[i, s].astype(F32))


VMEM = pl.BlockSpec(memory_space=pltpu.VMEM)
SMEM = pl.BlockSpec(memory_space=pltpu.SMEM)


def params():
    return pltpu.CompilerParams(vmem_limit_bytes=32 * 1024 * 1024)


def on_device(right_side, diag_tiles, off_tiles, src_part, src_slot):
    columns, levels, rows, size = right_side.shape
    fanout = src_part.shape[2]
    nodes = lax.axis_size("node")
    chips = nodes // 2
    node, z = lax.axis_index("node"), lax.axis_index("rhs")

    def inward(x):
        return lax.ppermute(x, "rhs", [(0, 1), (3, 2)])

    def outward(x):
        return lax.ppermute(x, "rhs", [(1, 0), (2, 3)])

    def between(x):
        return lax.ppermute(x, "rhs", [(1, 2), (2, 1)])

    def shift(x, d):
        return lax.ppermute(x, "node", [(n, n ^ d) for n in range(nodes)])

    def after(x, *others):
        return lax.optimization_barrier((x, *others))[0]

    held, where = {}, {}

    def hold(level, arrays, places):
        held[level], where[level] = arrays, places

    pieces = [diag_tiles[0][:, None]] + [
        jnp.concatenate([off_tiles[level - 1], diag_tiles[level][:, None]], axis=1)
        for level in range(1, levels)
    ]
    near, both = {}, {}

    def join(level, *others):
        block, at = near[level]
        pair = jnp.stack([pieces[level], block if at is None else block[at]])
        both[level] = between(after(pair, *others))
        places = [(0, None, 0), (1, at, 0), (2, 0, 0), (2, 1, 0)]
        hold(level, [pieces[level], block, both[level]], places)

    facing = between(jnp.concatenate(pieces[:2], axis=1))
    other_right = inward(right_side)
    near[0] = inward(pieces[0]), None
    near[1] = inward(after(pieces[1], near[0][0])), None
    middle = inward(after(jnp.stack(pieces[2:4]), near[0][0]))
    near[2], near[3] = (middle, 0), (middle, 1)

    def meet(level, *others):
        block, at = near[level]
        corner = between(after(block if at is None else block[at], *others))
        places = [(0, None, 0), (1, at, 0), (2, None, level % 2), (3, None, 0)]
        hold(level, [pieces[level], block, facing if level < 2 else second, corner], places)
        return corner

    meet(0)
    second = between(after(pieces[2], facing))

    rel = after(src_part, facing) ^ node
    pair = (src_slot >> 1) ^ z
    inner = (pair ^ (pair >> 1)) * 2 + (src_slot & 1)
    place = (((rel >> 1) + (rel & 1) * chips) * rows + inner).reshape(-1)

    vec = (rows, 2 * columns, size)
    own = (rows, columns, size)

    def run(level, down, up, inputs):
        linked = level > 0
        config = dict(
            rows=rows,
            fanout=fanout,
            level=level,
            down=down,
            up=up,
            tiles=where[level],
        )
        args = ([place] if linked else []) + list(held[level]) + list(inputs)
        shapes, scratch = [], []
        if down:
            scratch.append(pltpu.VMEM(vec, F32))
        if not up:
            shapes.append(jax.ShapeDtypeStruct(vec, BF16))
        else:
            shapes += [jax.ShapeDtypeStruct(own, t) for t in (F32, BF16)]
            if linked:
                shapes += [jax.ShapeDtypeStruct((chips * rows,) + vec[1:], t) for t in (F32, BF16)]
                scratch.append(pltpu.VMEM((nodes * rows,) + vec[1:], F32))
        dots = rows * ((fanout if linked else 0) + 1) * (int(down) + int(up))
        return pl.pallas_call(
            functools.partial(level_kernel, config),
            in_specs=([SMEM] if linked else []) + [VMEM] * (len(args) - int(linked)),
            out_specs=[VMEM] * len(shapes),
            out_shape=shapes,
            scratch_shapes=scratch,
            compiler_params=params(),
            cost_estimate=pl.CostEstimate(
                flops=4 * dots * columns * size * size,
                bytes_accessed=dots * size * size * 2,
                transcendentals=0,
            ),
        )(*args)

    def gather(value, *early):
        met = jnp.concatenate([value] + [shift(value, 2 * d) for d in range(1, chips)])
        core = after(met, *early)
        return jnp.concatenate([core, shift(core, 1)])

    def scatter(keep, sent):
        summed = keep + shift(sent, 1).astype(F32)
        parts = [summed[d * rows : (d + 1) * rows] for d in range(chips)]
        incoming = parts[0]
        for d in range(chips - 1, 0, -1):
            incoming = incoming + shift(parts[d].astype(BF16), 2 * d).astype(F32)
        return incoming

    stored = []
    inputs = [right_side, after(other_right, place)]
    for level in range(levels - 1):
        (value,) = run(level, True, False, inputs)
        stored.append(value)
        if level == 0:
            early = [meet(1, value), middle]
        elif level == 1:
            early = [meet(2, stored[0]), near[4][0]]
        else:
            early = [both[level + 1]]
        gathered = gather(value, *early)
        if level == 0:
            near[4] = inward(after(pieces[4], gathered)), None
        if level < 2:
            join(level + 3, gathered)
        if level == 0:
            gathered = after(gathered, second)
        inputs = [right_side, other_right, gathered]
    mine, others = [None] * levels, [None] * levels
    mine[-1], others[-1], *sums = run(levels - 1, True, True, inputs)
    for level in range(levels - 2, -1, -1):
        outs = run(level, False, True, [stored[level], scatter(*sums)])
        mine[level], others[level], *sums = outs
    spans = [list(range(levels - 1, 0, -1)), [0]]
    args = []
    for span in spans:
        args += [outward(jnp.stack([others[x] for x in span]))] + [mine[x] for x in span]
    return pl.pallas_call(
        functools.partial(finish_kernel, spans),
        in_specs=[VMEM] * len(args),
        out_specs=VMEM,
        out_shape=jax.ShapeDtypeStruct(right_side.shape, F32),
        compiler_params=params(),
    )(*args)


def solution(mesh):
    placed = (
        P("rhs", None, "node", None),
        P(None, ("node", "rhs"), None, None),
        P(None, ("node", "rhs"), None, None, None),
        P(None, "node", None),
        P(None, "node", None),
    )
    return jax.shard_map(
        on_device,
        mesh=mesh,
        in_specs=placed,
        out_specs=P("rhs", None, "node", None),
        check_vma=False,
    )
```

```python
import functools

import jax
import jax.numpy as jnp
from jax import lax
from jax.experimental import pallas as pl
from jax.experimental.pallas import tpu as pltpu
from jax.sharding import PartitionSpec as P

F32 = jnp.float32
BF16 = jnp.bfloat16
NT = (((1,), (1,)), ((), ()))
NN = (((1,), (0,)), ((), ()))

ORDER = (0, 1, 3, 2)


def dot(a, b, dims):
    return lax.dot_general(a, b, dims, preferred_element_type=F32)


def slot_of(v, z):
    return (ORDER[v // 2] ^ z) * 2 + v % 2


def level_kernel(config, *refs):
    refs = list(refs)
    take = lambda n: [refs.pop(0) for _ in range(n)]
    rows, fanout = config["rows"], config["fanout"]
    level, down, up = config["level"], config["down"], config["up"]
    linked = level > 0
    last = fanout if linked else 0
    z = lax.axis_index("rhs")
    place = take(1)[0] if linked else None
    tiles = take(max(spec[0] for spec in config["tiles"]) + 1)
    tiles = [(tiles[ref], at, skip) for ref, at, skip in config["tiles"]]
    if down:
        mine, other = take(2)
        solved = take(1)[0] if linked else None
    else:
        stored, incoming = take(2)
    out_f = take(1)[0] if not up else None
    if up:
        result_mine, result_other = take(2)
        keep, sent = take(2) if linked else (None, None)
    right = take(1)[0] if down else None
    total = take(1)[0] if up and linked else None

    def tile(v, k):
        ref, at, skip = tiles[v // 2]
        return ref[v % 2, skip + k] if at is None else ref[at, v % 2, skip + k]

    def wide(v):
        return jnp.concatenate([tile(v, k) for k in range(fanout)], axis=1)

    def places(v):
        base = ((level - 1) * rows + slot_of(v, z)) * fanout
        return [place[base + k] for k in range(fanout)]

    if total is not None:
        total[...] = jnp.zeros_like(total)
    if down:
        columns = mine.shape[0]
        for s in range(rows):
            right[s, :columns] = mine[:, level, s, :]
            right[s, columns:] = other[:, level, s, :]
        values = []
        for v in range(rows):
            current = right[slot_of(v, z)]
            if linked:
                picked = jnp.concatenate([solved[at] for at in places(v)], axis=1)
                current = current - dot(picked, wide(v), NT)
            values.append(current.astype(BF16))
        values = [dot(values[v], tile(v, last), NT).astype(BF16) for v in range(rows)]
        if not up:
            for v in range(rows):
                out_f[v] = values[v]
            return
    else:
        values = []
        for v in range(rows):
            values.append((stored[v].astype(F32) - incoming[v]).astype(BF16))
    answers = [dot(values[v], tile(v, last), NN) for v in range(rows)]
    columns = result_mine.shape[1]
    for v in range(rows):
        result_mine[slot_of(v, z)] = answers[v][:columns]
        result_other[slot_of(v, z)] = answers[v][columns:].astype(result_other.dtype)
    if not linked:
        return
    size = answers[0].shape[1]
    for v in range(rows):
        terms = dot(answers[v].astype(BF16), wide(v), NN)
        for k, at in enumerate(places(v)):
            total[at] += terms[:, k * size : (k + 1) * size]
    middle = total.shape[0] // 2
    keep[...] = total[:middle]
    sent[...] = total[middle:].astype(BF16)


def finish_kernel(span, home, *refs):
    z = lax.axis_index("rhs")
    inner = (z == 1) | (z == 2)
    out = refs[-1]
    for i, level in enumerate(span):
        mine = refs[i]
        for s in range(mine.shape[0]):
            out[:, level, s, :] = jnp.where(inner, mine[s], home[i, s].astype(F32))


VMEM = pl.BlockSpec(memory_space=pltpu.VMEM)
SMEM = pl.BlockSpec(memory_space=pltpu.SMEM)


def params():
    return pltpu.CompilerParams(vmem_limit_bytes=32 * 1024 * 1024)


def on_device(right_side, diag_tiles, off_tiles, src_part, src_slot):
    columns, levels, rows, size = right_side.shape
    fanout = src_part.shape[2]
    nodes = lax.axis_size("node")
    chips = nodes // 2
    node, z = lax.axis_index("node"), lax.axis_index("rhs")

    def inward(x):
        return lax.ppermute(x, "rhs", [(0, 1), (3, 2)])

    def outward(x):
        return lax.ppermute(x, "rhs", [(1, 0), (2, 3)])

    def between(x):
        return lax.ppermute(x, "rhs", [(1, 2), (2, 1)])

    def shift(x, d):
        return lax.ppermute(x, "node", [(n, n ^ d) for n in range(nodes)])

    def after(x, *others):
        return lax.optimization_barrier((x, *others))[0]

    held, where = {}, {}

    def hold(level, arrays, places):
        held[level], where[level] = arrays, places

    pieces = [diag_tiles[0][:, None]] + [
        jnp.concatenate([off_tiles[level - 1], diag_tiles[level][:, None]], axis=1)
        for level in range(1, levels)
    ]
    near, both = {}, {}

    def join(level, *others):
        block, at = near[level]
        pair = jnp.stack([pieces[level], block if at is None else block[at]])
        both[level] = between(after(pair, *others))
        places = [(0, None, 0), (1, at, 0), (2, 0, 0), (2, 1, 0)]
        hold(level, [pieces[level], block, both[level]], places)

    facing = between(jnp.concatenate(pieces[:2], axis=1))
    other_right = inward(right_side)
    near[0] = inward(pieces[0]), None
    near[1] = inward(after(pieces[1], near[0][0])), None
    middle = inward(after(jnp.stack(pieces[2:4]), near[0][0]))
    near[2], near[3] = (middle, 0), (middle, 1)

    def meet(level, *others):
        block, at = near[level]
        corner = between(after(block if at is None else block[at], *others))
        places = [(0, None, 0), (1, at, 0), (2, None, level % 2), (3, None, 0)]
        hold(level, [pieces[level], block, facing if level < 2 else second, corner], places)
        return corner

    meet(0)
    second = between(after(pieces[2], facing))

    rel = after(src_part, facing) ^ node
    pair = (src_slot >> 1) ^ z
    inner = (pair ^ (pair >> 1)) * 2 + (src_slot & 1)
    place = (((rel >> 1) + (rel & 1) * chips) * rows + inner).reshape(-1)

    vec = (rows, 2 * columns, size)
    own = (rows, columns, size)

    def run(level, down, up, inputs):
        linked = level > 0
        config = dict(
            rows=rows,
            fanout=fanout,
            level=level,
            down=down,
            up=up,
            tiles=where[level],
        )
        args = ([place] if linked else []) + list(held[level]) + list(inputs)
        shapes, scratch = [], []
        if down:
            scratch.append(pltpu.VMEM(vec, F32))
        if not up:
            shapes.append(jax.ShapeDtypeStruct(vec, BF16))
        else:
            shapes += [jax.ShapeDtypeStruct(own, t) for t in (F32, BF16)]
            if linked:
                shapes += [jax.ShapeDtypeStruct((chips * rows,) + vec[1:], t) for t in (F32, BF16)]
                scratch.append(pltpu.VMEM((nodes * rows,) + vec[1:], F32))
        dots = rows * ((fanout if linked else 0) + 1) * (int(down) + int(up))
        return pl.pallas_call(
            functools.partial(level_kernel, config),
            in_specs=([SMEM] if linked else []) + [VMEM] * (len(args) - int(linked)),
            out_specs=[VMEM] * len(shapes),
            out_shape=shapes,
            scratch_shapes=scratch,
            compiler_params=params(),
            cost_estimate=pl.CostEstimate(
                flops=4 * dots * columns * size * size,
                bytes_accessed=dots * size * size * 2,
                transcendentals=0,
            ),
        )(*args)

    def gather(value, *early):
        met = jnp.concatenate([value] + [shift(value, 2 * d) for d in range(1, chips)])
        core = after(met, *early)
        return jnp.concatenate([core, shift(core, 1)])

    def scatter(keep, sent):
        summed = keep + shift(sent, 1).astype(F32)
        parts = [summed[d * rows : (d + 1) * rows] for d in range(chips)]
        incoming = parts[0]
        for d in range(chips - 1, 0, -1):
            incoming = incoming + shift(parts[d].astype(BF16), 2 * d).astype(F32)
        return incoming

    stored = []
    inputs = [right_side, after(other_right, place)]
    for level in range(levels - 1):
        (value,) = run(level, True, False, inputs)
        stored.append(value)
        if level == 0:
            early = [meet(1, value), middle]
        elif level == 1:
            near[4] = inward(after(pieces[4], value)), None
            early = [meet(2, stored[0]), near[4][0]]
        else:
            early = [both[level + 1]]
        gathered = gather(value, *early)
        if level < 2:
            join(level + 3, gathered)
        if level == 0:
            gathered = after(gathered, second)
        inputs = [right_side, other_right, gathered]
    mine, others = [None] * levels, [None] * levels
    mine[-1], others[-1], *sums = run(levels - 1, True, True, inputs)
    for level in range(levels - 2, -1, -1):
        outs = run(level, False, True, [stored[level], scatter(*sums)])
        mine[level], others[level], *sums = outs
    def finish(span, whole):
        args = [outward(jnp.stack([others[x] for x in span]))] + [mine[x] for x in span]
        specs = [VMEM] * len(args)
        height = levels
        if whole is not None:
            args.append(whole)
            specs.append(pl.BlockSpec(memory_space=pl.ANY))
            height = 1
        return pl.pallas_call(
            functools.partial(finish_kernel, span),
            grid=(1,),
            in_specs=specs,
            out_specs=pl.BlockSpec((columns, height, rows, size), lambda i: (0, 0, 0, 0)),
            out_shape=jax.ShapeDtypeStruct(right_side.shape, F32),
            input_output_aliases={} if whole is None else {len(args) - 1: 0},
            compiler_params=params(),
        )(*args)

    return finish([0], finish(list(range(levels - 1, 0, -1)), None))


def solution(mesh):
    placed = (
        P("rhs", None, "node", None),
        P(None, ("node", "rhs"), None, None),
        P(None, ("node", "rhs"), None, None, None),
        P(None, "node", None),
        P(None, "node", None),
    )
    return jax.shard_map(
        on_device,
        mesh=mesh,
        in_specs=placed,
        out_specs=P("rhs", None, "node", None),
        check_vma=False,
    )
```

```python
import functools

import jax
import jax.numpy as jnp
from jax import lax
from jax.experimental import pallas as pl
from jax.experimental.pallas import tpu as pltpu
from jax.sharding import PartitionSpec as P

F32 = jnp.float32
BF16 = jnp.bfloat16
NT = (((1,), (1,)), ((), ()))
NN = (((1,), (0,)), ((), ()))

ORDER = (0, 1, 3, 2)


def dot(a, b, dims):
    return lax.dot_general(a, b, dims, preferred_element_type=F32)


def slot_of(v, z):
    return (ORDER[v // 2] ^ z) * 2 + v % 2


def level_kernel(config, *refs):
    refs = list(refs)
    take = lambda n: [refs.pop(0) for _ in range(n)]
    rows, fanout = config["rows"], config["fanout"]
    level, down, up = config["level"], config["down"], config["up"]
    linked = level > 0
    last = fanout if linked else 0
    z = lax.axis_index("rhs")
    place = take(1)[0] if linked else None
    tiles = take(max(spec[0] for spec in config["tiles"]) + 1)
    tiles = [(tiles[ref], at, skip) for ref, at, skip in config["tiles"]]
    if down:
        mine, other = take(2)
        solved = take(1)[0] if linked else None
    else:
        stored, incoming = take(2)
    out_f = take(1)[0] if not up else None
    if up:
        result_mine, result_other = take(2)
        keep, sent = take(2) if linked else (None, None)
    right = take(1)[0] if down else None
    total = take(1)[0] if up and linked else None

    def tile(v, k):
        ref, at, skip = tiles[v // 2]
        return ref[v % 2, skip + k] if at is None else ref[at, v % 2, skip + k]

    def wide(v):
        return jnp.concatenate([tile(v, k) for k in range(fanout)], axis=1)

    def places(v):
        base = ((level - 1) * rows + slot_of(v, z)) * fanout
        return [place[base + k] for k in range(fanout)]

    if total is not None:
        total[...] = jnp.zeros_like(total)
    if down:
        columns = mine.shape[0]
        for s in range(rows):
            right[s, :columns] = mine[:, level, s, :]
            right[s, columns:] = other[:, level, s, :]
        values = []
        for v in range(rows):
            current = right[slot_of(v, z)]
            if linked:
                picked = jnp.concatenate([solved[at] for at in places(v)], axis=1)
                current = current - dot(picked, wide(v), NT)
            values.append(current.astype(BF16))
        values = [dot(values[v], tile(v, last), NT).astype(BF16) for v in range(rows)]
        if not up:
            for v in range(rows):
                out_f[v] = values[v]
            return
    else:
        values = []
        for v in range(rows):
            values.append((stored[v].astype(F32) - incoming[v]).astype(BF16))
    answers = [dot(values[v], tile(v, last), NN) for v in range(rows)]
    columns = result_mine.shape[1]
    for v in range(rows):
        result_mine[slot_of(v, z)] = answers[v][:columns]
        result_other[slot_of(v, z)] = answers[v][columns:].astype(result_other.dtype)
    if not linked:
        return
    size = answers[0].shape[1]
    for v in range(rows):
        terms = dot(answers[v].astype(BF16), wide(v), NN)
        for k, at in enumerate(places(v)):
            total[at] += terms[:, k * size : (k + 1) * size]
    middle = total.shape[0] // 2
    keep[...] = total[:middle]
    sent[...] = total[middle:].astype(BF16)


def finish_kernel(span, home, *refs):
    z = lax.axis_index("rhs")
    inner = (z == 1) | (z == 2)
    out = refs[-1]
    for i, level in enumerate(span):
        mine = refs[i]
        for s in range(mine.shape[0]):
            out[:, level, s, :] = jnp.where(inner, mine[s], home[i, s].astype(F32))


VMEM = pl.BlockSpec(memory_space=pltpu.VMEM)
SMEM = pl.BlockSpec(memory_space=pltpu.SMEM)


def params():
    return pltpu.CompilerParams(vmem_limit_bytes=32 * 1024 * 1024)


def on_device(right_side, diag_tiles, off_tiles, src_part, src_slot):
    columns, levels, rows, size = right_side.shape
    fanout = src_part.shape[2]
    nodes = lax.axis_size("node")
    chips = nodes // 2
    node, z = lax.axis_index("node"), lax.axis_index("rhs")

    def inward(x):
        return lax.ppermute(x, "rhs", [(0, 1), (3, 2)])

    def outward(x):
        return lax.ppermute(x, "rhs", [(1, 0), (2, 3)])

    def between(x):
        return lax.ppermute(x, "rhs", [(1, 2), (2, 1)])

    def shift(x, d):
        return lax.ppermute(x, "node", [(n, n ^ d) for n in range(nodes)])

    def after(x, *others):
        return lax.optimization_barrier((x, *others))[0]

    held, where = {}, {}

    def hold(level, arrays, places):
        held[level], where[level] = arrays, places

    pieces = [diag_tiles[0][:, None]] + [
        jnp.concatenate([off_tiles[level - 1], diag_tiles[level][:, None]], axis=1)
        for level in range(1, levels)
    ]
    near, both = {}, {}

    def join(level, *others):
        block, at = near[level]
        pair = jnp.stack([pieces[level], block if at is None else block[at]])
        both[level] = between(after(pair, *others))
        places = [(0, None, 0), (1, at, 0), (2, 0, 0), (2, 1, 0)]
        hold(level, [pieces[level], block, both[level]], places)

    facing = between(jnp.concatenate(pieces[:2], axis=1))
    other_right = inward(right_side)
    near[0] = inward(pieces[0]), None
    near[1] = inward(after(pieces[1], near[0][0])), None
    middle = inward(after(jnp.stack(pieces[2:4]), near[0][0]))
    near[2], near[3] = (middle, 0), (middle, 1)

    def meet(level, *others):
        block, at = near[level]
        corner = between(after(block if at is None else block[at], *others))
        places = [(0, None, 0), (1, at, 0), (2, None, level % 2), (3, None, 0)]
        hold(level, [pieces[level], block, facing if level < 2 else second, corner], places)
        return corner

    meet(0)
    second = between(after(pieces[2], facing))

    rel = after(src_part, facing) ^ node
    pair = (src_slot >> 1) ^ z
    inner = (pair ^ (pair >> 1)) * 2 + (src_slot & 1)
    place = (((rel >> 1) + (rel & 1) * chips) * rows + inner).reshape(-1)

    vec = (rows, 2 * columns, size)
    own = (rows, columns, size)

    def run(level, down, up, inputs):
        linked = level > 0
        config = dict(
            rows=rows,
            fanout=fanout,
            level=level,
            down=down,
            up=up,
            tiles=where[level],
        )
        args = ([place] if linked else []) + list(held[level]) + list(inputs)
        shapes, scratch = [], []
        if down:
            scratch.append(pltpu.VMEM(vec, F32))
        if not up:
            shapes.append(jax.ShapeDtypeStruct(vec, BF16))
        else:
            shapes += [jax.ShapeDtypeStruct(own, t) for t in (F32, BF16)]
            if linked:
                shapes += [jax.ShapeDtypeStruct((chips * rows,) + vec[1:], t) for t in (F32, BF16)]
                scratch.append(pltpu.VMEM((nodes * rows,) + vec[1:], F32))
        dots = rows * ((fanout if linked else 0) + 1) * (int(down) + int(up))
        return pl.pallas_call(
            functools.partial(level_kernel, config),
            in_specs=([SMEM] if linked else []) + [VMEM] * (len(args) - int(linked)),
            out_specs=[VMEM] * len(shapes),
            out_shape=shapes,
            scratch_shapes=scratch,
            compiler_params=params(),
            cost_estimate=pl.CostEstimate(
                flops=4 * dots * columns * size * size,
                bytes_accessed=dots * size * size * 2,
                transcendentals=0,
            ),
        )(*args)

    def gather(value, *early):
        met = jnp.concatenate([value] + [shift(value, 2 * d) for d in range(1, chips)])
        core = after(met, *early)
        return jnp.concatenate([core, shift(core, 1)])

    def scatter(keep, sent):
        summed = keep + shift(sent, 1).astype(F32)
        parts = [summed[d * rows : (d + 1) * rows] for d in range(chips)]
        incoming = parts[0]
        for d in range(chips - 1, 0, -1):
            incoming = incoming + shift(parts[d].astype(BF16), 2 * d).astype(F32)
        return incoming

    stored = []
    inputs = [right_side, after(other_right, place)]
    for level in range(levels - 1):
        (value,) = run(level, True, False, inputs)
        stored.append(value)
        if level == 0:
            early = [meet(1, value), middle]
        elif level == 1:
            early = [meet(2, stored[0]), near[4][0]]
        else:
            early = [both[level + 1]]
        gathered = gather(value, *early)
        if level == 0:
            near[4] = inward(after(pieces[4], gathered)), None
        if level < 2:
            join(level + 3, gathered)
        if level == 0:
            gathered = after(gathered, second)
        inputs = [right_side, other_right, gathered]
    mine, others = [None] * levels, [None] * levels
    mine[-1], others[-1], *sums = run(levels - 1, True, True, inputs)
    for level in range(levels - 2, -1, -1):
        outs = run(level, False, True, [stored[level], scatter(*sums)])
        mine[level], others[level], *sums = outs
    def finish(span, whole):
        args = [outward(jnp.stack([others[x] for x in span]))] + [mine[x] for x in span]
        specs = [VMEM] * len(args)
        height = levels
        if whole is not None:
            args.append(whole)
            specs.append(pl.BlockSpec(memory_space=pl.ANY))
            height = 1
        return pl.pallas_call(
            functools.partial(finish_kernel, span),
            grid=(1,),
            in_specs=specs,
            out_specs=pl.BlockSpec((columns, height, rows, size), lambda i: (0, 0, 0, 0)),
            out_shape=jax.ShapeDtypeStruct(right_side.shape, F32),
            input_output_aliases={} if whole is None else {len(args) - 1: 0},
            compiler_params=params(),
        )(*args)

    return finish([0], finish(list(range(levels - 1, 0, -1)), None))


def solution(mesh):
    placed = (
        P("rhs", None, "node", None),
        P(None, ("node", "rhs"), None, None),
        P(None, ("node", "rhs"), None, None, None),
        P(None, "node", None),
        P(None, "node", None),
    )
    return jax.shard_map(
        on_device,
        mesh=mesh,
        in_specs=placed,
        out_specs=P("rhs", None, "node", None),
        check_vma=False,
    )
```
